128 devices in a mesh: dom: 128 (over y, x, z, core).
Axes of the slice: x: 4, y: 4, z: 4, core: 2. Of those that a mesh axis runs over, the one named last changes fastest.
Arguments:
- initial_dofs: float32 [4, 35, 32768], P(None, None, 'dom'), may hold values from -6 to 6
- cluster: int32 [32768], P('dom'), may hold values from 0 to 2, as said below
- neighbours: int32 [4, 32768], P(None, 'dom'), may hold values from -2 to 255, as said below
- orientation: int32 [4, 32768], P(None, 'dom'), may hold values from 0 to 23, as said below
- send_slots: int32 [8, 8192], P(None, 'dom'), may hold values from -1 to 1023, as said below
- recv_slots: int32 [8, 8192], P(None, 'dom'), may hold values from -1 to 1023, as said below
- inv_jacobian: float32 [3, 3, 32768], P(None, None, 'dom'), may hold values from -3 to 3
- normals: float32 [4, 3, 32768], P(None, None, 'dom'), may hold values from -1 to 1, as said below
- face_area: float32 [4, 32768], P(None, 'dom'), may hold values from 0.3 to 1
- bulk_modulus: float32 [32768], P('dom'), may hold values from 0.5 to 2
- inv_density: float32 [32768], P('dom'), may hold values from 0.5 to 2
- deriv_mats: float32 [3, 35, 35], replicated, may hold values from -1 to 1
- face_proj: float32 [4, 15, 35], replicated, may hold values from -1 to 1
Outputs:
- final_dofs: float32 [4, 35, 32768], P(None, None, 'dom')
The draws below stay inside these ranges and needn't reach their ends.
Inputs may be any that keep to these rules, and one draw needn't show every extreme that they name: Within each partition the cluster numbers never fall along the element numbers; each of 0, 1 and 2 holds a positive multiple of 32 elements of every partition. `neighbours`: local element numbers within the same partition, -1 for a wall face, and -2 exactly for the faces listed in recv_slots (which are also exactly those listed in send_slots) of the same partition. For a face listed in recv_slots, orientation // 6 is the face number (0 to 3) of the sending face. `send_slots`: face numbers f * 256 + e of the partition, -1 for empty slots; the live slots of each row come first; the count of live slots in row k of partition r equals that in row 7 - k of partition r + offset_k, zero where that partition does not exist; no face appears twice in a partition; rows of offset 1 and -1 are full wherever the partner exists. `recv_slots`: same encoding and counts as send_slots of the same partition and row, the same set of faces in another order; slot j of row k takes what slot j of row 7 - k of partition r + offset_k sends. `normals`: unit vectors.
All inputs are finite; a program needn't handle non-finite values.
Results may differ from the reference program's by a relative error of at most 0.0003.
Values sent between devices are 32-bit elements; how exact they have to be, the bound alone decides.
A program may use at most 128 MiB of HBM per device.

```python
import math
import jax
import jax.numpy as jnp
import numpy as np
from jax import lax

QUANT = 4
BASIS = 35
FACE_BASIS = 15
E_DEV = 256
REACH = 4
SUBSTEPS = 4
CAP = 64
ELEMS = 32768
N_DOM = 128


def topology(key):
    device_count = N_DOM
    elem_count = E_DEV
    face_count = 4 * E_DEV
    offset_count = 2 * REACH
    keys = jax.random.split(key, 7)
    devices = jnp.arange(device_count, dtype=jnp.int32)
    pair_counts = jax.random.randint(keys[0], (device_count, REACH), CAP // 2, CAP + 1)
    pair_counts = pair_counts.at[:, 0].set(CAP)
    pair_exists = devices[:, None] + jnp.arange(1, REACH + 1, dtype=jnp.int32)[None, :] < device_count
    pair_counts = jnp.where(pair_exists, pair_counts, 0).astype(jnp.int32)
    columns = []
    for k in range(offset_count):
        if k < REACH:
            reach_now = REACH - k
            column = pair_counts[:, reach_now - 1]
            column = jnp.concatenate([jnp.zeros((reach_now,), jnp.int32), column[:-reach_now]])
        else:
            column = pair_counts[:, k - REACH]
        columns.append(column)
    slot_counts = jnp.stack(columns, axis=1)
    offsets = jnp.array([k - REACH if k < REACH else k - REACH + 1 for k in range(offset_count)], jnp.int32)
    orders = jax.vmap(lambda sub_key: jax.random.permutation(sub_key, face_count))(jax.random.split(keys[1], device_count)).astype(jnp.int32)
    slot_faces = orders[:, :offset_count * CAP].reshape(device_count, offset_count, CAP)
    slot_range = jnp.arange(CAP, dtype=jnp.int32)
    live_slot = slot_range[None, None, :] < slot_counts[:, :, None]
    scores = jax.random.randint(keys[2], (device_count, offset_count, CAP), 0, 1 << 20) * CAP + slot_range
    scores = jnp.where(live_slot, scores, (1 << 30) + slot_range)
    send_order = jnp.argsort(scores, axis=-1, stable=True).astype(jnp.int32)
    send_table = jnp.where(live_slot, jnp.take_along_axis(slot_faces, send_order, axis=-1), -1)
    source_dev = jnp.clip(devices[:, None] + offsets[None, :], 0, device_count - 1)
    reverse_row = (offset_count - 1 - jnp.arange(offset_count, dtype=jnp.int32))[None, :]
    source_order = send_order[source_dev, reverse_row]
    recv_table = jnp.where(live_slot, jnp.take_along_axis(slot_faces, source_order, axis=-1), -1)
    base_nbr = jax.random.randint(keys[3], (device_count, face_count), 0, elem_count)
    wall_pick = jax.random.randint(keys[4], (device_count, face_count), 0, 10) == 0
    nbr_table = jnp.where(wall_pick, -1, base_nbr)
    dev_rows = devices[:, None, None]
    remote_flag = jnp.zeros((device_count, face_count), bool).at[dev_rows, jnp.where(live_slot, slot_faces, face_count)].set(True, mode='drop')
    nbr_table = jnp.where(remote_flag, -2, nbr_table).astype(jnp.int32)
    code_table = jax.random.randint(keys[5], (device_count, face_count), 0, 24)
    sender_face = send_table[source_dev, reverse_row] // elem_count
    turn_pick = jax.random.randint(keys[6], (device_count, offset_count, CAP), 0, 6)
    code_table = code_table.at[dev_rows, jnp.where(live_slot, recv_table, face_count)].set(sender_face * 6 + turn_pick, mode='drop').astype(jnp.int32)
    nbr_out = nbr_table.reshape(device_count, 4, elem_count).transpose(1, 0, 2).reshape(4, -1)
    code_out = code_table.reshape(device_count, 4, elem_count).transpose(1, 0, 2).reshape(4, -1)
    send_out = send_table.transpose(1, 0, 2).reshape(offset_count, -1).astype(jnp.int32)
    recv_out = recv_table.transpose(1, 0, 2).reshape(offset_count, -1).astype(jnp.int32)
    return (nbr_out, code_out, send_out, recv_out)


def draw_neighbours(key, part):
    return topology(key)[0]


def draw_orientation(key, part):
    return topology(key)[1]


def draw_send_slots(key, part):
    return topology(key)[2]


def draw_recv_slots(key, part):
    return topology(key)[3]


def draw_cluster(key, part):
    key = jax.random.fold_in(key, 11)
    first_key, second_key = jax.random.split(key)
    first_count = jax.random.randint(first_key, (N_DOM, 1), 1, 7)
    second_count = jax.random.randint(second_key, (N_DOM, 1), 0, 1 << 20) % (7 - first_count) + 1
    block_size = E_DEV // 8
    block_of = jnp.arange(E_DEV, dtype=jnp.int32)[None, :] // block_size
    labels = jnp.where(block_of < first_count, 0, jnp.where(block_of < first_count + second_count, 1, 2))
    return labels.reshape(-1).astype(jnp.int32)


def draw_normals(key, part):
    key = jax.random.fold_in(key, 13)
    first_key, second_key = jax.random.split(key)
    polar = jax.random.uniform(first_key, (4, N_DOM * E_DEV), jnp.float32, 0.0, jnp.pi)
    azimuth = jax.random.uniform(second_key, (4, N_DOM * E_DEV), jnp.float32, -jnp.pi, jnp.pi)
    vectors = jnp.stack([jnp.sin(polar) * jnp.cos(azimuth), jnp.sin(polar) * jnp.sin(azimuth), jnp.cos(polar)], axis=1)
    return vectors.astype(jnp.float32)


def level_of(rng, extent, cuts, low, top_value):
    level = 1.0
    for axis_at, shards_of in cuts:
        draws = jax.random.uniform(jax.random.fold_in(jax.random.fold_in(rng, 6), axis_at), (shards_of,), jnp.float32, low / len(cuts), top_value / len(cuts))
        level = level * jnp.repeat(jnp.exp(draws), extent[axis_at] // shards_of).reshape((-1,) + (1,) * (len(extent) - 1 - axis_at))
    return level


def bell_draw(own_key, dims, spread, most, shards=(), kind=jnp.bfloat16):
    values = spread * jax.random.normal(own_key, dims, jnp.float32)
    if shards:
        values = values * level_of(own_key, dims, shards, -0.22, 0.18)
    return jnp.clip(values, -most, most).astype(kind)


def setup_inputs(seed: int = 0) -> dict:
    seeds = jax.random.split(jax.random.key(seed), 14)
    return {
        "initial_dofs": bell_draw(seeds[0], (QUANT, BASIS, ELEMS), 1.0, 6.0, ((2, 128),), jnp.float32),
        "cluster": draw_cluster(jax.random.fold_in(seeds[13], 71), 0),
        "neighbours": draw_neighbours(jax.random.fold_in(seeds[13], 71), 0),
        "orientation": draw_orientation(jax.random.fold_in(seeds[13], 71), 0),
        "send_slots": draw_send_slots(jax.random.fold_in(seeds[13], 71), 0),
        "recv_slots": draw_recv_slots(jax.random.fold_in(seeds[13], 71), 0),
        "inv_jacobian": bell_draw(seeds[6], (3, 3, ELEMS), 0.5, 3.0, ((2, 128),), jnp.float32),
        "normals": draw_normals(jax.random.fold_in(seeds[13], 71), 0),
        "face_area": jnp.clip(jnp.exp(math.log(1.0) - 1.2039728 * jax.random.uniform(seeds[8], (4, ELEMS), jnp.float32) ** level_of(seeds[8], (4, ELEMS), ((1, 128),), -0.2, 0.2)), 0.3, 1.0),
        "bulk_modulus": jnp.clip(jnp.exp(math.log(2.0) - 1.3862944 * jax.random.uniform(seeds[9], (ELEMS,), jnp.float32) ** level_of(seeds[9], (ELEMS,), ((0, 128),), -0.2, 0.2)), 0.5, 2.0),
        "inv_density": jnp.clip(jnp.exp(math.log(2.0) - 1.3862944 * jax.random.uniform(seeds[10], (ELEMS,), jnp.float32) ** level_of(seeds[10], (ELEMS,), ((0, 128),), -0.2, 0.2)), 0.5, 2.0),
        "deriv_mats": bell_draw(seeds[11], (3, BASIS, BASIS), BASIS ** -0.5, 1.0, (), jnp.float32),
        "face_proj": bell_draw(seeds[12], (4, FACE_BASIS, BASIS), BASIS ** -0.5, 1.0, (), jnp.float32),
    }


STEP_LENGTH = 0.3
HIGH = lax.Precision.HIGHEST

def node_orders():
    node_list = [(i, j) for i in range(5) for j in range(5 - i)]
    place_of = {lattice_node: position for position, lattice_node in enumerate(node_list)}
    turn_list = [(0, 1, 2), (1, 2, 0), (2, 0, 1), (0, 2, 1), (2, 1, 0), (1, 0, 2)]
    order_table = []
    for one_turn in turn_list:
        row_list = []
        for lattice_node in node_list:
            corner_triple = (lattice_node[0], lattice_node[1], 4 - lattice_node[0] - lattice_node[1])
            row_list.append(place_of[corner_triple[one_turn[0]], corner_triple[one_turn[1]]])
        order_table.append(row_list)
    return np.array(order_table, dtype=np.int32)

def element_periods(cluster):
    return jnp.where(cluster == 0, 1, jnp.where(cluster == 1, 2, 4)).astype(jnp.int32)

def derivative_rows(values, deriv_mats, inv_jacobian):
    mixed = jnp.einsum('jab,qbe->jqae', deriv_mats, values, precision=HIGH)
    divergence = jnp.einsum('jie,jiae->ae', inv_jacobian, mixed[:, 1:], precision=HIGH)
    gradient = jnp.einsum('jie,jae->iae', inv_jacobian, mixed[:, 0], precision=HIGH)
    return (divergence, gradient)

def spatial(values, deriv_mats, inv_jacobian, bulk_modulus, inv_density):
    divergence, gradient = derivative_rows(values, deriv_mats, inv_jacobian)
    return jnp.concatenate([(-bulk_modulus * divergence)[None], -inv_density * gradient], axis=0)

def volume_term(values, deriv_mats, inv_jacobian, bulk_modulus, inv_density):
    divergence, gradient = derivative_rows(values, jnp.swapaxes(deriv_mats, 1, 2), inv_jacobian)
    return jnp.concatenate([(bulk_modulus * divergence)[None], inv_density * gradient], axis=0)

def predict(s, values, taylor, cluster, deriv_mats, inv_jacobian, bulk_modulus, inv_density):
    phase = s % element_periods(cluster)
    starting = phase == 0
    fresh = [values]
    for term_index in range(1, 5):
        fresh.append(spatial(fresh[-1], deriv_mats, inv_jacobian, bulk_modulus, inv_density))
    taylor = tuple((jnp.where(starting, fresh[term_index], taylor[term_index]) for term_index in range(5)))
    begin = phase.astype(jnp.float32) * STEP_LENGTH
    finish = begin + STEP_LENGTH
    integral = jnp.zeros_like(values)
    for term_index in range(5):
        weight_now = (finish ** (term_index + 1) - begin ** (term_index + 1)) / math.factorial(term_index + 1)
        integral = integral + taylor[term_index] * weight_now
    return (taylor, integral)

def face_traces(values, face_proj):
    traced = jnp.einsum('fnb,qbe->qnfe', face_proj, values, precision=HIGH)
    return traced.reshape(traced.shape[0], traced.shape[1], -1)

def rotate_faces(raw_traces, codes):
    order_table = node_orders()
    turn_code = codes % 6
    result = jnp.zeros_like(raw_traces)
    for turn_index in range(6):
        result = result + jnp.where(turn_code == turn_index, raw_traces[:, order_table[turn_index], :], 0.0)
    return result

def gather_local(traced, neighbours, orientation):
    elem_count = neighbours.shape[1]
    flat_nbr = neighbours.reshape(-1)
    flat_code = orientation.reshape(-1)
    source = flat_code // 6 * elem_count + jnp.maximum(flat_nbr, 0)
    return jnp.where(flat_nbr >= 0, traced[:, :, source], 0.0)

def place_remote(raw_traces, received, recv_slots):
    target = jnp.where(recv_slots >= 0, recv_slots, raw_traces.shape[2]).reshape(-1)
    payload = received.reshape(received.shape[0], received.shape[1], -1)
    return raw_traces.at[:, :, target].set(payload, mode='drop')

def apply_update(s, values, integral_sum, neighbour_sum, cluster, neighbours, orientation, normals, face_area, bulk_modulus, inv_density, deriv_mats, inv_jacobian, face_proj):
    finished = (s + 1) % element_periods(cluster) == 0
    own_side = jnp.einsum('fnb,qbe->qnfe', face_proj, integral_sum, precision=HIGH)
    far_side = rotate_faces(neighbour_sum, orientation.reshape(-1)).reshape(own_side.shape)
    wall = (neighbours == -1)[None]
    direction = jnp.swapaxes(normals, 0, 1)[:, None]
    normal_own = lax.optimization_barrier(jnp.sum(direction * own_side[1:], axis=0))
    normal_far = jnp.where(wall, -normal_own, lax.optimization_barrier(jnp.sum(direction * far_side[1:], axis=0)))
    pressure_own = own_side[0]
    pressure_far = jnp.where(wall, pressure_own, far_side[0])
    impedance = jnp.sqrt(bulk_modulus / inv_density)
    pressure_star = 0.5 * (pressure_own + pressure_far) + 0.5 * impedance * (normal_own - normal_far)
    velocity_star = 0.5 * (normal_own + normal_far) + 0.5 * (pressure_own - pressure_far) / impedance
    flux_pressure = bulk_modulus * velocity_star * face_area
    flux_velocity = direction * (inv_density * pressure_star * face_area)[None]
    flux = jnp.concatenate([flux_pressure[None], flux_velocity], axis=0)
    lifted = jnp.einsum('fnb,qnfe->qbe', face_proj, flux, precision=HIGH)
    change = volume_term(integral_sum, deriv_mats, inv_jacobian, bulk_modulus, inv_density) - lifted
    values = jnp.where(finished, values + change, values)
    integral_sum = jnp.where(finished, 0.0, integral_sum)
    neighbour_sum = jnp.where(jnp.tile(finished, 4), 0.0, neighbour_sum)
    return (values, integral_sum, neighbour_sum)

def reference(initial_dofs, cluster, neighbours, orientation, send_slots, recv_slots, inv_jacobian, normals, face_area, bulk_modulus, inv_density, deriv_mats, face_proj):
    device_count = N_DOM

    def blocks(array):
        shaped = array.reshape(array.shape[:-1] + (device_count, array.shape[-1] // device_count))
        return jnp.moveaxis(shaped, -2, 0)
    values = blocks(initial_dofs)
    cluster_b = blocks(cluster)
    nbr_b = blocks(neighbours)
    code_b = blocks(orientation)
    send_b = blocks(send_slots)
    recv_b = blocks(recv_slots)
    jac_b = blocks(inv_jacobian)
    normal_b = blocks(normals)
    area_b = blocks(face_area)
    bulk_b = blocks(bulk_modulus)
    density_b = blocks(inv_density)
    offset_count = 2 * REACH
    offsets = [k - REACH if k < REACH else k - REACH + 1 for k in range(offset_count)]
    taylor = tuple((jnp.zeros_like(values) for term_index in range(5)))
    integral_sum = jnp.zeros_like(values)
    neighbour_sum = jnp.zeros((device_count, values.shape[1], face_proj.shape[1], 4 * values.shape[3]), jnp.float32)
    for s in range(SUBSTEPS):

        def predict_block(pieces):
            vals_dev, taylor_dev, cluster_dev, jac_dev, bulk_dev, density_dev = pieces
            taylor_dev, integral_dev = predict(s, vals_dev, taylor_dev, cluster_dev, deriv_mats, jac_dev, bulk_dev, density_dev)
            return (taylor_dev, integral_dev, face_traces(integral_dev, face_proj))
        taylor, integral, traced = lax.map(predict_block, (values, taylor, cluster_b, jac_b, bulk_b, density_b))
        integral_sum = integral_sum + integral

        def outgoing_of(trace_dev, slots_dev):
            flat_slots = slots_dev.reshape(-1)
            picked = jnp.where(flat_slots >= 0, trace_dev[:, :, jnp.maximum(flat_slots, 0)], 0.0)
            return picked.reshape(picked.shape[0], picked.shape[1], offset_count, -1)
        outgoing = jax.vmap(outgoing_of)(traced, send_b)
        arrived = []
        for k in range(offset_count):
            distance = offsets[k]
            source_block = outgoing[:, :, :, offset_count - 1 - k]
            blank_rows = jnp.zeros_like(source_block[:abs(distance)])
            if distance > 0:
                shifted = jnp.concatenate([source_block[distance:], blank_rows], axis=0)
            else:
                shifted = jnp.concatenate([blank_rows, source_block[:distance]], axis=0)
            arrived.append(shifted)
        received = jnp.stack(arrived, axis=3)
        raw_traces = jax.vmap(lambda t, n, o, r, q: place_remote(gather_local(t, n, o), r, q))(traced, nbr_b, code_b, received, recv_b)
        neighbour_sum = neighbour_sum + raw_traces

        def update_block(pieces):
            vals_dev, own_dev, near_dev, cluster_dev, nbr_dev, code_dev, normal_dev, area_dev, bulk_dev, density_dev, jac_dev = pieces
            return apply_update(s, vals_dev, own_dev, near_dev, cluster_dev, nbr_dev, code_dev, normal_dev, area_dev, bulk_dev, density_dev, deriv_mats, jac_dev, face_proj)
        values, integral_sum, neighbour_sum = lax.map(update_block, (values, integral_sum, neighbour_sum, cluster_b, nbr_b, code_b, normal_b, area_b, bulk_b, density_b, jac_b))
    return jnp.moveaxis(values, 0, -2).reshape(initial_dofs.shape)
```

```python
import math

import jax
import jax.numpy as jnp
import numpy as np
from jax import lax
from jax.experimental import pallas as pl
from jax.experimental.pallas import tpu as pltpu
from jax.sharding import PartitionSpec as P

SUBSTEPS = 4
STEP_LENGTH = 0.3
QUANT = 4
BASIS = 35
ROWS = 40
NODES = 15
NROWS = 16
ELEMS = 256
FACES = 4 * ELEMS
OFFSETS = 8
CAP = 64
SLOTS = OFFSETS * CAP
F32, BF16 = jnp.float32, jnp.bfloat16
PAIRS = ((0, 0), (1, 1), (2, 2), (0, 1), (0, 2), (1, 2))


def node_orders():
    nodes = [(i, j) for i in range(5) for j in range(5 - i)]
    place = {node: position for position, node in enumerate(nodes)}
    turns = [(0, 1, 2), (1, 2, 0), (2, 0, 1), (0, 2, 1), (2, 1, 0), (1, 0, 2)]
    table = []
    for turn in turns:
        row = []
        for node in nodes:
            corner = (node[0], node[1], 4 - node[0] - node[1])
            row.append(place[corner[turn[0]], corner[turn[1]]])
        table.append(row)
    return table


def turn_matrix():
    out = np.zeros((6 * NROWS, 128), np.float32)
    for t, row in enumerate(node_orders()):
        for n, source in enumerate(row):
            out[t * NROWS + n, source] = 1.0
    return out


def dot(a, b):
    return lax.dot_general(a, b, (((1,), (0,)), ((), ())), preferred_element_type=F32)


def exact_dot(a, b):
    return lax.dot_general(
        a, b, (((1,), (0,)), ((), ())), precision=lax.Precision.HIGHEST, preferred_element_type=F32
    )


def halves(x):
    hi = x.astype(BF16).astype(F32)
    return hi, x - hi


def stack3(x):
    hi, lo = halves(x)
    return jnp.concatenate([hi, lo, hi, jnp.zeros((8, x.shape[1]), F32)], axis=0).astype(BF16)


def left3(a):
    hi, lo = halves(a)
    return (hi + pltpu.roll(hi, 40, 1) + pltpu.roll(lo, 80, 1)).astype(BF16)


def kernel(
    n_dev,
    dofs, cluster, neighbours, orientation, send_slots, recv_slots, jac, normals, area, bulk, invd,
    deriv, proj, turns, out,
    u_s, a_s, own_s, near_s, pad_s, fpad_s, grad_s, gradt_s, div_s, divt_s, second_s,
    trace_s, lift_s, choose_s, pick_send, pick_local, place_recv, slot_s, zn_s, zline_s,
    zslot_s, code_send, code_local, face_recv, coef_s, tell_out, tell_in, send_buf, recv_buf,
    tell_send, tell_recv, send_sem, recv_sem,
):
    me = lax.axis_index("dom")
    steps = [k - 4 if k < 4 else k - 3 for k in range(OFFSETS)]
    partner = [lax.rem(me + (step + n_dev), n_dev) for step in steps]
    barrier = pltpu.get_barrier_semaphore()
    for k in range(OFFSETS):
        pl.semaphore_signal(
            barrier, inc=1, device_id=(partner[k],), device_id_type=pl.DeviceIdType.MESH
        )

    low = lax.broadcasted_iota(jnp.int32, (8, 128), 1) < CAP
    low1 = lax.broadcasted_iota(jnp.int32, (1, 128), 1) < CAP

    slot_s[...] = jnp.zeros((16, 128), jnp.int32)
    slot_s[0:8, 0:CAP] = send_slots[...]
    slot_s[8:16, 0:CAP] = recv_slots[...]
    both = slot_s[...]
    both = both + pltpu.roll(both, CAP, 1)

    def slot_row(first):
        tiles = [
            jnp.where(
                low1,
                both[first + 2 * p : first + 2 * p + 1],
                both[first + 2 * p + 1 : first + 2 * p + 2],
            )
            for p in range(4)
        ]
        row = jnp.concatenate(tiles, axis=1)
        one, zero = jnp.ones_like(row), jnp.zeros_like(row)
        face = (
            jnp.where(row >= ELEMS, one, zero)
            + jnp.where(row >= 2 * ELEMS, one, zero)
            + jnp.where(row >= 3 * ELEMS, one, zero)
        )
        elem = jnp.where(row >= 0, row - face * ELEMS, -one)
        face = jnp.where(row >= 0, face, -one)
        return face, elem

    send_face, send_elem = slot_row(0)
    recv_face, recv_elem = slot_row(8)

    bulk_r, invd_r = bulk[...], invd[...]
    imp = jnp.sqrt(bulk_r / invd_r)
    code = orientation[...]
    one4, zero4 = jnp.ones_like(code), jnp.zeros_like(code)
    turn_f = (
        code
        - 6 * jnp.where(code >= 6, one4, zero4)
        - 6 * jnp.where(code >= 12, one4, zero4)
        - 6 * jnp.where(code >= 18, one4, zero4)
    ).astype(F32)
    table = []
    for f in range(4):
        zn = normals[f] * imp
        for i in range(3):
            zline_s[i : i + 1, f * ELEMS : (f + 1) * ELEMS] = zn[i : i + 1]
        zn_s[f] = jnp.zeros((8, ELEMS), F32)
        zn_s[f, 0:3] = zn
        zn_s[f, 3:4] = turn_f[f : f + 1]
        code_local[:, f * ELEMS : (f + 1) * ELEMS] = jnp.broadcast_to(code[f : f + 1], (8, ELEMS))
        table.append(zn_s[f])
    table = jnp.concatenate(table, axis=0)
    t_hi, t_rest = halves(table)
    t_mid, t_lo = halves(t_rest)
    table = jnp.concatenate([t_hi, t_mid, t_lo], axis=0).astype(BF16)
    elem_rows = lax.broadcasted_iota(jnp.int32, (ELEMS, SLOTS), 0)
    seen = dot(table, jnp.where(elem_rows == recv_elem, 1.0, 0.0).astype(BF16))
    seen = seen[0:32] + seen[32:64] + seen[64:96]
    tell = jnp.zeros((8, SLOTS), F32)
    for f in range(4):
        tell = jnp.where(recv_face == f, seen[8 * f : 8 * f + 8], tell)
    for k in range(OFFSETS):
        tell_out[k] = tell[:, (k // 2) * 128 : (k // 2 + 1) * 128]

    pl.semaphore_wait(barrier, OFFSETS)

    def tell_copy(k):
        return pltpu.make_async_remote_copy(
            src_ref=tell_out.at[k],
            dst_ref=tell_in.at[OFFSETS - 1 - k],
            send_sem=tell_send.at[k],
            recv_sem=tell_recv.at[OFFSETS - 1 - k],
            device_id=(partner[k],),
            device_id_type=pl.DeviceIdType.MESH,
        )

    for k in range(OFFSETS):
        tell_copy(k).start()

    pick = jnp.where(elem_rows == send_elem, 1.0, 0.0).astype(BF16)
    pick_send[0:ELEMS] = pick
    pick_send[ELEMS:] = pick
    elem_rows1 = lax.broadcasted_iota(jnp.int32, (ELEMS, ELEMS), 0)
    for f in range(4):
        pick = jnp.where(elem_rows1 == neighbours[f : f + 1], 1.0, 0.0).astype(BF16)
        pick_local[0:ELEMS, f * ELEMS : (f + 1) * ELEMS] = pick
        pick_local[ELEMS:, f * ELEMS : (f + 1) * ELEMS] = pick
    elem_lanes = lax.broadcasted_iota(jnp.int32, (128, ELEMS), 1).astype(F32)
    recv_float = recv_elem.astype(F32)
    for p in range(4):
        column = jnp.broadcast_to(recv_float[:, p * 128 : (p + 1) * 128], (128, 128)).T
        column = jnp.concatenate([column, column], axis=1)
        place_recv[p * 128 : (p + 1) * 128] = jnp.where(column == elem_lanes, 1.0, 0.0).astype(BF16)
    face_recv[...] = jnp.broadcast_to(recv_face, (8, SLOTS))

    pad_s[...] = jnp.zeros_like(pad_s)
    fpad_s[...] = jnp.zeros_like(fpad_s)
    for j in range(3):
        pad_s[j, 0:BASIS, 0:BASIS] = deriv[j]
    for f in range(4):
        fpad_s[f, 0:NODES, 0:BASIS] = proj[f]
    d = [pad_s[j] for j in range(3)]
    grad = jnp.concatenate([m[0:ROWS] for m in d], axis=0)
    dt = [m.T for m in d]
    gradt = jnp.concatenate([m[0:ROWS] for m in dt], axis=0)
    grad_s[...] = left3(grad)
    gradt_s[...] = left3(gradt)
    for ref, mats in ((div_s, d), (divt_s, dt)):
        wide = (
            mats[0][0:ROWS]
            + pltpu.roll(mats[1][0:ROWS], 40, 1)
            + pltpu.roll(mats[2][0:ROWS], 80, 1)
        )
        hi, lo = halves(wide)
        ref[...] = jnp.concatenate([hi, hi, lo], axis=1).astype(BF16)
    products = [exact_dot(grad, d[k]) for k in range(3)]
    second = []
    for j, k in PAIRS:
        term = products[k][j * ROWS : (j + 1) * ROWS]
        if j != k:
            term = term + products[j][k * ROWS : (k + 1) * ROWS]
        second.append(term)
    second_s[...] = left3(jnp.concatenate(second, axis=0))
    faces = jnp.concatenate([fpad_s[f, 0:NROWS] for f in range(4)], axis=0)
    trace_s[...] = left3(faces)
    lifts = jnp.concatenate([faces, jnp.zeros((64, 128), F32)], axis=0).T[0:ROWS]
    hi, lo = halves(lifts)
    lift_s[...] = jnp.concatenate(
        [hi + pltpu.roll(hi, 64, 1), lo + pltpu.roll(lo, 64, 1)], axis=1
    ).astype(BF16)
    turn_rows = turns[...]
    for f in range(4):
        choose_s[f * 96 : (f + 1) * 96] = left3(exact_dot(turn_rows, fpad_s[f]))

    kappa = bulk_r * invd_r
    g = [[jac[j, i : i + 1, :] for i in range(3)] for j in range(3)]
    for j in range(3):
        for i in range(3):
            coef_s[3 * j + i : 3 * j + i + 1] = g[j][i]
            coef_s[9 + 3 * j + i : 10 + 3 * j + i] = -invd_r * g[j][i]
    for c, (j, k) in enumerate(PAIRS):
        coef_s[18 + c : 19 + c] = kappa * (
            g[j][0] * g[k][0] + g[j][1] * g[k][1] + g[j][2] * g[k][2]
        )
    for f in range(4):
        size = area[f : f + 1]
        coef_s[24 + f : 25 + f] = 0.5 * size * bulk_r / imp
        for i in range(3):
            row = 28 + 3 * f + i
            coef_s[row : row + 1] = 0.5 * size * invd_r * normals[f, i : i + 1]

    u_s[...] = jnp.zeros_like(u_s)
    for q in range(QUANT):
        u_s[q, 0:BASIS] = dofs[q]
    a_s[...] = jnp.zeros_like(a_s)
    near_s[...] = jnp.zeros_like(near_s)
    own_s[...] = jnp.zeros_like(own_s)

    def coef(row):
        return coef_s[row : row + 1]

    for k in range(OFFSETS):
        tell_copy(k).wait()
    for p in range(4):
        tile = pltpu.roll(jnp.where(low, tell_in[2 * p + 1], tell_in[2 * p]), CAP, 1)
        zslot_s[:, p * 128 : (p + 1) * 128] = tile
    code_send[...] = jnp.broadcast_to(
        send_face * 6 + zslot_s[3:4].astype(jnp.int32), (8, SLOTS)
    )

    def chosen(parts, codes):
        first = jnp.zeros((8, codes.shape[1]), F32)
        second = first
        for c in range(24):
            mask = codes == c
            first = jnp.where(mask, parts[c * 16 : c * 16 + 8], first)
            second = jnp.where(mask, parts[c * 16 + 8 : c * 16 + 16], second)
        return first, second

    def step(s, carry):
        kind = cluster[...]
        s_vec = jnp.full(kind.shape, 0, jnp.int32) + s
        odd = jnp.bitwise_and(s_vec, 1)
        zero = jnp.zeros_like(kind)
        phase = jnp.where(kind == 0, zero, jnp.where(kind == 1, odd, s_vec))
        begin = phase.astype(F32) * STEP_LENGTH
        finish = begin + STEP_LENGTH
        b_pow, f_pow, c = begin, finish, []
        for k in range(5):
            c.append((f_pow - b_pow) * (1.0 / math.factorial(k + 1)))
            b_pow, f_pow = b_pow * begin, f_pow * finish
        left = jnp.where(
            kind == 0, zero, jnp.where(kind == 1, 1 - odd, jnp.bitwise_and(s_vec + 1, 3))
        )
        done = left == 0

        p0 = u_s[0]
        u = [u_s[i + 1] for i in range(3)]

        def contra(v):
            return [
                coef(3 * j) * v[0] + coef(3 * j + 1) * v[1] + coef(3 * j + 2) * v[2]
                for j in range(3)
            ]

        def stack_div(w):
            parts = [halves(x) for x in w]
            pad = jnp.zeros((8, ELEMS), F32)
            his = [p[0] for p in parts] + [pad]
            los = [p[1] for p in parts] + [pad]
            return jnp.concatenate(his + los + his, axis=0).astype(BF16)

        def twice(e):
            total = coef(18) * e[0:ROWS]
            for c_at in range(1, 6):
                total = total + coef(18 + c_at) * e[c_at * ROWS : (c_at + 1) * ROWS]
            return total

        bulk_now, invd_now = bulk[...], invd[...]
        p1 = -bulk_now * dot(div_s[...], stack_div(contra(u)))
        p2 = twice(dot(second_s[...], stack3(p0)))
        e12 = dot(second_s[...], jnp.concatenate([stack3(p1), stack3(p2)], axis=1))
        p3, p4 = twice(e12[:, 0:ELEMS]), twice(e12[:, ELEMS:])
        slope = dot(grad_s[...], stack3(c[1] * p0 + c[2] * p1 + c[3] * p2 + c[4] * p3))
        j_all = [c[0] * p0 + c[1] * p1 + c[2] * p2 + c[3] * p3 + c[4] * p4]
        for i in range(3):
            total = c[0] * u[i]
            for j in range(3):
                total = total + coef(9 + 3 * j + i) * slope[j * ROWS : (j + 1) * ROWS]
            j_all.append(total)
        parts = [halves(x) for x in j_all]
        j_two = jnp.concatenate(
            [
                jnp.concatenate([p[0] for p in parts], axis=0),
                jnp.concatenate([p[1] for p in parts], axis=0),
            ],
            axis=1,
        ).astype(BF16)

        at_slot = dot(j_two, pick_send[...])
        mix = at_slot[0:ROWS]
        for i in range(3):
            mix = mix - zslot_s[i : i + 1] * at_slot[(i + 1) * ROWS : (i + 2) * ROWS]
        first, second = chosen(dot(choose_s[...], stack3(mix)), code_send[...])
        for p in range(4):
            x0 = first[:, p * 128 : (p + 1) * 128]
            x1 = pltpu.roll(second[:, p * 128 : (p + 1) * 128], CAP, 1)
            send_buf[s, 2 * p] = jnp.where(low, x0, x1)
            send_buf[s, 2 * p + 1] = jnp.where(low, x1, x0)

        def trace_copy(k):
            return pltpu.make_async_remote_copy(
                src_ref=send_buf.at[s, k],
                dst_ref=recv_buf.at[s, OFFSETS - 1 - k],
                send_sem=send_sem.at[s, k],
                recv_sem=recv_sem.at[s, OFFSETS - 1 - k],
                device_id=(partner[k],),
                device_id_type=pl.DeviceIdType.MESH,
            )

        for k in range(OFFSETS):
            trace_copy(k).start()

        at_face = dot(j_two, pick_local[...])
        mix = at_face[0:ROWS]
        for i in range(3):
            mix = mix - zline_s[i : i + 1] * at_face[(i + 1) * ROWS : (i + 2) * ROWS]
        first, second = chosen(dot(choose_s[...], stack3(mix)), code_local[...])
        traced = dot(trace_s[...], jnp.concatenate([stack3(x) for x in j_all], axis=1))
        for f in range(4):
            rows = slice(f * NROWS, (f + 1) * NROWS)
            near_s[f * NROWS : f * NROWS + 8] += first[:, f * ELEMS : (f + 1) * ELEMS]
            near_s[f * NROWS + 8 : f * NROWS + 16] += second[:, f * ELEMS : (f + 1) * ELEMS]
            mine = traced[rows, 0:ELEMS]
            for i in range(3):
                mine = mine + zn_s[f, i : i + 1] * traced[rows, (i + 1) * ELEMS : (i + 2) * ELEMS]
            a_s[rows] += mine
        own = [own_s[q] + j_all[q] for q in range(QUANT)]
        change_p = bulk_now * dot(divt_s[...], stack_div(contra(own[1:])))
        slope = dot(gradt_s[...], stack3(own[0]))
        change = [change_p]
        for i in range(3):
            total = coef(9 + i) * slope[0:ROWS]
            for j in range(1, 3):
                total = total + coef(9 + 3 * j + i) * slope[j * ROWS : (j + 1) * ROWS]
            change.append(-total)
        for q in range(QUANT):
            own_s[q] = jnp.where(done, 0.0, own[q])
            u_s[q] = jnp.where(done, u_s[q] + change[q], u_s[q])

        for k in range(OFFSETS):
            trace_copy(k).wait()
        r0, r1 = [], []
        for p in range(4):
            even, odd_block = recv_buf[s, 2 * p], recv_buf[s, 2 * p + 1]
            r0.append(pltpu.roll(jnp.where(low, odd_block, even), CAP, 1))
            r1.append(jnp.where(low, even, odd_block))
        r0, r1 = jnp.concatenate(r0, axis=1), jnp.concatenate(r1, axis=1)
        r0h, r0l = halves(r0)
        r1h, r1l = halves(r1)
        slot_face = face_recv[...]
        his, los = [], []
        for f in range(4):
            mask = slot_face == f
            his += [jnp.where(mask, r0h, 0.0), jnp.where(mask, r1h, 0.0)]
            los += [jnp.where(mask, r0l, 0.0), jnp.where(mask, r1l, 0.0)]
        placed = dot(jnp.concatenate(his + los, axis=0).astype(BF16), place_recv[...])
        near_all = near_s[...] + placed[0:64] + placed[64:128]
        a_all = a_s[...]
        near_s[...] = jnp.where(done, 0.0, near_all)
        a_s[...] = jnp.where(done, 0.0, a_all)

        flux = [[], [], [], []]
        for f in range(4):
            rows = slice(f * NROWS, (f + 1) * NROWS)
            own_f = a_all[rows]
            far_f = jnp.where(neighbours[f : f + 1] == -1, own_f, near_all[rows])
            flux[0].append(coef(24 + f) * (own_f - far_f))
            plus = own_f + far_f
            for i in range(3):
                flux[i + 1].append(coef(28 + 3 * f + i) * plus)
        flux = jnp.concatenate([jnp.concatenate(rows, axis=0) for rows in flux], axis=1)
        hi, lo = halves(flux)
        lifted = dot(lift_s[...], jnp.concatenate([hi, lo, hi, lo], axis=0).astype(BF16))
        for q in range(QUANT):
            part = lifted[:, q * ELEMS : (q + 1) * ELEMS]
            u_s[q] = jnp.where(done, u_s[q] - part, u_s[q])
        return carry

    lax.fori_loop(0, SUBSTEPS, step, 0)
    for q in range(QUANT):
        out[q] = u_s[q, 0:BASIS]


def body(
    initial_dofs, cluster, neighbours, orientation, send_slots, recv_slots, inv_jacobian, normals,
    face_area, bulk_modulus, inv_density, deriv_mats, face_proj,
):
    n_dev = lax.axis_size("dom")
    vmem = pl.BlockSpec(memory_space=pltpu.VMEM)

    def call(*operands):
        return pl.pallas_call(
            lambda *refs: kernel(n_dev, *refs),
            out_shape=jax.ShapeDtypeStruct((QUANT, BASIS, ELEMS), F32),
            in_specs=[vmem] * len(operands),
            out_specs=vmem,
            scratch_shapes=[
                pltpu.VMEM((QUANT, ROWS, ELEMS), F32),
                pltpu.VMEM((4 * NROWS, ELEMS), F32),
                pltpu.VMEM((QUANT, ROWS, ELEMS), F32),
                pltpu.VMEM((4 * NROWS, ELEMS), F32),
                pltpu.VMEM((3, 128, 128), F32),
                pltpu.VMEM((4, 128, 128), F32),
                pltpu.VMEM((3 * ROWS, 128), BF16),
                pltpu.VMEM((3 * ROWS, 128), BF16),
                pltpu.VMEM((ROWS, 384), BF16),
                pltpu.VMEM((ROWS, 384), BF16),
                pltpu.VMEM((6 * ROWS, 128), BF16),
                pltpu.VMEM((4 * NROWS, 128), BF16),
                pltpu.VMEM((ROWS, 256), BF16),
                pltpu.VMEM((24 * NROWS, 128), BF16),
                pltpu.VMEM((2 * ELEMS, SLOTS), BF16),
                pltpu.VMEM((2 * ELEMS, FACES), BF16),
                pltpu.VMEM((SLOTS, ELEMS), BF16),
                pltpu.VMEM((16, 128), jnp.int32),
                pltpu.VMEM((4, 8, ELEMS), F32),
                pltpu.VMEM((8, FACES), F32),
                pltpu.VMEM((8, SLOTS), F32),
                pltpu.VMEM((8, SLOTS), jnp.int32),
                pltpu.VMEM((8, FACES), jnp.int32),
                pltpu.VMEM((8, SLOTS), jnp.int32),
                pltpu.VMEM((40, ELEMS), F32),
                pltpu.VMEM((OFFSETS, 8, 128), F32),
                pltpu.VMEM((OFFSETS, 8, 128), F32),
                pltpu.VMEM((SUBSTEPS, OFFSETS, 8, 128), F32),
                pltpu.VMEM((SUBSTEPS, OFFSETS, 8, 128), F32),
                pltpu.SemaphoreType.DMA((OFFSETS,)),
                pltpu.SemaphoreType.DMA((OFFSETS,)),
                pltpu.SemaphoreType.DMA((SUBSTEPS, OFFSETS)),
                pltpu.SemaphoreType.DMA((SUBSTEPS, OFFSETS)),
            ],
            compiler_params=pltpu.CompilerParams(
                collective_id=0, has_side_effects=True, vmem_limit_bytes=48 * 1024 * 1024
            ),
        )(*operands)

    return call(
        initial_dofs,
        cluster.reshape(1, ELEMS),
        neighbours,
        orientation,
        send_slots,
        recv_slots,
        inv_jacobian,
        normals,
        face_area,
        bulk_modulus.reshape(1, ELEMS),
        inv_density.reshape(1, ELEMS),
        deriv_mats,
        face_proj,
        jnp.asarray(turn_matrix()),
    )


def solution(mesh):
    return jax.shard_map(
        body,
        mesh=mesh,
        in_specs=(
            P(None, None, "dom"),
            P("dom"),
            P(None, "dom"),
            P(None, "dom"),
            P(None, "dom"),
            P(None, "dom"),
            P(None, None, "dom"),
            P(None, None, "dom"),
            P(None, "dom"),
            P("dom"),
            P("dom"),
            P(),
            P(),
        ),
        out_specs=P(None, None, "dom"),
        check_vma=False,
    )
```

```python
import math

import jax
import jax.numpy as jnp
import numpy as np
from jax import lax
from jax.experimental import pallas as pl
from jax.experimental.pallas import tpu as pltpu
from jax.sharding import PartitionSpec as P

SUBSTEPS = 4
STEP_LENGTH = 0.3
QUANT = 4
BASIS = 35
ROWS = 40
NODES = 15
NROWS = 16
ELEMS = 256
FACES = 4 * ELEMS
OFFSETS = 8
CAP = 64
SLOTS = OFFSETS * CAP
F32, BF16 = jnp.float32, jnp.bfloat16
TILES = (0, 3, 1, 2)
FAR_FIRST = (0, 7, 1, 6, 2, 5, 3, 4)
PAIRS = ((0, 0), (1, 1), (2, 2), (0, 1), (0, 2), (1, 2))


def node_orders():
    nodes = [(i, j) for i in range(5) for j in range(5 - i)]
    place = {node: position for position, node in enumerate(nodes)}
    turns = [(0, 1, 2), (1, 2, 0), (2, 0, 1), (0, 2, 1), (2, 1, 0), (1, 0, 2)]
    table = []
    for turn in turns:
        row = []
        for node in nodes:
            corner = (node[0], node[1], 4 - node[0] - node[1])
            row.append(place[corner[turn[0]], corner[turn[1]]])
        table.append(row)
    return table


def turn_matrix():
    out = np.zeros((6 * NROWS, 128), np.float32)
    for t, row in enumerate(node_orders()):
        for n, source in enumerate(row):
            out[t * NROWS + n, source] = 1.0
    return out


def dot(a, b):
    return lax.dot_general(a, b, (((1,), (0,)), ((), ())), preferred_element_type=F32)


def halves(x):
    hi = x.astype(BF16).astype(F32)
    return hi, x - hi


def stack3(x):
    hi, lo = halves(x)
    return jnp.concatenate([hi, lo, hi, jnp.zeros((8, x.shape[1]), F32)], axis=0).astype(BF16)


def left3(a):
    hi, lo = halves(a)
    return (hi + pltpu.roll(hi, 40, 1) + pltpu.roll(lo, 80, 1)).astype(BF16)


def kernel(
    n_dev,
    dofs, cluster, neighbours, orientation, send_slots, recv_slots, jac, normals, area, bulk, invd,
    deriv, proj, turns, out,
    dofs_v, cluster_v, neigh_v, code_v, send_v, recv_v, jac_v, normal_v, area_v, bulk_v, invd_v,
    deriv_v, proj_v, turns_v,
    u_s, a_s, own_s, near_s, pad_s, fpad_s, grad_s, gradt_s, div_s, divt_s, second_s,
    trace_s, lift_s, choose_s, turn_s, pick_send, pick_local, place_recv, slot_s, zn_s, zline_s,
    zslot_s, tell_s, code_send, code_local, face_recv, coef_s,
    send0_buf, recv0_buf, send_buf, recv_buf,
    in_sem, send_sem, recv_sem,
):
    me = lax.axis_index("dom")
    steps = [k - 4 if k < 4 else k - 3 for k in range(OFFSETS)]
    partner = [lax.rem(me + (step + n_dev), n_dev) for step in steps]
    there = [me >= -step if step < 0 else me < n_dev - step for step in steps]
    barrier = pltpu.get_barrier_semaphore()
    for k in FAR_FIRST:

        @pl.when(there[k])
        def _():
            pl.semaphore_signal(
                barrier, inc=1, device_id=(partner[k],), device_id_type=pl.DeviceIdType.MESH
            )

    loads = {}

    def load(name, source, target):
        loads.setdefault(name, []).append((source, target))

    load("recv", recv_slots, recv_v)
    load("send", send_slots, send_v)
    load("code", orientation, code_v)
    load("bulk", bulk, bulk_v)
    load("invd", invd, invd_v)
    load("normal", normals, normal_v)
    load("deriv", deriv, deriv_v)
    for q in range(QUANT):
        load("dofs", dofs.at[:, q, :], dofs_v.at[q])
    load("jac", jac, jac_v)
    for f in range(4):
        load("proj", proj.at[:, f, :], proj_v.at[f])
    load("cluster", cluster, cluster_v)
    load("neigh", neighbours, neigh_v)
    load("area", area, area_v)
    load("turns", turns, turns_v)
    count = 0
    for name in loads:
        copies = []
        for source, target in loads[name]:
            copies.append(pltpu.make_async_copy(source, target, in_sem.at[count]))
            copies[-1].start()
            count += 1
        loads[name] = copies

    def ready(*names):
        for name in names:
            for copy in loads[name]:
                copy.wait()

    low = lax.broadcasted_iota(jnp.int32, (8, 128), 1) < CAP
    low1 = lax.broadcasted_iota(jnp.int32, (1, 128), 1) < CAP
    pad_s[...] = jnp.zeros_like(pad_s)
    fpad_s[...] = jnp.zeros_like(fpad_s)
    u_s[...] = jnp.zeros_like(u_s)
    slot_s[...] = jnp.zeros((16, 128), jnp.int32)

    ready("recv", "send")
    slot_s[0:8, 0:CAP] = send_v[...]
    slot_s[8:16, 0:CAP] = recv_v[...]
    both = slot_s[...]
    both = both + pltpu.roll(both, CAP, 1)

    def slot_row(first):
        tiles = [
            jnp.where(
                low1,
                both[first + 2 * p : first + 2 * p + 1],
                both[first + 2 * p + 1 : first + 2 * p + 2],
            )
            for p in TILES
        ]
        row = jnp.concatenate(tiles, axis=1)
        one, zero = jnp.ones_like(row), jnp.zeros_like(row)
        face = (
            jnp.where(row >= ELEMS, one, zero)
            + jnp.where(row >= 2 * ELEMS, one, zero)
            + jnp.where(row >= 3 * ELEMS, one, zero)
        )
        elem = jnp.where(row >= 0, row - face * ELEMS, -one)
        face = jnp.where(row >= 0, face, -one)
        return face, elem

    send_face, send_elem = slot_row(0)
    recv_face, recv_elem = slot_row(8)
    elem_rows = lax.broadcasted_iota(jnp.int32, (ELEMS, SLOTS), 0)
    pick = jnp.where(elem_rows == send_elem, 1.0, 0.0).astype(BF16)
    pick_send[0:ELEMS] = pick
    pick_send[ELEMS:] = pick

    ready("code", "bulk", "invd", "normal")
    bulk_r, invd_r = bulk_v[...], invd_v[...]
    imp = jnp.sqrt(bulk_r / invd_r)
    code = code_v[...]
    one4, zero4 = jnp.ones_like(code), jnp.zeros_like(code)
    turn_f = (
        code
        - 6 * jnp.where(code >= 6, one4, zero4)
        - 6 * jnp.where(code >= 12, one4, zero4)
        - 6 * jnp.where(code >= 18, one4, zero4)
    ).astype(F32)
    znormal = [normal_v[i] * imp for i in range(3)]
    table = []
    for f in range(4):
        zn_s[f] = jnp.zeros((8, ELEMS), F32)
        for i in range(3):
            zn_s[f, i : i + 1] = znormal[i][f : f + 1]
        zn_s[f, 3:4] = turn_f[f : f + 1]
        table.append(zn_s[f])
    table = jnp.concatenate(table, axis=0)
    t_hi, t_rest = halves(table)
    t_mid, t_lo = halves(t_rest)
    table = jnp.concatenate([t_hi, t_mid, t_lo], axis=0).astype(BF16)
    seen = dot(table, jnp.where(elem_rows == recv_elem, 1.0, 0.0).astype(BF16))
    seen = seen[0:32] + seen[32:64] + seen[64:96]
    tell = jnp.zeros((8, SLOTS), F32)
    for f in range(4):
        tell = jnp.where(recv_face == f, seen[8 * f : 8 * f + 8], tell)
    tell_s[...] = tell

    ready("deriv")
    for j in range(3):
        pad_s[j, 0:BASIS, 0:BASIS] = deriv_v[j]
    d = [pad_s[j] for j in range(3)]
    grad = jnp.concatenate([m[0:ROWS] for m in d], axis=0)
    grad_s[...] = left3(grad)

    def set_div(ref, mats):
        wide = (
            mats[0][0:ROWS]
            + pltpu.roll(mats[1][0:ROWS], 40, 1)
            + pltpu.roll(mats[2][0:ROWS], 80, 1)
        )
        hi, lo = halves(wide)
        ref[...] = jnp.concatenate([hi, hi, lo], axis=1).astype(BF16)

    set_div(div_s, d)
    products = dot(grad_s[...], jnp.concatenate([stack3(m[0:ROWS]) for m in d], axis=1))
    second = []
    for j, k in PAIRS:
        term = products[j * ROWS : (j + 1) * ROWS, k * 128 : (k + 1) * 128]
        if j != k:
            term = term + products[k * ROWS : (k + 1) * ROWS, j * 128 : (j + 1) * 128]
        second.append(term)
    second_s[...] = left3(jnp.concatenate(second, axis=0))

    ready("jac", "dofs")
    kappa = bulk_r * invd_r
    g = [[jac_v[j, i : i + 1, :] for i in range(3)] for j in range(3)]
    for j in range(3):
        for i in range(3):
            coef_s[3 * j + i : 3 * j + i + 1] = g[j][i]
            coef_s[9 + 3 * j + i : 10 + 3 * j + i] = -invd_r * g[j][i]
    for c, (j, k) in enumerate(PAIRS):
        coef_s[18 + c : 19 + c] = kappa * (
            g[j][0] * g[k][0] + g[j][1] * g[k][1] + g[j][2] * g[k][2]
        )
    for q in range(QUANT):
        u_s[q, 0:BASIS] = dofs_v[q]
    ready("proj", "cluster")
    for f in range(4):
        fpad_s[f, 0:NODES, 0:BASIS] = proj_v[f]
    faces = jnp.concatenate([fpad_s[f] for f in range(4)], axis=0)
    trace_s[...] = left3(faces)

    def coef(row):
        return coef_s[row : row + 1]

    def contra(v):
        return [
            coef(3 * j) * v[0] + coef(3 * j + 1) * v[1] + coef(3 * j + 2) * v[2] for j in range(3)
        ]

    def stack_div(w):
        parts = [halves(x) for x in w]
        pad = jnp.zeros((8, ELEMS), F32)
        his = [p[0] for p in parts] + [pad]
        los = [p[1] for p in parts] + [pad]
        return jnp.concatenate(his + los + his, axis=0).astype(BF16)

    def twice(e):
        total = coef(18) * e[0:ROWS]
        for c_at in range(1, 6):
            total = total + coef(18 + c_at) * e[c_at * ROWS : (c_at + 1) * ROWS]
        return total

    def predict(s):
        kind = cluster_v[...]
        s_vec = jnp.full(kind.shape, 0, jnp.int32) + s
        odd = jnp.bitwise_and(s_vec, 1)
        zero = jnp.zeros_like(kind)
        phase = jnp.where(kind == 0, zero, jnp.where(kind == 1, odd, s_vec))
        begin = phase.astype(F32) * STEP_LENGTH
        finish = begin + STEP_LENGTH
        b_pow, f_pow, c = begin, finish, []
        for k in range(5):
            c.append((f_pow - b_pow) * (1.0 / math.factorial(k + 1)))
            b_pow, f_pow = b_pow * begin, f_pow * finish
        left = jnp.where(
            kind == 0, zero, jnp.where(kind == 1, 1 - odd, jnp.bitwise_and(s_vec + 1, 3))
        )
        p0 = u_s[0]
        u = [u_s[i + 1] for i in range(3)]
        p1 = -bulk_v[...] * dot(div_s[...], stack_div(contra(u)))
        p2 = twice(dot(second_s[...], stack3(p0)))
        e12 = dot(second_s[...], jnp.concatenate([stack3(p1), stack3(p2)], axis=1))
        p3, p4 = twice(e12[:, 0:ELEMS]), twice(e12[:, ELEMS:])
        slope = dot(grad_s[...], stack3(c[1] * p0 + c[2] * p1 + c[3] * p2 + c[4] * p3))
        j_all = [c[0] * p0 + c[1] * p1 + c[2] * p2 + c[3] * p3 + c[4] * p4]
        for i in range(3):
            total = c[0] * u[i]
            for j in range(3):
                total = total + coef(9 + 3 * j + i) * slope[j * ROWS : (j + 1) * ROWS]
            j_all.append(total)
        return j_all, left == 0

    def two_parts(rows):
        parts = [halves(x) for x in rows]
        his = jnp.concatenate([p[0] for p in parts], axis=0)
        los = jnp.concatenate([p[1] for p in parts], axis=0)
        return jnp.concatenate([his, los], axis=1).astype(BF16)

    def chosen(parts, codes, options):
        first = jnp.zeros((8, codes.shape[1]), F32)
        second = first
        for c in range(options):
            mask = codes == c
            first = jnp.where(mask, parts[c * 16 : c * 16 + 8], first)
            second = jnp.where(mask, parts[c * 16 + 8 : c * 16 + 16], second)
        return first, second

    def packed(x0, x1):
        x1 = pltpu.roll(x1, CAP, 1)
        return jnp.where(low, x0, x1), jnp.where(low, x1, x0)

    def unpacked(even, odd):
        return pltpu.roll(jnp.where(low, odd, even), CAP, 1), jnp.where(low, even, odd)

    def first_copy(k):
        return pltpu.make_async_remote_copy(
            src_ref=send0_buf.at[k],
            dst_ref=recv0_buf.at[OFFSETS - 1 - k],
            send_sem=send_sem.at[k],
            recv_sem=recv_sem.at[0, OFFSETS - 1 - k],
            device_id=(partner[k],),
            device_id_type=pl.DeviceIdType.MESH,
        )

    def later_copy(s):
        parity = lax.rem(s, 2)

        def at(k):
            return pltpu.make_async_remote_copy(
                src_ref=send_buf.at[k],
                dst_ref=recv_buf.at[parity, OFFSETS - 1 - k],
                send_sem=send_sem.at[k],
                recv_sem=recv_sem.at[parity, OFFSETS - 1 - k],
                device_id=(partner[k],),
                device_id_type=pl.DeviceIdType.MESH,
            )

        return at

    def start(copy, rows):
        for k in rows:
            pl.when(there[k])(lambda k=k: copy(k).start())

    def finish_sends(copy):
        for k in FAR_FIRST:
            pl.when(there[k])(lambda k=k: copy(k).wait_send())

    def arrive(copy):
        for k in FAR_FIRST[::-1]:
            pl.when(there[k])(lambda k=k: copy(OFFSETS - 1 - k).wait_recv())

    def meanwhile(j_all, j_two, traced, done):
        at_face = dot(j_two, pick_local[...])
        mix = at_face[0:ROWS]
        for i in range(3):
            mix = mix - zline_s[i : i + 1] * at_face[(i + 1) * ROWS : (i + 2) * ROWS]
        first, second = chosen(dot(choose_s[...], stack3(mix)), code_local[...], 24)
        for f in range(4):
            rows = slice(f * NROWS, (f + 1) * NROWS)
            near_s[f * NROWS : f * NROWS + 8] += first[:, f * ELEMS : (f + 1) * ELEMS]
            near_s[f * NROWS + 8 : f * NROWS + 16] += second[:, f * ELEMS : (f + 1) * ELEMS]
            mine = traced[rows, 0:ELEMS]
            for i in range(3):
                mine = mine + zn_s[f, i : i + 1] * traced[rows, (i + 1) * ELEMS : (i + 2) * ELEMS]
            a_s[rows] += mine
        own = [own_s[q] + j_all[q] for q in range(QUANT)]
        change_p = bulk_v[...] * dot(divt_s[...], stack_div(contra(own[1:])))
        slope = dot(gradt_s[...], stack3(own[0]))
        change = [change_p]
        for i in range(3):
            total = coef(9 + i) * slope[0:ROWS]
            for j in range(1, 3):
                total = total + coef(9 + 3 * j + i) * slope[j * ROWS : (j + 1) * ROWS]
            change.append(-total)
        for q in range(QUANT):
            own_s[q] = jnp.where(done, 0.0, own[q])
            u_s[q] = jnp.where(done, u_s[q] + change[q], u_s[q])

    def complete(r0, r1, done):
        r0h, r0l = halves(r0)
        r1h, r1l = halves(r1)
        slot_face = face_recv[...]
        his, los = [], []
        for f in range(4):
            mask = slot_face == f
            his += [jnp.where(mask, r0h, 0.0), jnp.where(mask, r1h, 0.0)]
            los += [jnp.where(mask, r0l, 0.0), jnp.where(mask, r1l, 0.0)]
        placed = dot(jnp.concatenate(his + los, axis=0).astype(BF16), place_recv[...])
        near_all = near_s[...] + placed[0:64] + placed[64:128]
        a_all = a_s[...]
        near_s[...] = jnp.where(done, 0.0, near_all)
        a_s[...] = jnp.where(done, 0.0, a_all)
        flux = [[], [], [], []]
        for f in range(4):
            rows = slice(f * NROWS, (f + 1) * NROWS)
            own_f = a_all[rows]
            far_f = jnp.where(neigh_v[f : f + 1] == -1, own_f, near_all[rows])
            flux[0].append(coef(24 + f) * (own_f - far_f))
            plus = own_f + far_f
            for i in range(3):
                flux[i + 1].append(coef(28 + 3 * f + i) * plus)
        flux = jnp.concatenate([jnp.concatenate(rows, axis=0) for rows in flux], axis=1)
        hi, lo = halves(flux)
        lifted = dot(lift_s[...], jnp.concatenate([hi, lo, hi, lo], axis=0).astype(BF16))
        for q in range(QUANT):
            part = lifted[:, q * ELEMS : (q + 1) * ELEMS]
            u_s[q] = jnp.where(done, u_s[q] - part, u_s[q])

    def traces(j_all):
        return dot(trace_s[...], jnp.concatenate([stack3(x) for x in j_all], axis=1))

    j_all, done = predict(0)
    traced = traces(j_all)
    face_rows = two_parts([traced[:, q * ELEMS : (q + 1) * ELEMS] for q in range(QUANT)])
    for pos, p in enumerate(TILES):
        k0, k1 = 2 * p, 2 * p + 1
        cols = slice(pos * 128, (pos + 1) * 128)
        send0_buf[k0, 32:40] = tell[:, cols]
        send0_buf[k1, 32:40] = tell[:, cols]
    at_slot = dot(face_rows, pick_send[...])
    for q in range(QUANT):
        x = [jnp.zeros((8, SLOTS), F32)] * 2
        for f in range(4):
            for half in range(2):
                row = q * 64 + f * NROWS + 8 * half
                x[half] = jnp.where(send_face == f, at_slot[row : row + 8], x[half])
        for pos, p in enumerate(TILES):
            cols = slice(pos * 128, (pos + 1) * 128)
            b0, b1 = packed(x[0][:, cols], x[1][:, cols])
            send0_buf[2 * p, q * 8 : q * 8 + 8] = b0
            send0_buf[2 * p + 1, q * 8 : q * 8 + 8] = b1
    pl.semaphore_wait(barrier, sum(t.astype(jnp.int32) for t in there))
    start(first_copy, FAR_FIRST)

    ready("neigh", "area", "turns")
    for k in range(OFFSETS):

        @pl.when(jnp.logical_not(there[k]))
        def _():
            recv0_buf[k] = jnp.zeros((40, 128), F32)
            recv_buf[0, k] = jnp.zeros((8, 128), F32)
            recv_buf[1, k] = jnp.zeros((8, 128), F32)

    a_s[...] = jnp.zeros_like(a_s)
    near_s[...] = jnp.zeros_like(near_s)
    own_s[...] = jnp.zeros_like(own_s)
    elem_rows1 = lax.broadcasted_iota(jnp.int32, (ELEMS, ELEMS), 0)
    for f in range(4):
        cols = slice(f * ELEMS, (f + 1) * ELEMS)
        pick = jnp.where(elem_rows1 == neigh_v[f : f + 1], 1.0, 0.0).astype(BF16)
        pick_local[0:ELEMS, cols] = pick
        pick_local[ELEMS:, cols] = pick
        for i in range(3):
            zline_s[i : i + 1, cols] = znormal[i][f : f + 1]
        code_local[:, cols] = jnp.broadcast_to(code[f : f + 1], (8, ELEMS))
        size = area_v[f : f + 1]
        coef_s[24 + f : 25 + f] = 0.5 * size * bulk_r / imp
        for i in range(3):
            row = 28 + 3 * f + i
            coef_s[row : row + 1] = 0.5 * size * invd_r * normal_v[i, f : f + 1]
    elem_lanes = lax.broadcasted_iota(jnp.int32, (128, ELEMS), 1).astype(F32)
    recv_float = recv_elem.astype(F32)
    for p in range(4):
        column = jnp.broadcast_to(recv_float[:, p * 128 : (p + 1) * 128], (128, 128)).T
        column = jnp.concatenate([column, column], axis=1)
        place_recv[p * 128 : (p + 1) * 128] = jnp.where(column == elem_lanes, 1.0, 0.0).astype(BF16)
    face_recv[...] = jnp.broadcast_to(recv_face, (8, SLOTS))
    dt = [pad_s[j].T for j in range(3)]
    gradt_s[...] = left3(jnp.concatenate([m[0:ROWS] for m in dt], axis=0))
    set_div(divt_s, dt)
    lifts = jnp.concatenate([faces, jnp.zeros((64, 128), F32)], axis=0).T[0:ROWS]
    hi, lo = halves(lifts)
    lift_s[...] = jnp.concatenate(
        [hi + pltpu.roll(hi, 64, 1), lo + pltpu.roll(lo, 64, 1)], axis=1
    ).astype(BF16)
    turn_rows = turns_v[...]
    turn_s[...] = (turn_rows + pltpu.roll(turn_rows, NROWS, 1)).astype(BF16)
    turn_b = turn_rows.astype(BF16)
    for f in range(4):
        rows = jnp.concatenate(
            [faces[f * NROWS : (f + 1) * NROWS], jnp.zeros((112, 128), F32)], axis=0
        )
        choose_s[f * 96 : (f + 1) * 96] = dot(turn_b, left3(rows)).astype(BF16)

    meanwhile(j_all, two_parts(j_all), traced, done)
    arrive(first_copy)
    chi = []
    for q in range(QUANT):
        tiles = [
            unpacked(
                recv0_buf[2 * p, q * 8 : q * 8 + 8], recv0_buf[2 * p + 1, q * 8 : q * 8 + 8]
            )
            for p in TILES
        ]
        both = [jnp.concatenate([t[half] for t in tiles], axis=1) for half in range(2)]
        if q == 0:
            chi = both
        else:
            chi = [x - tell_s[q - 1 : q] * y for x, y in zip(chi, both)]
    for pos, p in enumerate(TILES):
        tile = jnp.where(low, recv0_buf[2 * p + 1, 32:40], recv0_buf[2 * p, 32:40])
        zslot_s[:, pos * 128 : (pos + 1) * 128] = pltpu.roll(tile, CAP, 1)
    code_send[...] = jnp.broadcast_to(send_face * 6 + zslot_s[3:4].astype(jnp.int32), (8, SLOTS))
    hi, lo = halves(jnp.concatenate(chi, axis=0))
    chi = jnp.concatenate([hi, lo, jnp.zeros((96, SLOTS), F32)], axis=0).astype(BF16)
    turn_now = jnp.broadcast_to(tell_s[3:4], (8, SLOTS)).astype(jnp.int32)
    r0, r1 = chosen(dot(turn_s[...], chi), turn_now, 6)
    complete(r0, r1, done)
    finish_sends(first_copy)

    def step(s, carry):
        j_all, done = predict(s)
        j_two = two_parts(j_all)
        copy = later_copy(s)
        for half in range(2):
            cols = slice(half * 256, (half + 1) * 256)
            at_slot = dot(j_two, pick_send[:, cols])
            mix = at_slot[0:ROWS]
            for i in range(3):
                mix = mix - zslot_s[i : i + 1, cols] * at_slot[(i + 1) * ROWS : (i + 2) * ROWS]
            first, second = chosen(dot(choose_s[...], stack3(mix)), code_send[:, cols], 24)
            rows = []
            for at in range(2):
                p = TILES[2 * half + at]
                lanes = slice(at * 128, (at + 1) * 128)
                send_buf[2 * p], send_buf[2 * p + 1] = packed(first[:, lanes], second[:, lanes])
                rows += [2 * p, 2 * p + 1]
            start(copy, [k for k in FAR_FIRST if k in rows])
        meanwhile(j_all, j_two, traces(j_all), done)
        arrive(copy)
        parity = lax.rem(s, 2)
        tiles = [unpacked(recv_buf[parity, 2 * p], recv_buf[parity, 2 * p + 1]) for p in TILES]
        r0 = jnp.concatenate([t[0] for t in tiles], axis=1)
        r1 = jnp.concatenate([t[1] for t in tiles], axis=1)
        complete(r0, r1, done)
        finish_sends(copy)
        return carry

    lax.fori_loop(1, SUBSTEPS, step, 0)
    copies = []
    for q in range(QUANT):
        dofs_v[q] = u_s[q, 0:BASIS]
        copies.append(pltpu.make_async_copy(dofs_v.at[q], out.at[:, q, :], in_sem.at[q]))
        copies[-1].start()
    for copy in copies:
        copy.wait()


def body(
    initial_dofs, cluster, neighbours, orientation, send_slots, recv_slots, inv_jacobian, normals,
    face_area, bulk_modulus, inv_density, deriv_mats, face_proj,
):
    n_dev = lax.axis_size("dom")
    hbm = pl.BlockSpec(memory_space=pltpu.HBM)

    def call(*operands):
        return pl.pallas_call(
            lambda *refs: kernel(n_dev, *refs),
            out_shape=jax.ShapeDtypeStruct((BASIS, QUANT, ELEMS), F32),
            in_specs=[hbm] * len(operands),
            out_specs=hbm,
            scratch_shapes=[
                pltpu.VMEM((QUANT, BASIS, ELEMS), F32),
                pltpu.VMEM((1, ELEMS), jnp.int32),
                pltpu.VMEM((4, ELEMS), jnp.int32),
                pltpu.VMEM((4, ELEMS), jnp.int32),
                pltpu.VMEM((OFFSETS, CAP), jnp.int32),
                pltpu.VMEM((OFFSETS, CAP), jnp.int32),
                pltpu.VMEM((3, 3, ELEMS), F32),
                pltpu.VMEM((3, 4, ELEMS), F32),
                pltpu.VMEM((4, ELEMS), F32),
                pltpu.VMEM((1, ELEMS), F32),
                pltpu.VMEM((1, ELEMS), F32),
                pltpu.VMEM((3, BASIS, BASIS), F32),
                pltpu.VMEM((4, NODES, BASIS), F32),
                pltpu.VMEM((6 * NROWS, 128), F32),
                pltpu.VMEM((QUANT, ROWS, ELEMS), F32),
                pltpu.VMEM((4 * NROWS, ELEMS), F32),
                pltpu.VMEM((QUANT, ROWS, ELEMS), F32),
                pltpu.VMEM((4 * NROWS, ELEMS), F32),
                pltpu.VMEM((3, 128, 128), F32),
                pltpu.VMEM((4, NROWS, 128), F32),
                pltpu.VMEM((3 * ROWS, 128), BF16),
                pltpu.VMEM((3 * ROWS, 128), BF16),
                pltpu.VMEM((ROWS, 384), BF16),
                pltpu.VMEM((ROWS, 384), BF16),
                pltpu.VMEM((6 * ROWS, 128), BF16),
                pltpu.VMEM((4 * NROWS, 128), BF16),
                pltpu.VMEM((ROWS, 256), BF16),
                pltpu.VMEM((24 * NROWS, 128), BF16),
                pltpu.VMEM((6 * NROWS, 128), BF16),
                pltpu.VMEM((2 * ELEMS, SLOTS), BF16),
                pltpu.VMEM((2 * ELEMS, FACES), BF16),
                pltpu.VMEM((SLOTS, ELEMS), BF16),
                pltpu.VMEM((16, 128), jnp.int32),
                pltpu.VMEM((4, 8, ELEMS), F32),
                pltpu.VMEM((8, FACES), F32),
                pltpu.VMEM((8, SLOTS), F32),
                pltpu.VMEM((8, SLOTS), F32),
                pltpu.VMEM((8, SLOTS), jnp.int32),
                pltpu.VMEM((8, FACES), jnp.int32),
                pltpu.VMEM((8, SLOTS), jnp.int32),
                pltpu.VMEM((40, ELEMS), F32),
                pltpu.VMEM((OFFSETS, 40, 128), F32),
                pltpu.VMEM((OFFSETS, 40, 128), F32),
                pltpu.VMEM((OFFSETS, 8, 128), F32),
                pltpu.VMEM((2, OFFSETS, 8, 128), F32),
                pltpu.SemaphoreType.DMA((20,)),
                pltpu.SemaphoreType.DMA((OFFSETS,)),
                pltpu.SemaphoreType.DMA((2, OFFSETS)),
            ],
            compiler_params=pltpu.CompilerParams(
                collective_id=0, has_side_effects=True, vmem_limit_bytes=64 * 1024 * 1024
            ),
        )(*operands)

    result = call(
        jnp.transpose(initial_dofs, (1, 0, 2)),
        cluster.reshape(1, ELEMS),
        neighbours,
        orientation,
        send_slots,
        recv_slots,
        inv_jacobian,
        jnp.transpose(normals, (1, 0, 2)),
        face_area,
        bulk_modulus.reshape(1, ELEMS),
        inv_density.reshape(1, ELEMS),
        deriv_mats,
        jnp.transpose(face_proj, (1, 0, 2)),
        jnp.asarray(turn_matrix()),
    )
    return jnp.transpose(result, (1, 0, 2))


def solution(mesh):
    return jax.shard_map(
        body,
        mesh=mesh,
        in_specs=(
            P(None, None, "dom"),
            P("dom"),
            P(None, "dom"),
            P(None, "dom"),
            P(None, "dom"),
            P(None, "dom"),
            P(None, None, "dom"),
            P(None, None, "dom"),
            P(None, "dom"),
            P("dom"),
            P("dom"),
            P(),
            P(),
        ),
        out_specs=P(None, None, "dom"),
        check_vma=False,
    )
```

```python
import math

import jax
import jax.numpy as jnp
import numpy as np
from jax import lax
from jax.experimental import pallas as pl
from jax.experimental.pallas import tpu as pltpu
from jax.sharding import PartitionSpec as P

SUBSTEPS = 4
STEP_LENGTH = 0.3
QUANT = 4
BASIS = 35
ROWS = 40
NODES = 15
NROWS = 16
ELEMS = 256
FACES = 4 * ELEMS
OFFSETS = 8
CAP = 64
SLOTS = OFFSETS * CAP
F32, BF16 = jnp.float32, jnp.bfloat16
TILES = (0, 3, 1, 2)
FAR_FIRST = (0, 7, 1, 6, 2, 5, 3, 4)
PAIRS = ((0, 0), (1, 1), (2, 2), (0, 1), (0, 2), (1, 2))


def node_orders():
    nodes = [(i, j) for i in range(5) for j in range(5 - i)]
    place = {node: position for position, node in enumerate(nodes)}
    turns = [(0, 1, 2), (1, 2, 0), (2, 0, 1), (0, 2, 1), (2, 1, 0), (1, 0, 2)]
    table = []
    for turn in turns:
        row = []
        for node in nodes:
            corner = (node[0], node[1], 4 - node[0] - node[1])
            row.append(place[corner[turn[0]], corner[turn[1]]])
        table.append(row)
    return table


def turn_table():
    out = np.full((NROWS, 128), NODES, np.int32)
    for t, row in enumerate(node_orders()):
        out[:NODES, t] = row
    return out


def dot(a, b):
    return lax.dot_general(a, b, (((1,), (0,)), ((), ())), preferred_element_type=F32)


def halves(x):
    hi = x.astype(BF16).astype(F32)
    return hi, x - hi


def stack3(x):
    hi, lo = halves(x)
    return jnp.concatenate([hi, lo, hi, jnp.zeros((8, x.shape[1]), F32)], axis=0).astype(BF16)


def left3(a):
    hi, lo = halves(a)
    return (hi + pltpu.roll(hi, 40, 1) + pltpu.roll(lo, 80, 1)).astype(BF16)


def kernel(
    n_dev,
    dofs, cluster, neighbours, orientation, send_slots, recv_slots, jac, normals, area, bulk, invd,
    deriv, proj, turns, out,
    dofs_v, cluster_v, neigh_v, code_v, send_v, recv_v, jac_v, normal_v, area_v, bulk_v, invd_v,
    deriv_v, proj_v, turns_v,
    u_s, a_s, own_s, near_s, pad_s, fpad_s, grad_s, gradt_s, div_s, divt_s, second_s,
    trace_s, lift_s, pick_send, pick_local, place_recv, slot_s, zn_s, zline_s,
    zslot_s, face_send, face_local, face_recv, turn_send, turn_local, turn_recv, coef_s,
    tell_s, send0_buf, recv0_buf, send_buf, recv_buf,
    in_sem, send_sem, recv_sem,
):
    me = lax.axis_index("dom")
    steps = [k - 4 if k < 4 else k - 3 for k in range(OFFSETS)]
    partner = [lax.rem(me + (step + n_dev), n_dev) for step in steps]
    there = [me >= -step if step < 0 else me < n_dev - step for step in steps]
    barrier = pltpu.get_barrier_semaphore()
    for k in FAR_FIRST:

        @pl.when(there[k])
        def _():
            pl.semaphore_signal(
                barrier, inc=1, device_id=(partner[k],), device_id_type=pl.DeviceIdType.MESH
            )

    loads = {}

    def load(name, source, target):
        loads.setdefault(name, []).append((source, target))

    load("recv", recv_slots, recv_v)
    load("send", send_slots, send_v)
    load("code", orientation, code_v)
    load("bulk", bulk, bulk_v)
    load("invd", invd, invd_v)
    load("normal", normals, normal_v)
    load("deriv", deriv, deriv_v)
    for q in range(QUANT):
        load("dofs", dofs.at[:, q, :], dofs_v.at[q])
    load("jac", jac, jac_v)
    for f in range(4):
        load("proj", proj.at[:, f, :], proj_v.at[f])
    load("cluster", cluster, cluster_v)
    load("neigh", neighbours, neigh_v)
    load("area", area, area_v)
    load("turns", turns, turns_v)
    count = 0
    for name in loads:
        copies = []
        for source, target in loads[name]:
            copies.append(pltpu.make_async_copy(source, target, in_sem.at[count]))
            copies[-1].start()
            count += 1
        loads[name] = copies

    def ready(*names):
        for name in names:
            for copy in loads[name]:
                copy.wait()

    low = lax.broadcasted_iota(jnp.int32, (8, 128), 1) < CAP
    low1 = lax.broadcasted_iota(jnp.int32, (1, 128), 1) < CAP
    pad_s[...] = jnp.zeros_like(pad_s)
    fpad_s[...] = jnp.zeros_like(fpad_s)
    u_s[...] = jnp.zeros_like(u_s)
    slot_s[...] = jnp.zeros((16, 128), jnp.int32)

    ready("recv", "send")
    slot_s[0:8, 0:CAP] = send_v[...]
    slot_s[8:16, 0:CAP] = recv_v[...]
    both = slot_s[...]
    both = both + pltpu.roll(both, CAP, 1)

    def slot_row(first):
        tiles = [
            jnp.where(
                low1,
                both[first + 2 * p : first + 2 * p + 1],
                both[first + 2 * p + 1 : first + 2 * p + 2],
            )
            for p in TILES
        ]
        row = jnp.concatenate(tiles, axis=1)
        one, zero = jnp.ones_like(row), jnp.zeros_like(row)
        face = (
            jnp.where(row >= ELEMS, one, zero)
            + jnp.where(row >= 2 * ELEMS, one, zero)
            + jnp.where(row >= 3 * ELEMS, one, zero)
        )
        elem = jnp.where(row >= 0, row - face * ELEMS, -one)
        face = jnp.where(row >= 0, face, -one)
        return face, elem

    send_face, send_elem = slot_row(0)
    recv_face, recv_elem = slot_row(8)
    elem_rows = lax.broadcasted_iota(jnp.int32, (ELEMS, SLOTS), 0)
    pick = jnp.where(elem_rows == send_elem, 1.0, 0.0).astype(BF16)
    pick_send[0:ELEMS] = pick
    pick_send[ELEMS:] = pick

    ready("code", "bulk", "invd", "normal")
    bulk_r, invd_r = bulk_v[...], invd_v[...]
    imp = jnp.sqrt(bulk_r / invd_r)
    code = code_v[...]
    one4, zero4 = jnp.ones_like(code), jnp.zeros_like(code)
    source_face = (
        jnp.where(code >= 6, one4, zero4)
        + jnp.where(code >= 12, one4, zero4)
        + jnp.where(code >= 18, one4, zero4)
    )
    turn = code - 6 * source_face
    turn_f = turn.astype(F32)
    znormal = [normal_v[i] * imp for i in range(3)]
    table = []
    for f in range(4):
        zn_s[f] = jnp.zeros((8, ELEMS), F32)
        for i in range(3):
            zn_s[f, i : i + 1] = znormal[i][f : f + 1]
        zn_s[f, 3:4] = turn_f[f : f + 1]
        table.append(zn_s[f])
    table = jnp.concatenate(table, axis=0)
    t_hi, t_rest = halves(table)
    t_mid, t_lo = halves(t_rest)
    table = jnp.concatenate([t_hi, t_mid, t_lo], axis=0).astype(BF16)
    seen = dot(table, jnp.where(elem_rows == recv_elem, 1.0, 0.0).astype(BF16))
    seen = seen[0:32] + seen[32:64] + seen[64:96]
    tell = jnp.zeros((8, SLOTS), F32)
    for f in range(4):
        tell = jnp.where(recv_face == f, seen[8 * f : 8 * f + 8], tell)
    tell_s[...] = tell

    ready("deriv")
    for j in range(3):
        pad_s[j, 0:BASIS, 0:BASIS] = deriv_v[j]
    d = [pad_s[j] for j in range(3)]
    grad = jnp.concatenate([m[0:ROWS] for m in d], axis=0)
    grad_s[...] = left3(grad)

    def set_div(ref, mats):
        wide = (
            mats[0][0:ROWS]
            + pltpu.roll(mats[1][0:ROWS], 40, 1)
            + pltpu.roll(mats[2][0:ROWS], 80, 1)
        )
        hi, lo = halves(wide)
        ref[...] = jnp.concatenate([hi, hi, lo], axis=1).astype(BF16)

    set_div(div_s, d)
    products = dot(grad_s[...], jnp.concatenate([stack3(m[0:ROWS]) for m in d], axis=1))
    second = []
    for j, k in PAIRS:
        term = products[j * ROWS : (j + 1) * ROWS, k * 128 : (k + 1) * 128]
        if j != k:
            term = term + products[k * ROWS : (k + 1) * ROWS, j * 128 : (j + 1) * 128]
        second.append(term)
    second_s[...] = left3(jnp.concatenate(second, axis=0))

    ready("jac", "dofs")
    kappa = bulk_r * invd_r
    g = [[jac_v[j, i : i + 1, :] for i in range(3)] for j in range(3)]
    for j in range(3):
        for i in range(3):
            coef_s[3 * j + i : 3 * j + i + 1] = g[j][i]
            coef_s[9 + 3 * j + i : 10 + 3 * j + i] = -invd_r * g[j][i]
    for c, (j, k) in enumerate(PAIRS):
        coef_s[18 + c : 19 + c] = kappa * (
            g[j][0] * g[k][0] + g[j][1] * g[k][1] + g[j][2] * g[k][2]
        )
    for q in range(QUANT):
        u_s[q, 0:BASIS] = dofs_v[q]
    ready("proj", "cluster")
    for f in range(4):
        fpad_s[f, 0:NODES, 0:BASIS] = proj_v[f]
    faces = jnp.concatenate([fpad_s[f] for f in range(4)], axis=0)
    trace_s[...] = left3(faces)

    def coef(row):
        return coef_s[row : row + 1]

    def contra(v):
        return [
            coef(3 * j) * v[0] + coef(3 * j + 1) * v[1] + coef(3 * j + 2) * v[2] for j in range(3)
        ]

    def stack_div(w):
        parts = [halves(x) for x in w]
        pad = jnp.zeros((8, ELEMS), F32)
        his = [p[0] for p in parts] + [pad]
        los = [p[1] for p in parts] + [pad]
        return jnp.concatenate(his + los + his, axis=0).astype(BF16)

    def twice(e):
        total = coef(18) * e[0:ROWS]
        for c_at in range(1, 6):
            total = total + coef(18 + c_at) * e[c_at * ROWS : (c_at + 1) * ROWS]
        return total

    def predict(s):
        kind = cluster_v[...]
        s_vec = jnp.full(kind.shape, 0, jnp.int32) + s
        odd = jnp.bitwise_and(s_vec, 1)
        zero = jnp.zeros_like(kind)
        phase = jnp.where(kind == 0, zero, jnp.where(kind == 1, odd, s_vec))
        begin = phase.astype(F32) * STEP_LENGTH
        finish = begin + STEP_LENGTH
        b_pow, f_pow, c = begin, finish, []
        for k in range(5):
            c.append((f_pow - b_pow) * (1.0 / math.factorial(k + 1)))
            b_pow, f_pow = b_pow * begin, f_pow * finish
        left = jnp.where(
            kind == 0, zero, jnp.where(kind == 1, 1 - odd, jnp.bitwise_and(s_vec + 1, 3))
        )
        p0 = u_s[0]
        u = [u_s[i + 1] for i in range(3)]
        p1 = -bulk_v[...] * dot(div_s[...], stack_div(contra(u)))
        p2 = twice(dot(second_s[...], stack3(p0)))
        e12 = dot(second_s[...], jnp.concatenate([stack3(p1), stack3(p2)], axis=1))
        p3, p4 = twice(e12[:, 0:ELEMS]), twice(e12[:, ELEMS:])
        slope = dot(grad_s[...], stack3(c[1] * p0 + c[2] * p1 + c[3] * p2 + c[4] * p3))
        j_all = [c[0] * p0 + c[1] * p1 + c[2] * p2 + c[3] * p3 + c[4] * p4]
        for i in range(3):
            total = c[0] * u[i]
            for j in range(3):
                total = total + coef(9 + 3 * j + i) * slope[j * ROWS : (j + 1) * ROWS]
            j_all.append(total)
        return j_all, left == 0

    def two_parts(rows):
        parts = [halves(x) for x in rows]
        his = jnp.concatenate([p[0] for p in parts], axis=0)
        los = jnp.concatenate([p[1] for p in parts], axis=0)
        return jnp.concatenate([his, los], axis=1).astype(BF16)

    def chosen(parts, faces):
        first, second = parts[0:8], parts[8:16]
        for f in range(1, 4):
            mask = faces == f
            first = jnp.where(mask, parts[f * 16 : f * 16 + 8], first)
            second = jnp.where(mask, parts[f * 16 + 8 : f * 16 + 16], second)
        return first, second

    def set_turns(ref, turn_row):
        table = turns_v[...]
        for half in range(2):
            rows = slice(8 * half, 8 * half + 8)
            places = jnp.broadcast_to(table[rows, 0:1], (8, turn_row.shape[1]))
            for t in range(1, 6):
                places = jnp.where(turn_row == t, table[rows, t : t + 1], places)
            ref[rows] = places

    def turned(first, second, places):
        out = []
        for half in range(2):
            place = places[8 * half : 8 * half + 8]
            row = jnp.bitwise_and(place, 7)
            out.append(
                jnp.where(
                    place < 8,
                    jnp.take_along_axis(first, row, axis=0),
                    jnp.take_along_axis(second, row, axis=0),
                )
            )
        return out

    def packed(x0, x1):
        x1 = pltpu.roll(x1, CAP, 1)
        return jnp.where(low, x0, x1), jnp.where(low, x1, x0)

    def unpacked(even, odd):
        return pltpu.roll(jnp.where(low, odd, even), CAP, 1), jnp.where(low, even, odd)

    def first_copy(k):
        return pltpu.make_async_remote_copy(
            src_ref=send0_buf.at[k],
            dst_ref=recv0_buf.at[OFFSETS - 1 - k],
            send_sem=send_sem.at[k],
            recv_sem=recv_sem.at[0, OFFSETS - 1 - k],
            device_id=(partner[k],),
            device_id_type=pl.DeviceIdType.MESH,
        )

    def later_copy(s):
        parity = lax.rem(s, 2)

        def at(k):
            return pltpu.make_async_remote_copy(
                src_ref=send_buf.at[k],
                dst_ref=recv_buf.at[parity, OFFSETS - 1 - k],
                send_sem=send_sem.at[k],
                recv_sem=recv_sem.at[parity, OFFSETS - 1 - k],
                device_id=(partner[k],),
                device_id_type=pl.DeviceIdType.MESH,
            )

        return at

    def start(copy, rows):
        for k in rows:
            pl.when(there[k])(lambda k=k: copy(k).start())

    def finish_sends(copy):
        for k in FAR_FIRST:
            pl.when(there[k])(lambda k=k: copy(k).wait_send())

    def arrive(copy):
        for k in FAR_FIRST[::-1]:
            pl.when(there[k])(lambda k=k: copy(OFFSETS - 1 - k).wait_recv())

    def meanwhile(j_all, j_two, traced, done):
        at_face = dot(j_two, pick_local[...])
        mix = at_face[0:ROWS]
        for i in range(3):
            mix = mix - zline_s[i : i + 1] * at_face[(i + 1) * ROWS : (i + 2) * ROWS]
        first, second = chosen(dot(trace_s[...], stack3(mix)), face_local[...])
        first, second = turned(first, second, turn_local[...])
        for f in range(4):
            rows = slice(f * NROWS, (f + 1) * NROWS)
            near_s[f * NROWS : f * NROWS + 8] += first[:, f * ELEMS : (f + 1) * ELEMS]
            near_s[f * NROWS + 8 : f * NROWS + 16] += second[:, f * ELEMS : (f + 1) * ELEMS]
            mine = traced[rows, 0:ELEMS]
            for i in range(3):
                mine = mine + zn_s[f, i : i + 1] * traced[rows, (i + 1) * ELEMS : (i + 2) * ELEMS]
            a_s[rows] += mine
        own = [own_s[q] + j_all[q] for q in range(QUANT)]
        change_p = bulk_v[...] * dot(divt_s[...], stack_div(contra(own[1:])))
        slope = dot(gradt_s[...], stack3(own[0]))
        change = [change_p]
        for i in range(3):
            total = coef(9 + i) * slope[0:ROWS]
            for j in range(1, 3):
                total = total + coef(9 + 3 * j + i) * slope[j * ROWS : (j + 1) * ROWS]
            change.append(-total)
        for q in range(QUANT):
            own_s[q] = jnp.where(done, 0.0, own[q])
            u_s[q] = jnp.where(done, u_s[q] + change[q], u_s[q])

    def complete(r0, r1, done):
        r0h, r0l = halves(r0)
        r1h, r1l = halves(r1)
        slot_face = face_recv[...]
        his, los = [], []
        for f in range(4):
            mask = slot_face == f
            his += [jnp.where(mask, r0h, 0.0), jnp.where(mask, r1h, 0.0)]
            los += [jnp.where(mask, r0l, 0.0), jnp.where(mask, r1l, 0.0)]
        placed = dot(jnp.concatenate(his + los, axis=0).astype(BF16), place_recv[...])
        near_all = near_s[...] + placed[0:64] + placed[64:128]
        a_all = a_s[...]
        near_s[...] = jnp.where(done, 0.0, near_all)
        a_s[...] = jnp.where(done, 0.0, a_all)
        flux = [[], [], [], []]
        for f in range(4):
            rows = slice(f * NROWS, (f + 1) * NROWS)
            own_f = a_all[rows]
            far_f = jnp.where(neigh_v[f : f + 1] == -1, own_f, near_all[rows])
            flux[0].append(coef(24 + f) * (own_f - far_f))
            plus = own_f + far_f
            for i in range(3):
                flux[i + 1].append(coef(28 + 3 * f + i) * plus)
        flux = jnp.concatenate([jnp.concatenate(rows, axis=0) for rows in flux], axis=1)
        hi, lo = halves(flux)
        lifted = dot(lift_s[...], jnp.concatenate([hi, lo, hi, lo], axis=0).astype(BF16))
        for q in range(QUANT):
            part = lifted[:, q * ELEMS : (q + 1) * ELEMS]
            u_s[q] = jnp.where(done, u_s[q] - part, u_s[q])

    def traces(j_all):
        return dot(trace_s[...], jnp.concatenate([stack3(x) for x in j_all], axis=1))

    j_all, done = predict(0)
    traced = traces(j_all)
    face_rows = two_parts([traced[:, q * ELEMS : (q + 1) * ELEMS] for q in range(QUANT)])
    at_slot = dot(face_rows, pick_send[...])
    last_row = lax.broadcasted_iota(jnp.int32, (8, SLOTS), 0) == 7
    for q in range(QUANT):
        x = [jnp.zeros((8, SLOTS), F32)] * 2
        for f in range(4):
            for half in range(2):
                row = q * 64 + f * NROWS + 8 * half
                x[half] = jnp.where(send_face == f, at_slot[row : row + 8], x[half])
        x[1] = jnp.where(last_row, tell[q : q + 1], x[1])
        for pos, p in enumerate(TILES):
            cols = slice(pos * 128, (pos + 1) * 128)
            b0, b1 = packed(x[0][:, cols], x[1][:, cols])
            send0_buf[2 * p, q * 8 : q * 8 + 8] = b0
            send0_buf[2 * p + 1, q * 8 : q * 8 + 8] = b1
    pl.semaphore_wait(barrier, sum(t.astype(jnp.int32) for t in there))
    start(first_copy, FAR_FIRST)

    ready("neigh", "area", "turns")
    for k in range(OFFSETS):

        @pl.when(jnp.logical_not(there[k]))
        def _():
            recv0_buf[k] = jnp.zeros((32, 128), F32)
            recv_buf[0, k] = jnp.zeros((8, 128), F32)
            recv_buf[1, k] = jnp.zeros((8, 128), F32)

    a_s[...] = jnp.zeros_like(a_s)
    near_s[...] = jnp.zeros_like(near_s)
    own_s[...] = jnp.zeros_like(own_s)
    elem_rows1 = lax.broadcasted_iota(jnp.int32, (ELEMS, ELEMS), 0)
    for f in range(4):
        cols = slice(f * ELEMS, (f + 1) * ELEMS)
        pick = jnp.where(elem_rows1 == neigh_v[f : f + 1], 1.0, 0.0).astype(BF16)
        pick_local[0:ELEMS, cols] = pick
        pick_local[ELEMS:, cols] = pick
        for i in range(3):
            zline_s[i : i + 1, cols] = znormal[i][f : f + 1]
        face_local[:, cols] = jnp.broadcast_to(source_face[f : f + 1], (8, ELEMS))
        size = area_v[f : f + 1]
        coef_s[24 + f : 25 + f] = 0.5 * size * bulk_r / imp
        for i in range(3):
            row = 28 + 3 * f + i
            coef_s[row : row + 1] = 0.5 * size * invd_r * normal_v[i, f : f + 1]
    elem_lanes = lax.broadcasted_iota(jnp.int32, (128, ELEMS), 1).astype(F32)
    recv_float = recv_elem.astype(F32)
    for p in range(4):
        column = jnp.broadcast_to(recv_float[:, p * 128 : (p + 1) * 128], (128, 128)).T
        column = jnp.concatenate([column, column], axis=1)
        place_recv[p * 128 : (p + 1) * 128] = jnp.where(column == elem_lanes, 1.0, 0.0).astype(BF16)
    face_recv[...] = jnp.broadcast_to(recv_face, (8, SLOTS))
    dt = [pad_s[j].T for j in range(3)]
    gradt_s[...] = left3(jnp.concatenate([m[0:ROWS] for m in dt], axis=0))
    set_div(divt_s, dt)
    lifts = jnp.concatenate([faces, jnp.zeros((64, 128), F32)], axis=0).T[0:ROWS]
    hi, lo = halves(lifts)
    lift_s[...] = jnp.concatenate(
        [hi + pltpu.roll(hi, 64, 1), lo + pltpu.roll(lo, 64, 1)], axis=1
    ).astype(BF16)
    face_send[...] = jnp.broadcast_to(send_face, (8, SLOTS))
    set_turns(turn_local, jnp.concatenate([turn[f : f + 1] for f in range(4)], axis=1))
    set_turns(turn_recv, tell[3:4].astype(jnp.int32))

    meanwhile(j_all, two_parts(j_all), traced, done)
    arrive(first_copy)
    chi = []
    for q in range(QUANT):
        tiles = [
            unpacked(
                recv0_buf[2 * p, q * 8 : q * 8 + 8], recv0_buf[2 * p + 1, q * 8 : q * 8 + 8]
            )
            for p in TILES
        ]
        both = [jnp.concatenate([t[half] for t in tiles], axis=1) for half in range(2)]
        zslot_s[q : q + 1] = both[1][7:8]
        if q == 0:
            chi = both
        else:
            chi = [x - tell_s[q - 1 : q] * y for x, y in zip(chi, both)]
    r0, r1 = turned(chi[0], chi[1], turn_recv[...])
    complete(r0, r1, done)
    set_turns(turn_send, zslot_s[3:4].astype(jnp.int32))
    finish_sends(first_copy)

    def step(s, carry):
        j_all, done = predict(s)
        j_two = two_parts(j_all)
        copy = later_copy(s)
        for half in range(2):
            cols = slice(half * 256, (half + 1) * 256)
            at_slot = dot(j_two, pick_send[:, cols])
            mix = at_slot[0:ROWS]
            for i in range(3):
                mix = mix - zslot_s[i : i + 1, cols] * at_slot[(i + 1) * ROWS : (i + 2) * ROWS]
            first, second = chosen(dot(trace_s[...], stack3(mix)), face_send[:, cols])
            first, second = turned(first, second, turn_send[:, cols])
            rows = []
            for at in range(2):
                p = TILES[2 * half + at]
                lanes = slice(at * 128, (at + 1) * 128)
                send_buf[2 * p], send_buf[2 * p + 1] = packed(first[:, lanes], second[:, lanes])
                rows += [2 * p, 2 * p + 1]
            start(copy, [k for k in FAR_FIRST if k in rows])
        meanwhile(j_all, j_two, traces(j_all), done)
        arrive(copy)
        parity = lax.rem(s, 2)
        tiles = [unpacked(recv_buf[parity, 2 * p], recv_buf[parity, 2 * p + 1]) for p in TILES]
        r0 = jnp.concatenate([t[0] for t in tiles], axis=1)
        r1 = jnp.concatenate([t[1] for t in tiles], axis=1)
        complete(r0, r1, done)
        finish_sends(copy)
        return carry

    lax.fori_loop(1, SUBSTEPS, step, 0)
    copies = []
    for q in range(QUANT):
        dofs_v[q] = u_s[q, 0:BASIS]
        copies.append(pltpu.make_async_copy(dofs_v.at[q], out.at[:, q, :], in_sem.at[q]))
        copies[-1].start()
    for copy in copies:
        copy.wait()


def body(
    initial_dofs, cluster, neighbours, orientation, send_slots, recv_slots, inv_jacobian, normals,
    face_area, bulk_modulus, inv_density, deriv_mats, face_proj,
):
    n_dev = lax.axis_size("dom")
    hbm = pl.BlockSpec(memory_space=pltpu.HBM)

    def call(*operands):
        return pl.pallas_call(
            lambda *refs: kernel(n_dev, *refs),
            out_shape=jax.ShapeDtypeStruct((BASIS, QUANT, ELEMS), F32),
            in_specs=[hbm] * len(operands),
            out_specs=hbm,
            scratch_shapes=[
                pltpu.VMEM((QUANT, BASIS, ELEMS), F32),
                pltpu.VMEM((1, ELEMS), jnp.int32),
                pltpu.VMEM((4, ELEMS), jnp.int32),
                pltpu.VMEM((4, ELEMS), jnp.int32),
                pltpu.VMEM((OFFSETS, CAP), jnp.int32),
                pltpu.VMEM((OFFSETS, CAP), jnp.int32),
                pltpu.VMEM((3, 3, ELEMS), F32),
                pltpu.VMEM((3, 4, ELEMS), F32),
                pltpu.VMEM((4, ELEMS), F32),
                pltpu.VMEM((1, ELEMS), F32),
                pltpu.VMEM((1, ELEMS), F32),
                pltpu.VMEM((3, BASIS, BASIS), F32),
                pltpu.VMEM((4, NODES, BASIS), F32),
                pltpu.VMEM((NROWS, 128), jnp.int32),
                pltpu.VMEM((QUANT, ROWS, ELEMS), F32),
                pltpu.VMEM((4 * NROWS, ELEMS), F32),
                pltpu.VMEM((QUANT, ROWS, ELEMS), F32),
                pltpu.VMEM((4 * NROWS, ELEMS), F32),
                pltpu.VMEM((3, 128, 128), F32),
                pltpu.VMEM((4, NROWS, 128), F32),
                pltpu.VMEM((3 * ROWS, 128), BF16),
                pltpu.VMEM((3 * ROWS, 128), BF16),
                pltpu.VMEM((ROWS, 384), BF16),
                pltpu.VMEM((ROWS, 384), BF16),
                pltpu.VMEM((6 * ROWS, 128), BF16),
                pltpu.VMEM((4 * NROWS, 128), BF16),
                pltpu.VMEM((ROWS, 256), BF16),
                pltpu.VMEM((2 * ELEMS, SLOTS), BF16),
                pltpu.VMEM((2 * ELEMS, FACES), BF16),
                pltpu.VMEM((SLOTS, ELEMS), BF16),
                pltpu.VMEM((16, 128), jnp.int32),
                pltpu.VMEM((4, 8, ELEMS), F32),
                pltpu.VMEM((8, FACES), F32),
                pltpu.VMEM((8, SLOTS), F32),
                pltpu.VMEM((8, SLOTS), jnp.int32),
                pltpu.VMEM((8, FACES), jnp.int32),
                pltpu.VMEM((8, SLOTS), jnp.int32),
                pltpu.VMEM((NROWS, SLOTS), jnp.int32),
                pltpu.VMEM((NROWS, FACES), jnp.int32),
                pltpu.VMEM((NROWS, SLOTS), jnp.int32),
                pltpu.VMEM((40, ELEMS), F32),
                pltpu.VMEM((8, SLOTS), F32),
                pltpu.VMEM((OFFSETS, 32, 128), F32),
                pltpu.VMEM((OFFSETS, 32, 128), F32),
                pltpu.VMEM((OFFSETS, 8, 128), F32),
                pltpu.VMEM((2, OFFSETS, 8, 128), F32),
                pltpu.SemaphoreType.DMA((20,)),
                pltpu.SemaphoreType.DMA((OFFSETS,)),
                pltpu.SemaphoreType.DMA((2, OFFSETS)),
            ],
            compiler_params=pltpu.CompilerParams(
                collective_id=0, has_side_effects=True, vmem_limit_bytes=64 * 1024 * 1024
            ),
        )(*operands)

    result = call(
        jnp.transpose(initial_dofs, (1, 0, 2)),
        cluster.reshape(1, ELEMS),
        neighbours,
        orientation,
        send_slots,
        recv_slots,
        inv_jacobian,
        jnp.transpose(normals, (1, 0, 2)),
        face_area,
        bulk_modulus.reshape(1, ELEMS),
        inv_density.reshape(1, ELEMS),
        deriv_mats,
        jnp.transpose(face_proj, (1, 0, 2)),
        jnp.asarray(turn_table()),
    )
    return jnp.transpose(result, (1, 0, 2))


def solution(mesh):
    return jax.shard_map(
        body,
        mesh=mesh,
        in_specs=(
            P(None, None, "dom"),
            P("dom"),
            P(None, "dom"),
            P(None, "dom"),
            P(None, "dom"),
            P(None, "dom"),
            P(None, None, "dom"),
            P(None, None, "dom"),
            P(None, "dom"),
            P("dom"),
            P("dom"),
            P(),
            P(),
        ),
        out_specs=P(None, None, "dom"),
        check_vma=False,
    )
```

```python
import math

import jax
import jax.numpy as jnp
import numpy as np
from jax import lax
from jax.experimental import pallas as pl
from jax.experimental.pallas import tpu as pltpu
from jax.sharding import PartitionSpec as P

SUBSTEPS = 4
STEP_LENGTH = 0.3
VMEM_BYTES = 55112 * 1024
QUANT = 4
BASIS = 35
ROWS = 40
NODES = 15
NROWS = 16
ELEMS = 256
FACES = 4 * ELEMS
OFFSETS = 8
CAP = 64
SLOTS = OFFSETS * CAP
F32, BF16 = jnp.float32, jnp.bfloat16
TILES = (0, 3, 1, 2)
FAR_FIRST = (0, 7, 1, 6, 2, 5, 3, 4)
PAIRS = ((0, 0), (1, 1), (2, 2), (0, 1), (0, 2), (1, 2))


def node_orders():
    nodes = [(i, j) for i in range(5) for j in range(5 - i)]
    place = {node: position for position, node in enumerate(nodes)}
    turns = [(0, 1, 2), (1, 2, 0), (2, 0, 1), (0, 2, 1), (2, 1, 0), (1, 0, 2)]
    table = []
    for turn in turns:
        row = []
        for node in nodes:
            corner = (node[0], node[1], 4 - node[0] - node[1])
            row.append(place[corner[turn[0]], corner[turn[1]]])
        table.append(row)
    return table


def turn_table():
    out = np.full((NROWS, 128), NODES, np.int32)
    for t, row in enumerate(node_orders()):
        out[:NODES, t] = row
    return out


def dot(a, b):
    return lax.dot_general(a, b, (((1,), (0,)), ((), ())), preferred_element_type=F32)


def halves(x):
    hi = x.astype(BF16).astype(F32)
    return hi, x - hi


def stack3(x):
    hi, lo = halves(x)
    return jnp.concatenate([hi, lo, hi, jnp.zeros((8, x.shape[1]), F32)], axis=0).astype(BF16)


def left3(a):
    hi, lo = halves(a)
    return (hi + pltpu.roll(hi, 40, 1) + pltpu.roll(lo, 80, 1)).astype(BF16)


def kernel(
    n_dev,
    dofs, cluster, neighbours, orientation, send_slots, recv_slots, jac, normals, area, bulk, invd,
    deriv, proj, turns, out,
    dofs_v, cluster_v, neigh_v, code_v, send_v, recv_v, jac_v, normal_v, area_v, bulk_v, invd_v,
    deriv_v, proj_v, turns_v,
    u_s, a_s, own_s, near_s, pad_s, fpad_s, grad_s, gradt_s, div_s, divt_s, second_s,
    trace_s, lift_s, flux1_s, flux2_s, p_s, pick_send, pick_local, place_recv, slot_s, zn_s, zline_s,
    zslot_s, face_send, face_local, face_recv, turn_send, turn_local, turn_recv, coef_s,
    tell_s, send0_buf, recv0_buf, send_buf, recv_buf,
    in_sem, send_sem, recv_sem,
):
    me = lax.axis_index("dom")
    steps = [k - 4 if k < 4 else k - 3 for k in range(OFFSETS)]
    partner = [lax.rem(me + (step + n_dev), n_dev) for step in steps]
    there = [me >= -step if step < 0 else me < n_dev - step for step in steps]
    barrier = pltpu.get_barrier_semaphore()
    for k in FAR_FIRST:

        @pl.when(there[k])
        def _():
            pl.semaphore_signal(
                barrier, inc=1, device_id=(partner[k],), device_id_type=pl.DeviceIdType.MESH
            )

    loads = {}

    def load(name, source, target):
        loads.setdefault(name, []).append((source, target))

    load("recv", recv_slots, recv_v)
    load("send", send_slots, send_v)
    load("code", orientation, code_v)
    load("bulk", bulk, bulk_v)
    load("invd", invd, invd_v)
    load("normal", normals, normal_v)
    load("deriv", deriv, deriv_v)
    for q in range(QUANT):
        load("dofs", dofs.at[:, q, :], dofs_v.at[q])
    load("jac", jac, jac_v)
    for f in range(4):
        load("proj", proj.at[:, f, :], proj_v.at[f])
    load("cluster", cluster, cluster_v)
    load("neigh", neighbours, neigh_v)
    load("area", area, area_v)
    load("turns", turns, turns_v)
    count = 0
    for name in loads:
        copies = []
        for source, target in loads[name]:
            copies.append(pltpu.make_async_copy(source, target, in_sem.at[count]))
            copies[-1].start()
            count += 1
        loads[name] = copies

    def ready(*names):
        for name in names:
            for copy in loads[name]:
                copy.wait()

    low = lax.broadcasted_iota(jnp.int32, (8, 128), 1) < CAP
    low1 = lax.broadcasted_iota(jnp.int32, (1, 128), 1) < CAP
    pad_s[...] = jnp.zeros_like(pad_s)
    fpad_s[...] = jnp.zeros_like(fpad_s)
    u_s[...] = jnp.zeros_like(u_s)
    slot_s[...] = jnp.zeros((16, 128), jnp.int32)

    ready("recv", "send")
    slot_s[0:8, 0:CAP] = send_v[...]
    slot_s[8:16, 0:CAP] = recv_v[...]
    both = slot_s[...]
    both = both + pltpu.roll(both, CAP, 1)

    def slot_row(first):
        tiles = [
            jnp.where(
                low1,
                both[first + 2 * p : first + 2 * p + 1],
                both[first + 2 * p + 1 : first + 2 * p + 2],
            )
            for p in TILES
        ]
        row = jnp.concatenate(tiles, axis=1)
        one, zero = jnp.ones_like(row), jnp.zeros_like(row)
        face = (
            jnp.where(row >= ELEMS, one, zero)
            + jnp.where(row >= 2 * ELEMS, one, zero)
            + jnp.where(row >= 3 * ELEMS, one, zero)
        )
        elem = jnp.where(row >= 0, row - face * ELEMS, -one)
        face = jnp.where(row >= 0, face, -one)
        return face, elem

    send_face, send_elem = slot_row(0)
    recv_face, recv_elem = slot_row(8)
    elem_rows = lax.broadcasted_iota(jnp.int32, (ELEMS, SLOTS), 0)
    pick = jnp.where(elem_rows == send_elem, 1.0, 0.0).astype(BF16)
    pick_send[0:ELEMS] = pick
    pick_send[ELEMS:] = pick

    ready("code", "bulk", "invd", "normal")
    bulk_r, invd_r = bulk_v[...], invd_v[...]
    imp = jnp.sqrt(bulk_r / invd_r)
    code = code_v[...]
    one4, zero4 = jnp.ones_like(code), jnp.zeros_like(code)
    source_face = (
        jnp.where(code >= 6, one4, zero4)
        + jnp.where(code >= 12, one4, zero4)
        + jnp.where(code >= 18, one4, zero4)
    )
    turn = code - 6 * source_face
    turn_f = turn.astype(F32)
    znormal = [normal_v[i] * imp for i in range(3)]
    table = []
    for f in range(4):
        zn_s[f] = jnp.zeros((8, ELEMS), F32)
        for i in range(3):
            zn_s[f, i : i + 1] = znormal[i][f : f + 1]
        zn_s[f, 3:4] = turn_f[f : f + 1]
        table.append(zn_s[f])
    table = jnp.concatenate(table, axis=0)
    t_hi, t_rest = halves(table)
    t_mid, t_lo = halves(t_rest)
    table = jnp.concatenate([t_hi, t_mid, t_lo], axis=0).astype(BF16)
    seen = dot(table, jnp.where(elem_rows == recv_elem, 1.0, 0.0).astype(BF16))
    seen = seen[0:32] + seen[32:64] + seen[64:96]
    tell = jnp.zeros((8, SLOTS), F32)
    for f in range(4):
        tell = jnp.where(recv_face == f, seen[8 * f : 8 * f + 8], tell)
    tell_s[...] = tell

    ready("deriv")
    for j in range(3):
        pad_s[j, 0:BASIS, 0:BASIS] = deriv_v[j]
    d = [pad_s[j] for j in range(3)]
    grad = jnp.concatenate([m[0:ROWS] for m in d], axis=0)
    grad_s[...] = left3(grad)

    def set_div(ref, mats):
        wide = (
            mats[0][0:ROWS]
            + pltpu.roll(mats[1][0:ROWS], 40, 1)
            + pltpu.roll(mats[2][0:ROWS], 80, 1)
        )
        hi, lo = halves(wide)
        ref[...] = jnp.concatenate([hi, hi, lo], axis=1).astype(BF16)

    set_div(div_s, d)
    products = dot(grad_s[...], jnp.concatenate([stack3(m[0:ROWS]) for m in d], axis=1))
    second = []
    for j, k in PAIRS:
        term = products[j * ROWS : (j + 1) * ROWS, k * 128 : (k + 1) * 128]
        if j != k:
            term = term + products[k * ROWS : (k + 1) * ROWS, j * 128 : (j + 1) * 128]
        second.append(term)
    second_s[...] = left3(jnp.concatenate(second, axis=0))

    ready("jac", "dofs")
    kappa = bulk_r * invd_r
    g = [[jac_v[j, i : i + 1, :] for i in range(3)] for j in range(3)]
    for j in range(3):
        for i in range(3):
            coef_s[3 * j + i : 3 * j + i + 1] = g[j][i]
            coef_s[9 + 3 * j + i : 10 + 3 * j + i] = -invd_r * g[j][i]
    for c, (j, k) in enumerate(PAIRS):
        coef_s[18 + c : 19 + c] = kappa * (
            g[j][0] * g[k][0] + g[j][1] * g[k][1] + g[j][2] * g[k][2]
        )
    for q in range(QUANT):
        u_s[q, 0:BASIS] = dofs_v[q]
    ready("proj", "cluster")
    for f in range(4):
        fpad_s[f, 0:NODES, 0:BASIS] = proj_v[f]
    faces = jnp.concatenate([fpad_s[f] for f in range(4)], axis=0)
    trace_s[...] = left3(faces)

    def coef(row):
        return coef_s[row : row + 1]

    def contra(v):
        return [
            coef(3 * j) * v[0] + coef(3 * j + 1) * v[1] + coef(3 * j + 2) * v[2] for j in range(3)
        ]

    def stack_div(w):
        parts = [halves(x) for x in w]
        pad = jnp.zeros((8, ELEMS), F32)
        his = [p[0] for p in parts] + [pad]
        los = [p[1] for p in parts] + [pad]
        return jnp.concatenate(his + los + his, axis=0).astype(BF16)

    def twice(e):
        total = coef(18) * e[0:ROWS]
        for c_at in range(1, 6):
            total = total + coef(18 + c_at) * e[c_at * ROWS : (c_at + 1) * ROWS]
        return total

    def predict(s):
        kind = cluster_v[...]
        s_vec = jnp.full(kind.shape, 0, jnp.int32) + s
        odd = jnp.bitwise_and(s_vec, 1)
        zero = jnp.zeros_like(kind)
        phase = jnp.where(kind == 0, zero, jnp.where(kind == 1, odd, s_vec))
        begin = phase.astype(F32) * STEP_LENGTH
        finish = begin + STEP_LENGTH
        b_pow, f_pow, c = begin, finish, []
        for k in range(5):
            c.append((f_pow - b_pow) * (1.0 / math.factorial(k + 1)))
            b_pow, f_pow = b_pow * begin, f_pow * finish
        left = jnp.where(
            kind == 0, zero, jnp.where(kind == 1, 1 - odd, jnp.bitwise_and(s_vec + 1, 3))
        )
        p0, p1, p2 = u_s[0], p_s[0], p_s[1]
        u = [u_s[i + 1] for i in range(3)]
        e12 = dot(second_s[...], jnp.concatenate([stack3(p1), stack3(p2)], axis=1))
        p3, p4 = twice(e12[:, 0:ELEMS]), twice(e12[:, ELEMS:])
        slope = dot(grad_s[...], stack3(c[1] * p0 + c[2] * p1 + c[3] * p2 + c[4] * p3))
        j_all = [c[0] * p0 + c[1] * p1 + c[2] * p2 + c[3] * p3 + c[4] * p4]
        for i in range(3):
            total = c[0] * u[i]
            for j in range(3):
                total = total + coef(9 + 3 * j + i) * slope[j * ROWS : (j + 1) * ROWS]
            j_all.append(total)
        return j_all, left == 0

    def first_terms():
        p_s[0] = -bulk_v[...] * dot(div_s[...], stack_div(contra([u_s[i + 1] for i in range(3)])))
        p_s[1] = twice(dot(second_s[...], stack3(u_s[0])))

    def two_parts(rows):
        parts = [halves(x) for x in rows]
        his = jnp.concatenate([p[0] for p in parts], axis=0)
        los = jnp.concatenate([p[1] for p in parts], axis=0)
        return jnp.concatenate([his, los], axis=1).astype(BF16)

    def chosen(parts, faces):
        first, second = parts[0:8], parts[8:16]
        for f in range(1, 4):
            mask = faces == f
            first = jnp.where(mask, parts[f * 16 : f * 16 + 8], first)
            second = jnp.where(mask, parts[f * 16 + 8 : f * 16 + 16], second)
        return first, second

    def set_turns(ref, turn_row):
        table = turns_v[...]
        for half in range(2):
            rows = slice(8 * half, 8 * half + 8)
            places = jnp.broadcast_to(table[rows, 0:1], (8, turn_row.shape[1]))
            for t in range(1, 6):
                places = jnp.where(turn_row == t, table[rows, t : t + 1], places)
            ref[rows] = places

    def turned(first, second, places):
        out = []
        for half in range(2):
            place = places[8 * half : 8 * half + 8]
            row = jnp.bitwise_and(place, 7)
            out.append(
                jnp.where(
                    place < 8,
                    jnp.take_along_axis(first, row, axis=0),
                    jnp.take_along_axis(second, row, axis=0),
                )
            )
        return out

    def packed(x0, x1):
        x1 = pltpu.roll(x1, CAP, 1)
        return jnp.where(low, x0, x1), jnp.where(low, x1, x0)

    def unpacked(even, odd):
        return pltpu.roll(jnp.where(low, odd, even), CAP, 1), jnp.where(low, even, odd)

    def first_copy(k):
        return pltpu.make_async_remote_copy(
            src_ref=send0_buf.at[k],
            dst_ref=recv0_buf.at[OFFSETS - 1 - k],
            send_sem=send_sem.at[k],
            recv_sem=recv_sem.at[0, OFFSETS - 1 - k],
            device_id=(partner[k],),
            device_id_type=pl.DeviceIdType.MESH,
        )

    def later_copy(s):
        parity = lax.rem(s, 2)

        def at(k):
            return pltpu.make_async_remote_copy(
                src_ref=send_buf.at[k],
                dst_ref=recv_buf.at[parity, OFFSETS - 1 - k],
                send_sem=send_sem.at[k],
                recv_sem=recv_sem.at[parity, OFFSETS - 1 - k],
                device_id=(partner[k],),
                device_id_type=pl.DeviceIdType.MESH,
            )

        return at

    def start(copy, rows):
        for k in rows:
            pl.when(there[k])(lambda k=k: copy(k).start())

    def finish_sends(copy):
        for k in FAR_FIRST:
            pl.when(there[k])(lambda k=k: copy(k).wait_send())

    def arrive(copy):
        for k in FAR_FIRST[::-1]:
            pl.when(there[k])(lambda k=k: copy(OFFSETS - 1 - k).wait_recv())

    def meanwhile(j_all, j_two, traced, done):
        at_face = dot(j_two, pick_local[...])
        mix = at_face[0:ROWS]
        for i in range(3):
            mix = mix - zline_s[i : i + 1] * at_face[(i + 1) * ROWS : (i + 2) * ROWS]
        first, second = chosen(dot(trace_s[...], stack3(mix)), face_local[...])
        first, second = turned(first, second, turn_local[...])
        for f in range(4):
            rows = slice(f * NROWS, (f + 1) * NROWS)
            near_s[f * NROWS : f * NROWS + 8] += first[:, f * ELEMS : (f + 1) * ELEMS]
            near_s[f * NROWS + 8 : f * NROWS + 16] += second[:, f * ELEMS : (f + 1) * ELEMS]
            mine = traced[rows, 0:ELEMS]
            for i in range(3):
                mine = mine + zn_s[f, i : i + 1] * traced[rows, (i + 1) * ELEMS : (i + 2) * ELEMS]
            a_s[rows] += mine
        own = [own_s[q] + j_all[q] for q in range(QUANT)]
        change_p = bulk_v[...] * dot(divt_s[...], stack_div(contra(own[1:])))
        slope = dot(gradt_s[...], stack3(own[0]))
        change = [change_p]
        for i in range(3):
            total = coef(9 + i) * slope[0:ROWS]
            for j in range(1, 3):
                total = total + coef(9 + 3 * j + i) * slope[j * ROWS : (j + 1) * ROWS]
            change.append(-total)
        for q in range(QUANT):
            own_s[q] = jnp.where(done, 0.0, own[q])
            u_s[q] = jnp.where(done, u_s[q] + change[q], u_s[q])
        first_terms()

    def complete(r0, r1, done):
        r0h, r0l = halves(r0)
        r1h, r1l = halves(r1)
        slot_face = face_recv[...]
        his, los = [], []
        for f in range(4):
            mask = slot_face == f
            his += [jnp.where(mask, r0h, 0.0), jnp.where(mask, r1h, 0.0)]
            los += [jnp.where(mask, r0l, 0.0), jnp.where(mask, r1l, 0.0)]
        placed = dot(jnp.concatenate(his + los, axis=0).astype(BF16), place_recv[...])
        near_all = near_s[...] + placed[0:64] + placed[64:128]
        a_all = a_s[...]
        near_s[...] = jnp.where(done, 0.0, near_all)
        a_s[...] = jnp.where(done, 0.0, a_all)
        flux, slopes = [[], [], [], []], [[], [], []]
        for f in range(4):
            rows = slice(f * NROWS, (f + 1) * NROWS)
            own_f = a_all[rows]
            far_f = jnp.where(neigh_v[f : f + 1] == -1, own_f, near_all[rows])
            flux[0].append(coef(24 + f) * (own_f - far_f))
            plus = own_f + far_f
            for i in range(3):
                flux[i + 1].append(coef(28 + 3 * f + i) * plus)
                slopes[i].append(coef(40 + 3 * f + i) * plus)
        flux = jnp.concatenate([jnp.concatenate(rows, axis=0) for rows in flux], axis=1)
        hi, lo = halves(flux)
        flux = jnp.concatenate([hi, lo, hi, lo], axis=0).astype(BF16)
        hi, lo = halves(jnp.concatenate([x for rows in slopes for x in rows], axis=0))
        pad = jnp.zeros((64, ELEMS), F32)
        slopes = jnp.concatenate([hi, pad, lo, pad, hi, pad], axis=0).astype(BF16)
        change_1 = bulk_v[...] * dot(flux1_s[...], slopes)
        change_2 = twice(dot(flux2_s[...], flux[:, 0:ELEMS]))
        p_s[0] = jnp.where(done, p_s[0] + change_1, p_s[0])
        p_s[1] = jnp.where(done, p_s[1] - change_2, p_s[1])
        lifted = dot(lift_s[...], flux)
        for q in range(QUANT):
            part = lifted[:, q * ELEMS : (q + 1) * ELEMS]
            u_s[q] = jnp.where(done, u_s[q] - part, u_s[q])

    def traces(j_all):
        return dot(trace_s[...], jnp.concatenate([stack3(x) for x in j_all], axis=1))

    first_terms()
    j_all, done = predict(0)
    traced = traces(j_all)
    face_rows = two_parts([traced[:, q * ELEMS : (q + 1) * ELEMS] for q in range(QUANT)])
    at_slot = dot(face_rows, pick_send[...])
    last_row = lax.broadcasted_iota(jnp.int32, (8, SLOTS), 0) == 7
    for q in range(QUANT):
        x = [jnp.zeros((8, SLOTS), F32)] * 2
        for f in range(4):
            for half in range(2):
                row = q * 64 + f * NROWS + 8 * half
                x[half] = jnp.where(send_face == f, at_slot[row : row + 8], x[half])
        x[1] = jnp.where(last_row, tell[q : q + 1], x[1])
        for pos, p in enumerate(TILES):
            cols = slice(pos * 128, (pos + 1) * 128)
            b0, b1 = packed(x[0][:, cols], x[1][:, cols])
            send0_buf[2 * p, q * 8 : q * 8 + 8] = b0
            send0_buf[2 * p + 1, q * 8 : q * 8 + 8] = b1
    pl.semaphore_wait(barrier, sum(t.astype(jnp.int32) for t in there))
    start(first_copy, FAR_FIRST)

    ready("neigh", "area", "turns")
    for k in range(OFFSETS):

        @pl.when(jnp.logical_not(there[k]))
        def _():
            recv0_buf[k] = jnp.zeros((32, 128), F32)
            recv_buf[0, k] = jnp.zeros((8, 128), F32)
            recv_buf[1, k] = jnp.zeros((8, 128), F32)

    a_s[...] = jnp.zeros_like(a_s)
    near_s[...] = jnp.zeros_like(near_s)
    own_s[...] = jnp.zeros_like(own_s)
    elem_rows1 = lax.broadcasted_iota(jnp.int32, (ELEMS, ELEMS), 0)
    for f in range(4):
        cols = slice(f * ELEMS, (f + 1) * ELEMS)
        pick = jnp.where(elem_rows1 == neigh_v[f : f + 1], 1.0, 0.0).astype(BF16)
        pick_local[0:ELEMS, cols] = pick
        pick_local[ELEMS:, cols] = pick
        for i in range(3):
            zline_s[i : i + 1, cols] = znormal[i][f : f + 1]
        face_local[:, cols] = jnp.broadcast_to(source_face[f : f + 1], (8, ELEMS))
        size = area_v[f : f + 1]
        coef_s[24 + f : 25 + f] = 0.5 * size * bulk_r / imp
        for i in range(3):
            row = 28 + 3 * f + i
            coef_s[row : row + 1] = 0.5 * size * invd_r * normal_v[i, f : f + 1]
        for j in range(3):
            row = 40 + 3 * f + j
            coef_s[row : row + 1] = (0.5 * size * invd_r) * (
                g[j][0] * normal_v[0, f : f + 1]
                + g[j][1] * normal_v[1, f : f + 1]
                + g[j][2] * normal_v[2, f : f + 1]
            )
    elem_lanes = lax.broadcasted_iota(jnp.int32, (128, ELEMS), 1).astype(F32)
    recv_float = recv_elem.astype(F32)
    for p in range(4):
        column = jnp.broadcast_to(recv_float[:, p * 128 : (p + 1) * 128], (128, 128)).T
        column = jnp.concatenate([column, column], axis=1)
        place_recv[p * 128 : (p + 1) * 128] = jnp.where(column == elem_lanes, 1.0, 0.0).astype(BF16)
    face_recv[...] = jnp.broadcast_to(recv_face, (8, SLOTS))
    dt = [pad_s[j].T for j in range(3)]
    gradt_s[...] = left3(jnp.concatenate([m[0:ROWS] for m in dt], axis=0))
    set_div(divt_s, dt)
    lifts = jnp.concatenate([faces, jnp.zeros((64, 128), F32)], axis=0).T[0:ROWS]

    def left4(a):
        hi, lo = halves(a)
        return jnp.concatenate(
            [hi + pltpu.roll(hi, 64, 1), lo + pltpu.roll(lo, 64, 1)], axis=1
        ).astype(BF16)

    lift_s[...] = left4(lifts)
    lifts = stack3(lifts)
    flux2_s[...] = left4(dot(second_s[...], lifts))
    slope = dot(grad_s[...], lifts)
    wide = jnp.concatenate(
        [slope[0:ROWS] + pltpu.roll(slope[ROWS : 2 * ROWS], 64, 1), slope[2 * ROWS :]], axis=1
    )
    hi, lo = halves(wide)
    flux1_s[...] = jnp.concatenate([hi, hi, lo], axis=1).astype(BF16)
    face_send[...] = jnp.broadcast_to(send_face, (8, SLOTS))
    set_turns(turn_local, jnp.concatenate([turn[f : f + 1] for f in range(4)], axis=1))
    set_turns(turn_recv, tell[3:4].astype(jnp.int32))

    meanwhile(j_all, two_parts(j_all), traced, done)
    arrive(first_copy)
    chi = []
    for q in range(QUANT):
        tiles = [
            unpacked(
                recv0_buf[2 * p, q * 8 : q * 8 + 8], recv0_buf[2 * p + 1, q * 8 : q * 8 + 8]
            )
            for p in TILES
        ]
        both = [jnp.concatenate([t[half] for t in tiles], axis=1) for half in range(2)]
        zslot_s[q : q + 1] = both[1][7:8]
        if q == 0:
            chi = both
        else:
            chi = [x - tell_s[q - 1 : q] * y for x, y in zip(chi, both)]
    r0, r1 = turned(chi[0], chi[1], turn_recv[...])
    complete(r0, r1, done)
    set_turns(turn_send, zslot_s[3:4].astype(jnp.int32))
    finish_sends(first_copy)

    def step(s, carry):
        j_all, done = predict(s)
        j_two = two_parts(j_all)
        copy = later_copy(s)
        for half in range(2):
            cols = slice(half * 256, (half + 1) * 256)
            at_slot = dot(j_two, pick_send[:, cols])
            mix = at_slot[0:ROWS]
            for i in range(3):
                mix = mix - zslot_s[i : i + 1, cols] * at_slot[(i + 1) * ROWS : (i + 2) * ROWS]
            first, second = chosen(dot(trace_s[...], stack3(mix)), face_send[:, cols])
            first, second = turned(first, second, turn_send[:, cols])
            rows = []
            for at in range(2):
                p = TILES[2 * half + at]
                lanes = slice(at * 128, (at + 1) * 128)
                send_buf[2 * p], send_buf[2 * p + 1] = packed(first[:, lanes], second[:, lanes])
                rows += [2 * p, 2 * p + 1]
            start(copy, [k for k in FAR_FIRST if k in rows])
        meanwhile(j_all, j_two, traces(j_all), done)
        arrive(copy)
        parity = lax.rem(s, 2)
        tiles = [unpacked(recv_buf[parity, 2 * p], recv_buf[parity, 2 * p + 1]) for p in TILES]
        r0 = jnp.concatenate([t[0] for t in tiles], axis=1)
        r1 = jnp.concatenate([t[1] for t in tiles], axis=1)
        complete(r0, r1, done)
        finish_sends(copy)
        return carry

    lax.fori_loop(1, SUBSTEPS, step, 0)
    for q in range(QUANT):
        out[q] = u_s[q, 0:BASIS]


def body(
    initial_dofs, cluster, neighbours, orientation, send_slots, recv_slots, inv_jacobian, normals,
    face_area, bulk_modulus, inv_density, deriv_mats, face_proj,
):
    n_dev = lax.axis_size("dom")
    hbm = pl.BlockSpec(memory_space=pltpu.HBM)

    def call(*operands):
        return pl.pallas_call(
            lambda *refs: kernel(n_dev, *refs),
            out_shape=pltpu.VMEM((QUANT, BASIS, ELEMS), F32),
            in_specs=[hbm] * len(operands),
            out_specs=pl.BlockSpec(memory_space=pltpu.VMEM),
            scratch_shapes=[
                pltpu.VMEM((QUANT, BASIS, ELEMS), F32),
                pltpu.VMEM((1, ELEMS), jnp.int32),
                pltpu.VMEM((4, ELEMS), jnp.int32),
                pltpu.VMEM((4, ELEMS), jnp.int32),
                pltpu.VMEM((OFFSETS, CAP), jnp.int32),
                pltpu.VMEM((OFFSETS, CAP), jnp.int32),
                pltpu.VMEM((3, 3, ELEMS), F32),
                pltpu.VMEM((3, 4, ELEMS), F32),
                pltpu.VMEM((4, ELEMS), F32),
                pltpu.VMEM((1, ELEMS), F32),
                pltpu.VMEM((1, ELEMS), F32),
                pltpu.VMEM((3, BASIS, BASIS), F32),
                pltpu.VMEM((4, NODES, BASIS), F32),
                pltpu.VMEM((NROWS, 128), jnp.int32),
                pltpu.VMEM((QUANT, ROWS, ELEMS), F32),
                pltpu.VMEM((4 * NROWS, ELEMS), F32),
                pltpu.VMEM((QUANT, ROWS, ELEMS), F32),
                pltpu.VMEM((4 * NROWS, ELEMS), F32),
                pltpu.VMEM((3, 128, 128), F32),
                pltpu.VMEM((4, NROWS, 128), F32),
                pltpu.VMEM((3 * ROWS, 128), BF16),
                pltpu.VMEM((3 * ROWS, 128), BF16),
                pltpu.VMEM((ROWS, 384), BF16),
                pltpu.VMEM((ROWS, 384), BF16),
                pltpu.VMEM((6 * ROWS, 128), BF16),
                pltpu.VMEM((4 * NROWS, 128), BF16),
                pltpu.VMEM((ROWS, 256), BF16),
                pltpu.VMEM((ROWS, 768), BF16),
                pltpu.VMEM((6 * ROWS, 256), BF16),
                pltpu.VMEM((2, ROWS, ELEMS), F32),
                pltpu.VMEM((2 * ELEMS, SLOTS), BF16),
                pltpu.VMEM((2 * ELEMS, FACES), BF16),
                pltpu.VMEM((SLOTS, ELEMS), BF16),
                pltpu.VMEM((16, 128), jnp.int32),
                pltpu.VMEM((4, 8, ELEMS), F32),
                pltpu.VMEM((8, FACES), F32),
                pltpu.VMEM((8, SLOTS), F32),
                pltpu.VMEM((8, SLOTS), jnp.int32),
                pltpu.VMEM((8, FACES), jnp.int32),
                pltpu.VMEM((8, SLOTS), jnp.int32),
                pltpu.VMEM((NROWS, SLOTS), jnp.int32),
                pltpu.VMEM((NROWS, FACES), jnp.int32),
                pltpu.VMEM((NROWS, SLOTS), jnp.int32),
                pltpu.VMEM((56, ELEMS), F32),
                pltpu.VMEM((8, SLOTS), F32),
                pltpu.VMEM((OFFSETS, 32, 128), F32),
                pltpu.VMEM((OFFSETS, 32, 128), F32),
                pltpu.VMEM((OFFSETS, 8, 128), F32),
                pltpu.VMEM((2, OFFSETS, 8, 128), F32),
                pltpu.SemaphoreType.DMA((20,)),
                pltpu.SemaphoreType.DMA((OFFSETS,)),
                pltpu.SemaphoreType.DMA((2, OFFSETS)),
            ],
            compiler_params=pltpu.CompilerParams(
                collective_id=0, has_side_effects=True, vmem_limit_bytes=VMEM_BYTES
            ),
        )(*operands)

    result = call(
        jnp.transpose(initial_dofs, (1, 0, 2)),
        cluster.reshape(1, ELEMS),
        neighbours,
        orientation,
        send_slots,
        recv_slots,
        inv_jacobian,
        jnp.transpose(normals, (1, 0, 2)),
        face_area,
        bulk_modulus.reshape(1, ELEMS),
        inv_density.reshape(1, ELEMS),
        deriv_mats,
        jnp.transpose(face_proj, (1, 0, 2)),
        jnp.asarray(turn_table()),
    )
    return result


def solution(mesh):
    return jax.shard_map(
        body,
        mesh=mesh,
        in_specs=(
            P(None, None, "dom"),
            P("dom"),
            P(None, "dom"),
            P(None, "dom"),
            P(None, "dom"),
            P(None, "dom"),
            P(None, None, "dom"),
            P(None, None, "dom"),
            P(None, "dom"),
            P("dom"),
            P("dom"),
            P(),
            P(),
        ),
        out_specs=P(None, None, "dom"),
        check_vma=False,
    )
```

```python
import math

import jax
import jax.numpy as jnp
import numpy as np
from jax import lax
from jax.experimental import pallas as pl
from jax.experimental.pallas import tpu as pltpu
from jax.sharding import PartitionSpec as P

SUBSTEPS = 4
STEP_LENGTH = 0.3
VMEM_BYTES = 55112 * 1024
QUANT = 4
BASIS = 35
ROWS = 40
NODES = 15
NROWS = 16
ELEMS = 256
FACES = 4 * ELEMS
OFFSETS = 8
CAP = 64
SLOTS = OFFSETS * CAP
F32, BF16 = jnp.float32, jnp.bfloat16
TILES = (0, 3, 1, 2)
FAR_FIRST = (0, 7, 1, 6, 2, 5, 3, 4)
PAIRS = ((0, 0), (1, 1), (2, 2), (0, 1), (0, 2), (1, 2))


def node_orders():
    nodes = [(i, j) for i in range(5) for j in range(5 - i)]
    place = {node: position for position, node in enumerate(nodes)}
    turns = [(0, 1, 2), (1, 2, 0), (2, 0, 1), (0, 2, 1), (2, 1, 0), (1, 0, 2)]
    table = []
    for turn in turns:
        row = []
        for node in nodes:
            corner = (node[0], node[1], 4 - node[0] - node[1])
            row.append(place[corner[turn[0]], corner[turn[1]]])
        table.append(row)
    return table


def turn_table():
    out = np.full((NROWS, 128), NODES, np.int32)
    for t, row in enumerate(node_orders()):
        out[:NODES, t] = row
    return out


def dot(a, b):
    return lax.dot_general(a, b, (((1,), (0,)), ((), ())), preferred_element_type=F32)


def halves(x):
    hi = x.astype(BF16).astype(F32)
    return hi, x - hi


def stack3(x):
    hi, lo = halves(x)
    return jnp.concatenate([hi, lo, hi, jnp.zeros((8, x.shape[1]), F32)], axis=0).astype(BF16)


def left3(a):
    hi, lo = halves(a)
    return (hi + pltpu.roll(hi, 40, 1) + pltpu.roll(lo, 80, 1)).astype(BF16)


def kernel(
    n_dev,
    dofs, cluster, neighbours, orientation, send_slots, recv_slots, jac, normals, area, bulk, invd,
    deriv, proj, turns, out,
    dofs_v, cluster_v, neigh_v, code_v, send_v, recv_v, jac_v, normal_v, area_v, bulk_v, invd_v,
    deriv_v, proj_v, turns_v,
    u_s, a_s, own_s, near_s, pad_s, fpad_s, grad_s, gradt_s, div_s, divt_s, second_s,
    trace_s, lift_s, flux1_s, flux2_s, p_s, j_s, wide_s, gslot_s, yslot_s, pick_send, pick_local, place_recv, slot_s, zn_s, zline_s,
    zslot_s, face_send, face_local, face_recv, turn_send, turn_local, turn_recv, coef_s,
    tell_s, send0_buf, recv0_buf, send_buf, recv_buf,
    in_sem, send_sem, recv_sem,
):
    me = lax.axis_index("dom")
    steps = [k - 4 if k < 4 else k - 3 for k in range(OFFSETS)]
    partner = [lax.rem(me + (step + n_dev), n_dev) for step in steps]
    there = [me >= -step if step < 0 else me < n_dev - step for step in steps]
    barrier = pltpu.get_barrier_semaphore()
    for k in FAR_FIRST:

        @pl.when(there[k])
        def _():
            pl.semaphore_signal(
                barrier, inc=1, device_id=(partner[k],), device_id_type=pl.DeviceIdType.MESH
            )

    loads = {}

    def load(name, source, target):
        loads.setdefault(name, []).append((source, target))

    load("recv", recv_slots, recv_v)
    load("send", send_slots, send_v)
    load("code", orientation, code_v)
    load("bulk", bulk, bulk_v)
    load("invd", invd, invd_v)
    load("normal", normals, normal_v)
    load("deriv", deriv, deriv_v)
    for q in range(QUANT):
        load("dofs", dofs.at[:, q, :], dofs_v.at[q])
    load("jac", jac, jac_v)
    for f in range(4):
        load("proj", proj.at[:, f, :], proj_v.at[f])
    load("cluster", cluster, cluster_v)
    load("neigh", neighbours, neigh_v)
    load("area", area, area_v)
    load("turns", turns, turns_v)
    count = 0
    for name in loads:
        copies = []
        for source, target in loads[name]:
            copies.append(pltpu.make_async_copy(source, target, in_sem.at[count]))
            copies[-1].start()
            count += 1
        loads[name] = copies

    def ready(*names):
        for name in names:
            for copy in loads[name]:
                copy.wait()

    low = lax.broadcasted_iota(jnp.int32, (8, 128), 1) < CAP
    low1 = lax.broadcasted_iota(jnp.int32, (1, 128), 1) < CAP
    pad_s[...] = jnp.zeros_like(pad_s)
    fpad_s[...] = jnp.zeros_like(fpad_s)
    u_s[...] = jnp.zeros_like(u_s)
    slot_s[...] = jnp.zeros((16, 128), jnp.int32)

    ready("recv", "send")
    slot_s[0:8, 0:CAP] = send_v[...]
    slot_s[8:16, 0:CAP] = recv_v[...]
    both = slot_s[...]
    both = both + pltpu.roll(both, CAP, 1)

    def slot_row(first):
        tiles = [
            jnp.where(
                low1,
                both[first + 2 * p : first + 2 * p + 1],
                both[first + 2 * p + 1 : first + 2 * p + 2],
            )
            for p in TILES
        ]
        row = jnp.concatenate(tiles, axis=1)
        one, zero = jnp.ones_like(row), jnp.zeros_like(row)
        face = (
            jnp.where(row >= ELEMS, one, zero)
            + jnp.where(row >= 2 * ELEMS, one, zero)
            + jnp.where(row >= 3 * ELEMS, one, zero)
        )
        elem = jnp.where(row >= 0, row - face * ELEMS, -one)
        face = jnp.where(row >= 0, face, -one)
        return face, elem

    send_face, send_elem = slot_row(0)
    recv_face, recv_elem = slot_row(8)
    elem_rows = lax.broadcasted_iota(jnp.int32, (ELEMS, SLOTS), 0)
    pick = jnp.where(elem_rows == send_elem, 1.0, 0.0).astype(BF16)
    pick_send[0:ELEMS] = pick
    pick_send[ELEMS:] = pick

    ready("code", "bulk", "invd", "normal")
    bulk_r, invd_r = bulk_v[...], invd_v[...]
    imp = jnp.sqrt(bulk_r / invd_r)
    code = code_v[...]
    one4, zero4 = jnp.ones_like(code), jnp.zeros_like(code)
    source_face = (
        jnp.where(code >= 6, one4, zero4)
        + jnp.where(code >= 12, one4, zero4)
        + jnp.where(code >= 18, one4, zero4)
    )
    turn = code - 6 * source_face
    turn_f = turn.astype(F32)
    znormal = [normal_v[i] * imp for i in range(3)]
    table = []
    for f in range(4):
        zn_s[f] = jnp.zeros((8, ELEMS), F32)
        for i in range(3):
            zn_s[f, i : i + 1] = znormal[i][f : f + 1]
        zn_s[f, 3:4] = turn_f[f : f + 1]
        table.append(zn_s[f])
    table = jnp.concatenate(table, axis=0)
    t_hi, t_rest = halves(table)
    t_mid, t_lo = halves(t_rest)
    table = jnp.concatenate([t_hi, t_mid, t_lo], axis=0).astype(BF16)
    seen = dot(table, jnp.where(elem_rows == recv_elem, 1.0, 0.0).astype(BF16))
    seen = seen[0:32] + seen[32:64] + seen[64:96]
    tell = jnp.zeros((8, SLOTS), F32)
    for f in range(4):
        tell = jnp.where(recv_face == f, seen[8 * f : 8 * f + 8], tell)
    tell_s[...] = tell

    ready("deriv")
    for j in range(3):
        pad_s[j, 0:BASIS, 0:BASIS] = deriv_v[j]
    d = [pad_s[j] for j in range(3)]
    grad = jnp.concatenate([m[0:ROWS] for m in d], axis=0)
    grad_s[...] = left3(grad)

    def set_div(ref, mats):
        wide = (
            mats[0][0:ROWS]
            + pltpu.roll(mats[1][0:ROWS], 40, 1)
            + pltpu.roll(mats[2][0:ROWS], 80, 1)
        )
        hi, lo = halves(wide)
        ref[...] = jnp.concatenate([hi, hi, lo], axis=1).astype(BF16)

    set_div(div_s, d)
    products = dot(grad_s[...], jnp.concatenate([stack3(m[0:ROWS]) for m in d], axis=1))
    second = []
    for j, k in PAIRS:
        term = products[j * ROWS : (j + 1) * ROWS, k * 128 : (k + 1) * 128]
        if j != k:
            term = term + products[k * ROWS : (k + 1) * ROWS, j * 128 : (j + 1) * 128]
        second.append(term)
    second_s[...] = left3(jnp.concatenate(second, axis=0))

    ready("jac", "dofs")
    kappa = bulk_r * invd_r
    g = [[jac_v[j, i : i + 1, :] for i in range(3)] for j in range(3)]
    for j in range(3):
        for i in range(3):
            coef_s[3 * j + i : 3 * j + i + 1] = g[j][i]
            coef_s[9 + 3 * j + i : 10 + 3 * j + i] = -invd_r * g[j][i]
    for c, (j, k) in enumerate(PAIRS):
        coef_s[18 + c : 19 + c] = kappa * (
            g[j][0] * g[k][0] + g[j][1] * g[k][1] + g[j][2] * g[k][2]
        )
    for q in range(QUANT):
        u_s[q, 0:BASIS] = dofs_v[q]
    ready("proj", "cluster")
    for f in range(4):
        fpad_s[f, 0:NODES, 0:BASIS] = proj_v[f]
    faces = jnp.concatenate([fpad_s[f] for f in range(4)], axis=0)
    trace_s[...] = left3(faces)

    def coef(row):
        return coef_s[row : row + 1]

    def contra(v):
        return [
            coef(3 * j) * v[0] + coef(3 * j + 1) * v[1] + coef(3 * j + 2) * v[2] for j in range(3)
        ]

    def stack_div(w):
        parts = [halves(x) for x in w]
        pad = jnp.zeros((8, ELEMS), F32)
        his = [p[0] for p in parts] + [pad]
        los = [p[1] for p in parts] + [pad]
        return jnp.concatenate(his + los + his, axis=0).astype(BF16)

    def twice(e):
        total = coef(18) * e[0:ROWS]
        for c_at in range(1, 6):
            total = total + coef(18 + c_at) * e[c_at * ROWS : (c_at + 1) * ROWS]
        return total

    def weights(s):
        kind = cluster_v[...]
        s_vec = jnp.full(kind.shape, 0, jnp.int32) + s
        phase = jnp.where(
            kind == 0,
            jnp.zeros_like(kind),
            jnp.where(kind == 1, jnp.bitwise_and(s_vec, 1), s_vec),
        )
        begin = phase.astype(F32) * STEP_LENGTH
        finish = begin + STEP_LENGTH
        b_pow, f_pow, c = begin, finish, []
        for k in range(5):
            c.append((f_pow - b_pow) * (1.0 / math.factorial(k + 1)))
            b_pow, f_pow = b_pow * begin, f_pow * finish
        return c

    def series(s):
        c = weights(s)
        p0, p1, p2 = u_s[0], p_s[0], p_s[1]
        e12 = dot(second_s[...], jnp.concatenate([stack3(p1), stack3(p2)], axis=1))
        p3, p4 = twice(e12[:, 0:ELEMS]), twice(e12[:, ELEMS:])
        slope_of = c[1] * p0 + c[2] * p1 + c[3] * p2 + c[4] * p3
        pressure = c[0] * p0 + c[1] * p1 + c[2] * p2 + c[3] * p3 + c[4] * p4
        return pressure, slope_of, [c[0] * u_s[i + 1] for i in range(3)]

    def velocities(slope_of, start_u):
        slope = dot(grad_s[...], stack3(slope_of))
        out = []
        for i in range(3):
            total = start_u[i]
            for j in range(3):
                total = total + coef(9 + 3 * j + i) * slope[j * ROWS : (j + 1) * ROWS]
            out.append(total)
        return out

    def ending(s):
        kind = cluster_v[...]
        s_vec = jnp.full(kind.shape, 0, jnp.int32) + s
        left = jnp.where(
            kind == 0,
            jnp.zeros_like(kind),
            jnp.where(
                kind == 1, 1 - jnp.bitwise_and(s_vec, 1), jnp.bitwise_and(s_vec + 1, 3)
            ),
        )
        return left == 0

    def first_terms():
        p_s[0] = -bulk_v[...] * dot(div_s[...], stack_div(contra([u_s[i + 1] for i in range(3)])))
        p_s[1] = twice(dot(second_s[...], stack3(u_s[0])))

    def two_parts(rows):
        parts = [halves(x) for x in rows]
        his = jnp.concatenate([p[0] for p in parts], axis=0)
        los = jnp.concatenate([p[1] for p in parts], axis=0)
        return jnp.concatenate([his, los], axis=1).astype(BF16)

    def chosen(parts, faces):
        first, second = parts[0:8], parts[8:16]
        for f in range(1, 4):
            mask = faces == f
            first = jnp.where(mask, parts[f * 16 : f * 16 + 8], first)
            second = jnp.where(mask, parts[f * 16 + 8 : f * 16 + 16], second)
        return first, second

    def set_turns(ref, turn_row):
        table = turns_v[...]
        for half in range(2):
            rows = slice(8 * half, 8 * half + 8)
            places = jnp.broadcast_to(table[rows, 0:1], (8, turn_row.shape[1]))
            for t in range(1, 6):
                places = jnp.where(turn_row == t, table[rows, t : t + 1], places)
            ref[rows] = places

    def turned(first, second, places):
        out = []
        for half in range(2):
            place = places[8 * half : 8 * half + 8]
            row = jnp.bitwise_and(place, 7)
            out.append(
                jnp.where(
                    place < 8,
                    jnp.take_along_axis(first, row, axis=0),
                    jnp.take_along_axis(second, row, axis=0),
                )
            )
        return out

    def packed(x0, x1):
        x1 = pltpu.roll(x1, CAP, 1)
        return jnp.where(low, x0, x1), jnp.where(low, x1, x0)

    def unpacked(even, odd):
        return pltpu.roll(jnp.where(low, odd, even), CAP, 1), jnp.where(low, even, odd)

    def first_copy(k):
        return pltpu.make_async_remote_copy(
            src_ref=send0_buf.at[k],
            dst_ref=recv0_buf.at[OFFSETS - 1 - k],
            send_sem=send_sem.at[k],
            recv_sem=recv_sem.at[0, OFFSETS - 1 - k],
            device_id=(partner[k],),
            device_id_type=pl.DeviceIdType.MESH,
        )

    def later_copy(s):
        parity = lax.rem(s, 2)

        def at(k):
            return pltpu.make_async_remote_copy(
                src_ref=send_buf.at[k],
                dst_ref=recv_buf.at[parity, OFFSETS - 1 - k],
                send_sem=send_sem.at[k],
                recv_sem=recv_sem.at[parity, OFFSETS - 1 - k],
                device_id=(partner[k],),
                device_id_type=pl.DeviceIdType.MESH,
            )

        return at

    def start(copy, rows):
        for k in rows:
            pl.when(there[k])(lambda k=k: copy(k).start())

    def finish_sends(copy):
        for k in FAR_FIRST:
            pl.when(there[k])(lambda k=k: copy(k).wait_send())

    def arrive(copy, rows):
        for k in FAR_FIRST[::-1]:
            if k in rows:
                pl.when(there[k])(lambda k=k: copy(OFFSETS - 1 - k).wait_recv())

    def meanwhile(j_all, j_two, traced, done, last=False):
        at_face = dot(j_two, pick_local[...])
        mix = at_face[0:ROWS]
        for i in range(3):
            mix = mix - zline_s[i : i + 1] * at_face[(i + 1) * ROWS : (i + 2) * ROWS]
        first, second = chosen(dot(trace_s[...], stack3(mix)), face_local[...])
        first, second = turned(first, second, turn_local[...])
        flux = [[], [], [], []]
        for f in range(4):
            rows = slice(f * NROWS, (f + 1) * NROWS)
            cols = slice(f * ELEMS, (f + 1) * ELEMS)
            near = near_s[rows] + jnp.concatenate([first[:, cols], second[:, cols]], axis=0)
            near_s[rows] = near
            mine = a_s[rows] + traced[rows, 0:ELEMS]
            for i in range(3):
                mine = mine + zn_s[f, i : i + 1] * traced[rows, (i + 1) * ELEMS : (i + 2) * ELEMS]
            a_s[rows] = jnp.where(done, 0.0, mine)
            far = jnp.where(neigh_v[f : f + 1] == -1, mine, near)
            flux[0].append(coef(24 + f) * (mine - far))
            plus = mine + far
            for i in range(3):
                flux[i + 1].append(coef(28 + 3 * f + i) * plus)
        lifted = dot(lift_s[...], stack4(flux))
        own = [own_s[q] + j_all[q] for q in range(QUANT)]
        change_p = bulk_v[...] * dot(divt_s[...], stack_div(contra(own[1:])))
        slope = dot(gradt_s[...], stack3(own[0]))
        change = [change_p]
        for i in range(3):
            total = coef(9 + i) * slope[0:ROWS]
            for j in range(1, 3):
                total = total + coef(9 + 3 * j + i) * slope[j * ROWS : (j + 1) * ROWS]
            change.append(-total)
        for q in range(QUANT):
            own_s[q] = jnp.where(done, 0.0, own[q])
            part = lifted[:, q * ELEMS : (q + 1) * ELEMS]
            u_s[q] = jnp.where(done, u_s[q] + (change[q] - part), u_s[q])
        if not last:
            first_terms()

    def stack4(flux):
        flux = jnp.concatenate([jnp.concatenate(rows, axis=0) for rows in flux], axis=1)
        hi, lo = halves(flux)
        return jnp.concatenate([hi, lo, hi, lo], axis=0).astype(BF16)

    def placed(r0, r1, cols):
        r0h, r0l = halves(r0)
        r1h, r1l = halves(r1)
        slot_face = face_recv[:, cols]
        his, los = [], []
        for f in range(4):
            mask = slot_face == f
            his += [jnp.where(mask, r0h, 0.0), jnp.where(mask, r1h, 0.0)]
            los += [jnp.where(mask, r0l, 0.0), jnp.where(mask, r1l, 0.0)]
        both = dot(jnp.concatenate(his + los, axis=0).astype(BF16), place_recv[cols])
        return both[0:64] + both[64:128]

    def next_terms(flux, slopes, done):
        hi, lo = halves(jnp.concatenate([x for rows in slopes for x in rows], axis=0))
        pad = jnp.zeros((64, ELEMS), F32)
        slopes = jnp.concatenate([hi, pad, lo, pad, hi, pad], axis=0).astype(BF16)
        change_1 = bulk_v[...] * dot(flux1_s[...], slopes)
        change_2 = twice(dot(flux2_s[...], flux[:, 0:ELEMS]))
        p_s[0] = jnp.where(done, p_s[0] + change_1, p_s[0])
        p_s[1] = jnp.where(done, p_s[1] - change_2, p_s[1])

    def complete(chi, done, last=False):
        near_s[...] = jnp.where(done, 0.0, near_s[...] + chi)
        flux, slopes = [[], [], [], []], [[], [], []]
        for f in range(4):
            part = chi[f * NROWS : (f + 1) * NROWS]
            flux[0].append(-coef(24 + f) * part)
            for i in range(3):
                flux[i + 1].append(coef(28 + 3 * f + i) * part)
                slopes[i].append(coef(40 + 3 * f + i) * part)
        flux = stack4(flux)
        if not last:
            next_terms(flux, slopes, done)
        lifted = dot(lift_s[...], flux)
        for q in range(QUANT):
            part = lifted[:, q * ELEMS : (q + 1) * ELEMS]
            u_s[q] = jnp.where(done, u_s[q] - part, u_s[q])

    def traces(j_all):
        return dot(trace_s[...], jnp.concatenate([stack3(x) for x in j_all], axis=1))

    first_terms()
    pressure, slope_of, start_u = series(0)
    j_all, done = [pressure] + velocities(slope_of, start_u), ending(0)
    traced = traces(j_all)
    face_rows = two_parts([traced[:, q * ELEMS : (q + 1) * ELEMS] for q in range(QUANT)])
    at_slot = dot(face_rows, pick_send[...])
    last_row = lax.broadcasted_iota(jnp.int32, (8, SLOTS), 0) == 7
    for q in range(QUANT):
        x = [jnp.zeros((8, SLOTS), F32)] * 2
        for f in range(4):
            for half in range(2):
                row = q * 64 + f * NROWS + 8 * half
                x[half] = jnp.where(send_face == f, at_slot[row : row + 8], x[half])
        x[1] = jnp.where(last_row, tell[q : q + 1], x[1])
        for pos, p in enumerate(TILES):
            cols = slice(pos * 128, (pos + 1) * 128)
            b0, b1 = packed(x[0][:, cols], x[1][:, cols])
            send0_buf[2 * p, q * 8 : q * 8 + 8] = b0
            send0_buf[2 * p + 1, q * 8 : q * 8 + 8] = b1
    pl.semaphore_wait(barrier, sum(t.astype(jnp.int32) for t in there))
    start(first_copy, FAR_FIRST)

    ready("neigh", "area", "turns")
    for k in range(OFFSETS):

        @pl.when(jnp.logical_not(there[k]))
        def _():
            recv0_buf[k] = jnp.zeros((32, 128), F32)
            recv_buf[0, k] = jnp.zeros((8, 128), F32)
            recv_buf[1, k] = jnp.zeros((8, 128), F32)

    a_s[...] = jnp.zeros_like(a_s)
    near_s[...] = jnp.zeros_like(near_s)
    own_s[...] = jnp.zeros_like(own_s)
    elem_rows1 = lax.broadcasted_iota(jnp.int32, (ELEMS, ELEMS), 0)
    for f in range(4):
        cols = slice(f * ELEMS, (f + 1) * ELEMS)
        pick = jnp.where(elem_rows1 == neigh_v[f : f + 1], 1.0, 0.0).astype(BF16)
        pick_local[0:ELEMS, cols] = pick
        pick_local[ELEMS:, cols] = pick
        for i in range(3):
            zline_s[i : i + 1, cols] = znormal[i][f : f + 1]
        face_local[:, cols] = jnp.broadcast_to(source_face[f : f + 1], (8, ELEMS))
        size = area_v[f : f + 1]
        coef_s[24 + f : 25 + f] = 0.5 * size * bulk_r / imp
        for i in range(3):
            row = 28 + 3 * f + i
            coef_s[row : row + 1] = 0.5 * size * invd_r * normal_v[i, f : f + 1]
        for j in range(3):
            row = 40 + 3 * f + j
            coef_s[row : row + 1] = (0.5 * size * invd_r) * (
                g[j][0] * normal_v[0, f : f + 1]
                + g[j][1] * normal_v[1, f : f + 1]
                + g[j][2] * normal_v[2, f : f + 1]
            )
    elem_lanes = lax.broadcasted_iota(jnp.int32, (128, ELEMS), 1).astype(F32)
    recv_float = recv_elem.astype(F32)
    for p in range(4):
        column = jnp.broadcast_to(recv_float[:, p * 128 : (p + 1) * 128], (128, 128)).T
        column = jnp.concatenate([column, column], axis=1)
        place_recv[p * 128 : (p + 1) * 128] = jnp.where(column == elem_lanes, 1.0, 0.0).astype(BF16)
    face_recv[...] = jnp.broadcast_to(recv_face, (8, SLOTS))
    dt = [pad_s[j].T for j in range(3)]
    gradt_s[...] = left3(jnp.concatenate([m[0:ROWS] for m in dt], axis=0))
    set_div(divt_s, dt)
    lifts = jnp.concatenate([faces, jnp.zeros((64, 128), F32)], axis=0).T[0:ROWS]

    def left4(a):
        hi, lo = halves(a)
        return jnp.concatenate(
            [hi + pltpu.roll(hi, 64, 1), lo + pltpu.roll(lo, 64, 1)], axis=1
        ).astype(BF16)

    lift_s[...] = left4(lifts)
    slope = dot(trace_s[...], jnp.concatenate([stack3(m[0:ROWS]) for m in d], axis=1))
    wide_s[:, 0:128] = trace_s[...]
    for j in range(3):
        wide_s[:, (j + 1) * 128 : (j + 2) * 128] = left3(slope[:, j * 128 : (j + 1) * 128])
    table = jnp.concatenate([coef_s[9:18], jnp.zeros((7, ELEMS), F32)], axis=0)
    t_hi, t_rest = halves(table)
    t_mid, t_lo = halves(t_rest)
    seen = dot(
        jnp.concatenate([t_hi, t_mid, t_lo], axis=0).astype(BF16), pick_send[0:ELEMS]
    )
    gslot_s[...] = seen[0:16] + seen[16:32] + seen[32:48]
    lifts = stack3(lifts)
    flux2_s[...] = left4(dot(second_s[...], lifts))
    slope = dot(grad_s[...], lifts)
    wide = jnp.concatenate(
        [slope[0:ROWS] + pltpu.roll(slope[ROWS : 2 * ROWS], 64, 1), slope[2 * ROWS :]], axis=1
    )
    hi, lo = halves(wide)
    flux1_s[...] = jnp.concatenate([hi, hi, lo], axis=1).astype(BF16)
    face_send[...] = jnp.broadcast_to(send_face, (8, SLOTS))
    set_turns(turn_local, jnp.concatenate([turn[f : f + 1] for f in range(4)], axis=1))
    set_turns(turn_recv, tell[3:4].astype(jnp.int32))

    meanwhile(j_all, two_parts(j_all), traced, done)
    finish_sends(first_copy)
    total = None
    for half in (1, 0):
        pair = TILES[2 * half : 2 * half + 2]
        cols = slice(half * 256, (half + 1) * 256)
        arrive(first_copy, [2 * p + at for p in pair for at in range(2)])
        for q in range(QUANT):
            rows = slice(q * 8, q * 8 + 8)
            tiles = [unpacked(recv0_buf[2 * p, rows], recv0_buf[2 * p + 1, rows]) for p in pair]
            both = [jnp.concatenate([t[at] for t in tiles], axis=1) for at in range(2)]
            zslot_s[q : q + 1, cols] = both[1][7:8]
            if q == 0:
                chi = both
            else:
                chi = [x - tell_s[q - 1 : q, cols] * y for x, y in zip(chi, both)]
        r0, r1 = turned(chi[0], chi[1], turn_recv[:, cols])
        part = placed(r0, r1, cols)
        total = part if total is None else total + part
    complete(total, done)
    set_turns(turn_send, zslot_s[3:4].astype(jnp.int32))
    for j in range(3):
        total = zslot_s[0:1] * gslot_s[3 * j : 3 * j + 1]
        for i in range(1, 3):
            total = total + zslot_s[i : i + 1] * gslot_s[3 * j + i : 3 * j + i + 1]
        yslot_s[j : j + 1] = -total

    def advance(s):
        pressure, slope_of, start_u = series(s)
        j_s[0], j_s[1] = pressure, slope_of
        five = two_parts([pressure] + start_u + [slope_of, jnp.zeros((8, ELEMS), F32)])
        copy = later_copy(s)
        at_slot = dot(five, pick_send[...])
        mix = at_slot[0:ROWS]
        for i in range(3):
            mix = mix - zslot_s[i : i + 1] * at_slot[(i + 1) * ROWS : (i + 2) * ROWS]
        steep = at_slot[4 * ROWS : 5 * ROWS]
        mix = [stack3(mix)] + [stack3(yslot_s[j : j + 1] * steep) for j in range(3)]
        first, second = chosen(dot(wide_s[...], jnp.concatenate(mix, axis=0)), face_send[...])
        first, second = turned(first, second, turn_send[...])
        for pos, p in enumerate(TILES):
            lanes = slice(pos * 128, (pos + 1) * 128)
            send_buf[2 * p], send_buf[2 * p + 1] = packed(first[:, lanes], second[:, lanes])
        start(copy, FAR_FIRST)

    def finish(s, last=False):
        copy, done = later_copy(s), ending(s)
        c = weights(s)
        j_all = [j_s[0]] + velocities(j_s[1], [c[0] * u_s[i + 1] for i in range(3)])
        meanwhile(j_all, two_parts(j_all), traces(j_all), done, last)
        finish_sends(copy)
        parity = lax.rem(s, 2)
        total = None
        for half in (1, 0):
            pair = TILES[2 * half : 2 * half + 2]
            cols = slice(half * 256, (half + 1) * 256)
            arrive(copy, [2 * p + at for p in pair for at in range(2)])
            tiles = [unpacked(recv_buf[parity, 2 * p], recv_buf[parity, 2 * p + 1]) for p in pair]
            r0 = jnp.concatenate([t[0] for t in tiles], axis=1)
            r1 = jnp.concatenate([t[1] for t in tiles], axis=1)
            part = placed(r0, r1, cols)
            total = part if total is None else total + part
        complete(total, done, last)

    def step(s, carry):
        finish(s)
        advance(s + 1)
        return carry

    advance(1)
    lax.fori_loop(1, SUBSTEPS - 1, step, 0)
    finish(SUBSTEPS - 1, last=True)
    for q in range(QUANT):
        out[q] = u_s[q, 0:BASIS]


def body(
    initial_dofs, cluster, neighbours, orientation, send_slots, recv_slots, inv_jacobian, normals,
    face_area, bulk_modulus, inv_density, deriv_mats, face_proj,
):
    n_dev = lax.axis_size("dom")
    hbm = pl.BlockSpec(memory_space=pltpu.HBM)

    def call(*operands):
        return pl.pallas_call(
            lambda *refs: kernel(n_dev, *refs),
            out_shape=pltpu.VMEM((QUANT, BASIS, ELEMS), F32),
            in_specs=[hbm] * len(operands),
            out_specs=pl.BlockSpec(memory_space=pltpu.VMEM),
            scratch_shapes=[
                pltpu.VMEM((QUANT, BASIS, ELEMS), F32),
                pltpu.VMEM((1, ELEMS), jnp.int32),
                pltpu.VMEM((4, ELEMS), jnp.int32),
                pltpu.VMEM((4, ELEMS), jnp.int32),
                pltpu.VMEM((OFFSETS, CAP), jnp.int32),
                pltpu.VMEM((OFFSETS, CAP), jnp.int32),
                pltpu.VMEM((3, 3, ELEMS), F32),
                pltpu.VMEM((3, 4, ELEMS), F32),
                pltpu.VMEM((4, ELEMS), F32),
                pltpu.VMEM((1, ELEMS), F32),
                pltpu.VMEM((1, ELEMS), F32),
                pltpu.VMEM((3, BASIS, BASIS), F32),
                pltpu.VMEM((4, NODES, BASIS), F32),
                pltpu.VMEM((NROWS, 128), jnp.int32),
                pltpu.VMEM((QUANT, ROWS, ELEMS), F32),
                pltpu.VMEM((4 * NROWS, ELEMS), F32),
                pltpu.VMEM((QUANT, ROWS, ELEMS), F32),
                pltpu.VMEM((4 * NROWS, ELEMS), F32),
                pltpu.VMEM((3, 128, 128), F32),
                pltpu.VMEM((4, NROWS, 128), F32),
                pltpu.VMEM((3 * ROWS, 128), BF16),
                pltpu.VMEM((3 * ROWS, 128), BF16),
                pltpu.VMEM((ROWS, 384), BF16),
                pltpu.VMEM((ROWS, 384), BF16),
                pltpu.VMEM((6 * ROWS, 128), BF16),
                pltpu.VMEM((4 * NROWS, 128), BF16),
                pltpu.VMEM((ROWS, 256), BF16),
                pltpu.VMEM((ROWS, 768), BF16),
                pltpu.VMEM((6 * ROWS, 256), BF16),
                pltpu.VMEM((2, ROWS, ELEMS), F32),
                pltpu.VMEM((2, ROWS, ELEMS), F32),
                pltpu.VMEM((4 * NROWS, 512), BF16),
                pltpu.VMEM((16, SLOTS), F32),
                pltpu.VMEM((8, SLOTS), F32),
                pltpu.VMEM((2 * ELEMS, SLOTS), BF16),
                pltpu.VMEM((2 * ELEMS, FACES), BF16),
                pltpu.VMEM((SLOTS, ELEMS), BF16),
                pltpu.VMEM((16, 128), jnp.int32),
                pltpu.VMEM((4, 8, ELEMS), F32),
                pltpu.VMEM((8, FACES), F32),
                pltpu.VMEM((8, SLOTS), F32),
                pltpu.VMEM((8, SLOTS), jnp.int32),
                pltpu.VMEM((8, FACES), jnp.int32),
                pltpu.VMEM((8, SLOTS), jnp.int32),
                pltpu.VMEM((NROWS, SLOTS), jnp.int32),
                pltpu.VMEM((NROWS, FACES), jnp.int32),
                pltpu.VMEM((NROWS, SLOTS), jnp.int32),
                pltpu.VMEM((56, ELEMS), F32),
                pltpu.VMEM((8, SLOTS), F32),
                pltpu.VMEM((OFFSETS, 32, 128), F32),
                pltpu.VMEM((OFFSETS, 32, 128), F32),
                pltpu.VMEM((OFFSETS, 8, 128), F32),
                pltpu.VMEM((2, OFFSETS, 8, 128), F32),
                pltpu.SemaphoreType.DMA((20,)),
                pltpu.SemaphoreType.DMA((OFFSETS,)),
                pltpu.SemaphoreType.DMA((2, OFFSETS)),
            ],
            compiler_params=pltpu.CompilerParams(
                collective_id=0, has_side_effects=True, vmem_limit_bytes=VMEM_BYTES
            ),
        )(*operands)

    result = call(
        jnp.transpose(initial_dofs, (1, 0, 2)),
        cluster.reshape(1, ELEMS),
        neighbours,
        orientation,
        send_slots,
        recv_slots,
        inv_jacobian,
        jnp.transpose(normals, (1, 0, 2)),
        face_area,
        bulk_modulus.reshape(1, ELEMS),
        inv_density.reshape(1, ELEMS),
        deriv_mats,
        jnp.transpose(face_proj, (1, 0, 2)),
        jnp.asarray(turn_table()),
    )
    return result


def solution(mesh):
    return jax.shard_map(
        body,
        mesh=mesh,
        in_specs=(
            P(None, None, "dom"),
            P("dom"),
            P(None, "dom"),
            P(None, "dom"),
            P(None, "dom"),
            P(None, "dom"),
            P(None, None, "dom"),
            P(None, None, "dom"),
            P(None, "dom"),
            P("dom"),
            P("dom"),
            P(),
            P(),
        ),
        out_specs=P(None, None, "dom"),
        check_vma=False,
    )
```

```python
import math

import jax
import jax.numpy as jnp
import numpy as np
from jax import lax
from jax.experimental import pallas as pl
from jax.experimental.pallas import tpu as pltpu
from jax.sharding import PartitionSpec as P

SUBSTEPS = 4
STEP_LENGTH = 0.3
VMEM_BYTES = 55112 * 1024
QUANT = 4
BASIS = 35
ROWS = 40
NODES = 15
NROWS = 16
ELEMS = 256
FACES = 4 * ELEMS
OFFSETS = 8
CAP = 64
SLOTS = OFFSETS * CAP
F32, BF16 = jnp.float32, jnp.bfloat16
TILES = (0, 3, 1, 2)
FAR_FIRST = (0, 7, 1, 6, 2, 5, 3, 4)
PAIRS = ((0, 0), (1, 1), (2, 2), (0, 1), (0, 2), (1, 2))


def node_orders():
    nodes = [(i, j) for i in range(5) for j in range(5 - i)]
    place = {node: position for position, node in enumerate(nodes)}
    turns = [(0, 1, 2), (1, 2, 0), (2, 0, 1), (0, 2, 1), (2, 1, 0), (1, 0, 2)]
    table = []
    for turn in turns:
        row = []
        for node in nodes:
            corner = (node[0], node[1], 4 - node[0] - node[1])
            row.append(place[corner[turn[0]], corner[turn[1]]])
        table.append(row)
    return table


def turn_table():
    out = np.full((NROWS, 128), NODES, np.int32)
    for t, row in enumerate(node_orders()):
        out[:NODES, t] = row
    return out


def dot(a, b):
    return lax.dot_general(a, b, (((1,), (0,)), ((), ())), preferred_element_type=F32)


def halves(x):
    hi = x.astype(BF16).astype(F32)
    return hi, x - hi


def short_halves(x):
    hi = x.astype(BF16)
    return hi, (x - hi.astype(F32)).astype(BF16)


def stack3(x):
    hi, lo = halves(x)
    return jnp.concatenate([hi, lo, hi, jnp.zeros((8, x.shape[1]), F32)], axis=0).astype(BF16)


def left3(a):
    hi, lo = halves(a)
    return (hi + pltpu.roll(hi, 40, 1) + pltpu.roll(lo, 80, 1)).astype(BF16)


def kernel(
    n_dev,
    dofs, cluster, neighbours, orientation, send_slots, recv_slots, jac, normals, area, bulk, invd,
    deriv, proj, turns, out,
    dofs_v, cluster_v, neigh_v, code_v, send_v, recv_v, jac_v, normal_v, area_v, bulk_v, invd_v,
    deriv_v, proj_v, turns_v,
    u_s, a_s, own_s, near_s, pad_s, fpad_s, grad_s, gradt_s, div_s, divt_s, second_s,
    trace_s, lift_s, flux1_s, flux2_s, p_s, j_s, wide_s, gslot_s, yslot_s, pick_send, pick_local, place_recv, slot_s, zn_s, zline_s,
    zslot_s, face_send, face_local, face_recv, turn_send, turn_local, turn_recv, coef_s,
    tell_s, send0_buf, recv0_buf, send_buf, recv_buf,
    in_sem, send_sem, recv_sem,
):
    me = lax.axis_index("dom")
    steps = [k - 4 if k < 4 else k - 3 for k in range(OFFSETS)]
    partner = [lax.rem(me + (step + n_dev), n_dev) for step in steps]
    there = [me >= -step if step < 0 else me < n_dev - step for step in steps]
    barrier = pltpu.get_barrier_semaphore()
    for k in FAR_FIRST:

        @pl.when(there[k])
        def _():
            pl.semaphore_signal(
                barrier, inc=1, device_id=(partner[k],), device_id_type=pl.DeviceIdType.MESH
            )

    loads = {}

    def load(name, source, target):
        loads.setdefault(name, []).append((source, target))

    load("recv", recv_slots, recv_v)
    load("send", send_slots, send_v)
    load("code", orientation, code_v)
    load("bulk", bulk, bulk_v)
    load("invd", invd, invd_v)
    load("normal", normals, normal_v)
    load("deriv", deriv, deriv_v)
    for q in range(QUANT):
        load("dofs", dofs.at[:, q, :], dofs_v.at[q])
    load("jac", jac, jac_v)
    for f in range(4):
        load("proj", proj.at[:, f, :], proj_v.at[f])
    load("cluster", cluster, cluster_v)
    load("neigh", neighbours, neigh_v)
    load("area", area, area_v)
    load("turns", turns, turns_v)
    count = 0
    for name in loads:
        copies = []
        for source, target in loads[name]:
            copies.append(pltpu.make_async_copy(source, target, in_sem.at[count]))
            copies[-1].start()
            count += 1
        loads[name] = copies

    def ready(*names):
        for name in names:
            for copy in loads[name]:
                copy.wait()

    low = lax.broadcasted_iota(jnp.int32, (8, 128), 1) < CAP
    low1 = lax.broadcasted_iota(jnp.int32, (1, 128), 1) < CAP
    pad_s[...] = jnp.zeros_like(pad_s)
    fpad_s[...] = jnp.zeros_like(fpad_s)
    u_s[...] = jnp.zeros_like(u_s)
    slot_s[...] = jnp.zeros((16, 128), jnp.int32)

    ready("recv", "send")
    slot_s[0:8, 0:CAP] = send_v[...]
    slot_s[8:16, 0:CAP] = recv_v[...]
    both = slot_s[...]
    both = both + pltpu.roll(both, CAP, 1)

    def slot_row(first):
        tiles = [
            jnp.where(
                low1,
                both[first + 2 * p : first + 2 * p + 1],
                both[first + 2 * p + 1 : first + 2 * p + 2],
            )
            for p in TILES
        ]
        row = jnp.concatenate(tiles, axis=1)
        one, zero = jnp.ones_like(row), jnp.zeros_like(row)
        face = (
            jnp.where(row >= ELEMS, one, zero)
            + jnp.where(row >= 2 * ELEMS, one, zero)
            + jnp.where(row >= 3 * ELEMS, one, zero)
        )
        elem = jnp.where(row >= 0, row - face * ELEMS, -one)
        face = jnp.where(row >= 0, face, -one)
        return face, elem

    send_face, send_elem = slot_row(0)
    recv_face, recv_elem = slot_row(8)
    elem_rows = lax.broadcasted_iota(jnp.int32, (ELEMS, SLOTS), 0)
    pick = jnp.where(elem_rows == send_elem, 1.0, 0.0).astype(BF16)
    pick_send[0:ELEMS] = pick
    pick_send[ELEMS:] = pick

    ready("code", "bulk", "invd", "normal")
    bulk_r, invd_r = bulk_v[...], invd_v[...]
    imp = jnp.sqrt(bulk_r / invd_r)
    code = code_v[...]
    one4, zero4 = jnp.ones_like(code), jnp.zeros_like(code)
    source_face = (
        jnp.where(code >= 6, one4, zero4)
        + jnp.where(code >= 12, one4, zero4)
        + jnp.where(code >= 18, one4, zero4)
    )
    turn = code - 6 * source_face
    turn_f = turn.astype(F32)
    znormal = [normal_v[i] * imp for i in range(3)]
    table = []
    for f in range(4):
        zn_s[f] = jnp.zeros((8, ELEMS), F32)
        for i in range(3):
            zn_s[f, i : i + 1] = znormal[i][f : f + 1]
        zn_s[f, 3:4] = turn_f[f : f + 1]
        table.append(zn_s[f])
    table = jnp.concatenate(table, axis=0)
    t_hi, t_rest = halves(table)
    t_mid, t_lo = halves(t_rest)
    table = jnp.concatenate([t_hi, t_mid, t_lo], axis=0).astype(BF16)
    seen = dot(table, jnp.where(elem_rows == recv_elem, 1.0, 0.0).astype(BF16))
    seen = seen[0:32] + seen[32:64] + seen[64:96]
    tell = jnp.zeros((8, SLOTS), F32)
    for f in range(4):
        tell = jnp.where(recv_face == f, seen[8 * f : 8 * f + 8], tell)
    tell_s[...] = tell

    ready("deriv")
    for j in range(3):
        pad_s[j, 0:BASIS, 0:BASIS] = deriv_v[j]
    d = [pad_s[j] for j in range(3)]
    grad = jnp.concatenate([m[0:ROWS] for m in d], axis=0)
    grad_s[...] = left3(grad)

    def set_div(ref, mats):
        wide = (
            mats[0][0:ROWS]
            + pltpu.roll(mats[1][0:ROWS], 40, 1)
            + pltpu.roll(mats[2][0:ROWS], 80, 1)
        )
        hi, lo = halves(wide)
        ref[...] = jnp.concatenate([hi, hi, lo], axis=1).astype(BF16)

    set_div(div_s, d)
    products = dot(grad_s[...], jnp.concatenate([stack3(m[0:ROWS]) for m in d], axis=1))
    second = []
    for j, k in PAIRS:
        term = products[j * ROWS : (j + 1) * ROWS, k * 128 : (k + 1) * 128]
        if j != k:
            term = term + products[k * ROWS : (k + 1) * ROWS, j * 128 : (j + 1) * 128]
        second.append(term)
    second_s[...] = left3(jnp.concatenate(second, axis=0))

    ready("jac", "dofs")
    kappa = bulk_r * invd_r
    g = [[jac_v[j, i : i + 1, :] for i in range(3)] for j in range(3)]
    for j in range(3):
        for i in range(3):
            coef_s[3 * j + i : 3 * j + i + 1] = g[j][i]
            coef_s[9 + 3 * j + i : 10 + 3 * j + i] = -invd_r * g[j][i]
    for c, (j, k) in enumerate(PAIRS):
        coef_s[18 + c : 19 + c] = kappa * (
            g[j][0] * g[k][0] + g[j][1] * g[k][1] + g[j][2] * g[k][2]
        )
    for q in range(QUANT):
        u_s[q, 0:BASIS] = dofs_v[q]
    ready("proj", "cluster")
    for f in range(4):
        fpad_s[f, 0:NODES, 0:BASIS] = proj_v[f]
    faces = jnp.concatenate([fpad_s[f] for f in range(4)], axis=0)
    trace_s[...] = left3(faces)

    def coef(row):
        return coef_s[row : row + 1]

    def contra(v):
        return [
            coef(3 * j) * v[0] + coef(3 * j + 1) * v[1] + coef(3 * j + 2) * v[2] for j in range(3)
        ]

    def stack_div(w):
        parts = [halves(x) for x in w]
        pad = jnp.zeros((8, ELEMS), F32)
        his = [p[0] for p in parts] + [pad]
        los = [p[1] for p in parts] + [pad]
        return jnp.concatenate(his + los + his, axis=0).astype(BF16)

    def twice(e):
        total = coef(18) * e[0:ROWS]
        for c_at in range(1, 6):
            total = total + coef(18 + c_at) * e[c_at * ROWS : (c_at + 1) * ROWS]
        return total

    def weights(s):
        kind = cluster_v[...]
        s_vec = jnp.full(kind.shape, 0, jnp.int32) + s
        phase = jnp.where(
            kind == 0,
            jnp.zeros_like(kind),
            jnp.where(kind == 1, jnp.bitwise_and(s_vec, 1), s_vec),
        )
        begin = phase.astype(F32) * STEP_LENGTH
        finish = begin + STEP_LENGTH
        b_pow, f_pow, c = begin, finish, []
        for k in range(5):
            c.append((f_pow - b_pow) * (1.0 / math.factorial(k + 1)))
            b_pow, f_pow = b_pow * begin, f_pow * finish
        return c

    def series(s):
        c = weights(s)
        p0, p1, p2 = u_s[0], p_s[0], p_s[1]
        e12 = dot(second_s[...], jnp.concatenate([stack3(p1), stack3(p2)], axis=1))
        p3, p4 = twice(e12[:, 0:ELEMS]), twice(e12[:, ELEMS:])
        slope_of = c[1] * p0 + c[2] * p1 + c[3] * p2 + c[4] * p3
        pressure = c[0] * p0 + c[1] * p1 + c[2] * p2 + c[3] * p3 + c[4] * p4
        return pressure, slope_of, [c[0] * u_s[i + 1] for i in range(3)]

    def velocities(slope_of, start_u):
        slope = dot(grad_s[...], stack3(slope_of))
        out = []
        for i in range(3):
            total = start_u[i]
            for j in range(3):
                total = total + coef(9 + 3 * j + i) * slope[j * ROWS : (j + 1) * ROWS]
            out.append(total)
        return out

    def ending(s):
        kind = cluster_v[...]
        s_vec = jnp.full(kind.shape, 0, jnp.int32) + s
        left = jnp.where(
            kind == 0,
            jnp.zeros_like(kind),
            jnp.where(
                kind == 1, 1 - jnp.bitwise_and(s_vec, 1), jnp.bitwise_and(s_vec + 1, 3)
            ),
        )
        return left == 0

    def first_terms():
        p_s[0] = -bulk_v[...] * dot(div_s[...], stack_div(contra([u_s[i + 1] for i in range(3)])))
        p_s[1] = twice(dot(second_s[...], stack3(u_s[0])))

    def two_parts(rows):
        return jnp.concatenate(short_halves(jnp.concatenate(rows, axis=0)), axis=1)

    def chosen(parts, faces):
        first, second = parts[0:8], parts[8:16]
        for f in range(1, 4):
            mask = faces == f
            first = jnp.where(mask, parts[f * 16 : f * 16 + 8], first)
            second = jnp.where(mask, parts[f * 16 + 8 : f * 16 + 16], second)
        return first, second

    def set_turns(ref, turn_row):
        table = turns_v[...]
        for half in range(2):
            rows = slice(8 * half, 8 * half + 8)
            places = jnp.broadcast_to(table[rows, 0:1], (8, turn_row.shape[1]))
            for t in range(1, 6):
                places = jnp.where(turn_row == t, table[rows, t : t + 1], places)
            ref[rows] = places

    def turned(first, second, places):
        out = []
        for half in range(2):
            place = places[8 * half : 8 * half + 8]
            row = jnp.bitwise_and(place, 7)
            out.append(
                jnp.where(
                    place < 8,
                    jnp.take_along_axis(first, row, axis=0),
                    jnp.take_along_axis(second, row, axis=0),
                )
            )
        return out

    def packed(x0, x1):
        x1 = pltpu.roll(x1, CAP, 1)
        return jnp.where(low, x0, x1), jnp.where(low, x1, x0)

    def unpacked(even, odd):
        return pltpu.roll(jnp.where(low, odd, even), CAP, 1), jnp.where(low, even, odd)

    def first_copy(k):
        return pltpu.make_async_remote_copy(
            src_ref=send0_buf.at[k],
            dst_ref=recv0_buf.at[OFFSETS - 1 - k],
            send_sem=send_sem.at[k],
            recv_sem=recv_sem.at[0, OFFSETS - 1 - k],
            device_id=(partner[k],),
            device_id_type=pl.DeviceIdType.MESH,
        )

    def later_copy(s):
        parity = lax.rem(s, 2)

        def at(k):
            return pltpu.make_async_remote_copy(
                src_ref=send_buf.at[k],
                dst_ref=recv_buf.at[parity, OFFSETS - 1 - k],
                send_sem=send_sem.at[k],
                recv_sem=recv_sem.at[parity, OFFSETS - 1 - k],
                device_id=(partner[k],),
                device_id_type=pl.DeviceIdType.MESH,
            )

        return at

    def start(copy, rows):
        for k in rows:
            pl.when(there[k])(lambda k=k: copy(k).start())

    def finish_sends(copy):
        for k in FAR_FIRST:
            pl.when(there[k])(lambda k=k: copy(k).wait_send())

    def arrive(copy, rows):
        for k in FAR_FIRST[::-1]:
            if k in rows:
                pl.when(there[k])(lambda k=k: copy(OFFSETS - 1 - k).wait_recv())

    def meanwhile(j_all, j_two, traced, done, last=False):
        at_face = dot(j_two, pick_local[...])
        mix = at_face[0:ROWS]
        for i in range(3):
            mix = mix - zline_s[i : i + 1] * at_face[(i + 1) * ROWS : (i + 2) * ROWS]
        first, second = chosen(dot(trace_s[...], stack3(mix)), face_local[...])
        first, second = turned(first, second, turn_local[...])
        flux = [[], [], [], []]
        for f in range(4):
            rows = slice(f * NROWS, (f + 1) * NROWS)
            cols = slice(f * ELEMS, (f + 1) * ELEMS)
            near = near_s[rows] + jnp.concatenate([first[:, cols], second[:, cols]], axis=0)
            near_s[rows] = near
            mine = a_s[rows] + traced[rows, 0:ELEMS]
            for i in range(3):
                mine = mine + zn_s[f, i : i + 1] * traced[rows, (i + 1) * ELEMS : (i + 2) * ELEMS]
            a_s[rows] = jnp.where(done, 0.0, mine)
            far = jnp.where(neigh_v[f : f + 1] == -1, mine, near)
            flux[0].append(coef(24 + f) * (mine - far))
            plus = mine + far
            for i in range(3):
                flux[i + 1].append(coef(28 + 3 * f + i) * plus)
        lifted = dot(lift_s[...], stack4(flux))
        own = [own_s[q] + j_all[q] for q in range(QUANT)]
        change_p = bulk_v[...] * dot(divt_s[...], stack_div(contra(own[1:])))
        slope = dot(gradt_s[...], stack3(own[0]))
        change = [change_p]
        for i in range(3):
            total = coef(9 + i) * slope[0:ROWS]
            for j in range(1, 3):
                total = total + coef(9 + 3 * j + i) * slope[j * ROWS : (j + 1) * ROWS]
            change.append(-total)
        for q in range(QUANT):
            own_s[q] = jnp.where(done, 0.0, own[q])
            part = lifted[:, q * ELEMS : (q + 1) * ELEMS]
            u_s[q] = jnp.where(done, u_s[q] + (change[q] - part), u_s[q])
        if not last:
            first_terms()

    def stack4(flux):
        flux = jnp.concatenate([jnp.concatenate(rows, axis=0) for rows in flux], axis=1)
        hi, lo = short_halves(flux)
        return jnp.concatenate([hi, lo, hi, lo], axis=0)

    def placed(r0, r1, cols):
        r0h, r0l = halves(r0)
        r1h, r1l = halves(r1)
        slot_face = face_recv[:, cols]
        his, los = [], []
        for f in range(4):
            mask = slot_face == f
            his += [jnp.where(mask, r0h, 0.0), jnp.where(mask, r1h, 0.0)]
            los += [jnp.where(mask, r0l, 0.0), jnp.where(mask, r1l, 0.0)]
        both = dot(jnp.concatenate(his + los, axis=0).astype(BF16), place_recv[cols])
        return both[0:64] + both[64:128]

    def next_terms(flux, slopes, done):
        hi, lo = short_halves(jnp.concatenate([x for rows in slopes for x in rows], axis=0))
        pad = jnp.zeros((64, ELEMS), BF16)
        slopes = jnp.concatenate([hi, pad, lo, pad, hi, pad], axis=0)
        change_1 = bulk_v[...] * dot(flux1_s[...], slopes)
        change_2 = twice(dot(flux2_s[...], flux[:, 0:ELEMS]))
        p_s[0] = jnp.where(done, p_s[0] + change_1, p_s[0])
        p_s[1] = jnp.where(done, p_s[1] - change_2, p_s[1])

    def complete(chi, done, last=False):
        near_s[...] = jnp.where(done, 0.0, near_s[...] + chi)
        flux, slopes = [[], [], [], []], [[], [], []]
        for f in range(4):
            part = chi[f * NROWS : (f + 1) * NROWS]
            flux[0].append(-coef(24 + f) * part)
            for i in range(3):
                flux[i + 1].append(coef(28 + 3 * f + i) * part)
                slopes[i].append(coef(40 + 3 * f + i) * part)
        flux = stack4(flux)
        if not last:
            next_terms(flux, slopes, done)
        lifted = dot(lift_s[...], flux)
        for q in range(QUANT):
            part = lifted[:, q * ELEMS : (q + 1) * ELEMS]
            u_s[q] = jnp.where(done, u_s[q] - part, u_s[q])

    def traces(j_all):
        return dot(trace_s[...], jnp.concatenate([stack3(x) for x in j_all], axis=1))

    first_terms()
    pressure, slope_of, start_u = series(0)
    j_all, done = [pressure] + velocities(slope_of, start_u), ending(0)
    traced = traces(j_all)
    face_rows = two_parts([traced[:, q * ELEMS : (q + 1) * ELEMS] for q in range(QUANT)])
    at_slot = dot(face_rows, pick_send[...])
    last_row = lax.broadcasted_iota(jnp.int32, (8, SLOTS), 0) == 7
    for q in range(QUANT):
        x = [jnp.zeros((8, SLOTS), F32)] * 2
        for f in range(4):
            for half in range(2):
                row = q * 64 + f * NROWS + 8 * half
                x[half] = jnp.where(send_face == f, at_slot[row : row + 8], x[half])
        x[1] = jnp.where(last_row, tell[q : q + 1], x[1])
        for pos, p in enumerate(TILES):
            cols = slice(pos * 128, (pos + 1) * 128)
            b0, b1 = packed(x[0][:, cols], x[1][:, cols])
            send0_buf[2 * p, q * 8 : q * 8 + 8] = b0
            send0_buf[2 * p + 1, q * 8 : q * 8 + 8] = b1
    pl.semaphore_wait(barrier, sum(t.astype(jnp.int32) for t in there))
    start(first_copy, FAR_FIRST)

    ready("neigh", "area", "turns")
    for k in range(OFFSETS):

        @pl.when(jnp.logical_not(there[k]))
        def _():
            recv0_buf[k] = jnp.zeros((32, 128), F32)
            recv_buf[0, k] = jnp.zeros((8, 128), F32)
            recv_buf[1, k] = jnp.zeros((8, 128), F32)

    a_s[...] = jnp.zeros_like(a_s)
    near_s[...] = jnp.zeros_like(near_s)
    own_s[...] = jnp.zeros_like(own_s)
    elem_rows1 = lax.broadcasted_iota(jnp.int32, (ELEMS, ELEMS), 0)
    for f in range(4):
        cols = slice(f * ELEMS, (f + 1) * ELEMS)
        pick = jnp.where(elem_rows1 == neigh_v[f : f + 1], 1.0, 0.0).astype(BF16)
        pick_local[0:ELEMS, cols] = pick
        pick_local[ELEMS:, cols] = pick
        for i in range(3):
            zline_s[i : i + 1, cols] = znormal[i][f : f + 1]
        face_local[:, cols] = jnp.broadcast_to(source_face[f : f + 1], (8, ELEMS))
        size = area_v[f : f + 1]
        coef_s[24 + f : 25 + f] = 0.5 * size * bulk_r / imp
        for i in range(3):
            row = 28 + 3 * f + i
            coef_s[row : row + 1] = 0.5 * size * invd_r * normal_v[i, f : f + 1]
        for j in range(3):
            row = 40 + 3 * f + j
            coef_s[row : row + 1] = (0.5 * size * invd_r) * (
                g[j][0] * normal_v[0, f : f + 1]
                + g[j][1] * normal_v[1, f : f + 1]
                + g[j][2] * normal_v[2, f : f + 1]
            )
    elem_lanes = lax.broadcasted_iota(jnp.int32, (128, ELEMS), 1).astype(F32)
    recv_float = recv_elem.astype(F32)
    for p in range(4):
        column = jnp.broadcast_to(recv_float[:, p * 128 : (p + 1) * 128], (128, 128)).T
        column = jnp.concatenate([column, column], axis=1)
        place_recv[p * 128 : (p + 1) * 128] = jnp.where(column == elem_lanes, 1.0, 0.0).astype(BF16)
    face_recv[...] = jnp.broadcast_to(recv_face, (8, SLOTS))
    dt = [pad_s[j].T for j in range(3)]
    gradt_s[...] = left3(jnp.concatenate([m[0:ROWS] for m in dt], axis=0))
    set_div(divt_s, dt)
    lifts = jnp.concatenate([faces, jnp.zeros((64, 128), F32)], axis=0).T[0:ROWS]

    def left4(a):
        hi, lo = halves(a)
        return jnp.concatenate(
            [hi + pltpu.roll(hi, 64, 1), lo + pltpu.roll(lo, 64, 1)], axis=1
        ).astype(BF16)

    lift_s[...] = left4(lifts)
    slope = dot(trace_s[...], jnp.concatenate([stack3(m[0:ROWS]) for m in d], axis=1))
    wide_s[:, 0:128] = trace_s[...]
    for j in range(3):
        wide_s[:, (j + 1) * 128 : (j + 2) * 128] = left3(slope[:, j * 128 : (j + 1) * 128])
    table = jnp.concatenate([coef_s[9:18], jnp.zeros((7, ELEMS), F32)], axis=0)
    t_hi, t_rest = halves(table)
    t_mid, t_lo = halves(t_rest)
    seen = dot(
        jnp.concatenate([t_hi, t_mid, t_lo], axis=0).astype(BF16), pick_send[0:ELEMS]
    )
    gslot_s[...] = seen[0:16] + seen[16:32] + seen[32:48]
    lifts = stack3(lifts)
    flux2_s[...] = left4(dot(second_s[...], lifts))
    slope = dot(grad_s[...], lifts)
    wide = jnp.concatenate(
        [slope[0:ROWS] + pltpu.roll(slope[ROWS : 2 * ROWS], 64, 1), slope[2 * ROWS :]], axis=1
    )
    hi, lo = halves(wide)
    flux1_s[...] = jnp.concatenate([hi, hi, lo], axis=1).astype(BF16)
    face_send[...] = jnp.broadcast_to(send_face, (8, SLOTS))
    set_turns(turn_local, jnp.concatenate([turn[f : f + 1] for f in range(4)], axis=1))
    set_turns(turn_recv, tell[3:4].astype(jnp.int32))

    meanwhile(j_all, two_parts(j_all), traced, done)
    finish_sends(first_copy)
    total = None
    for half in (1, 0):
        pair = TILES[2 * half : 2 * half + 2]
        cols = slice(half * 256, (half + 1) * 256)
        arrive(first_copy, [2 * p + at for p in pair for at in range(2)])
        for q in range(QUANT):
            rows = slice(q * 8, q * 8 + 8)
            tiles = [unpacked(recv0_buf[2 * p, rows], recv0_buf[2 * p + 1, rows]) for p in pair]
            both = [jnp.concatenate([t[at] for t in tiles], axis=1) for at in range(2)]
            zslot_s[q : q + 1, cols] = both[1][7:8]
            if q == 0:
                chi = both
            else:
                chi = [x - tell_s[q - 1 : q, cols] * y for x, y in zip(chi, both)]
        r0, r1 = turned(chi[0], chi[1], turn_recv[:, cols])
        part = placed(r0, r1, cols)
        total = part if total is None else total + part
    complete(total, done)
    set_turns(turn_send, zslot_s[3:4].astype(jnp.int32))
    for j in range(3):
        total = zslot_s[0:1] * gslot_s[3 * j : 3 * j + 1]
        for i in range(1, 3):
            total = total + zslot_s[i : i + 1] * gslot_s[3 * j + i : 3 * j + i + 1]
        yslot_s[j : j + 1] = -total

    def advance(s):
        pressure, slope_of, start_u = series(s)
        j_s[0], j_s[1] = pressure, slope_of
        five = two_parts([pressure] + start_u + [slope_of, jnp.zeros((8, ELEMS), F32)])
        copy = later_copy(s)
        at_slot = dot(five, pick_send[...])
        mix = at_slot[0:ROWS]
        for i in range(3):
            mix = mix - zslot_s[i : i + 1] * at_slot[(i + 1) * ROWS : (i + 2) * ROWS]
        steep = at_slot[4 * ROWS : 5 * ROWS]
        mix = [stack3(mix)] + [stack3(yslot_s[j : j + 1] * steep) for j in range(3)]
        first, second = chosen(dot(wide_s[...], jnp.concatenate(mix, axis=0)), face_send[...])
        first, second = turned(first, second, turn_send[...])
        for pos, p in enumerate(TILES):
            lanes = slice(pos * 128, (pos + 1) * 128)
            send_buf[2 * p], send_buf[2 * p + 1] = packed(first[:, lanes], second[:, lanes])
        start(copy, FAR_FIRST)

    def finish(s, last=False):
        copy, done = later_copy(s), ending(s)
        c = weights(s)
        j_all = [j_s[0]] + velocities(j_s[1], [c[0] * u_s[i + 1] for i in range(3)])
        meanwhile(j_all, two_parts(j_all), traces(j_all), done, last)
        finish_sends(copy)
        parity = lax.rem(s, 2)
        total = None
        for half in (1, 0):
            pair = TILES[2 * half : 2 * half + 2]
            cols = slice(half * 256, (half + 1) * 256)
            arrive(copy, [2 * p + at for p in pair for at in range(2)])
            tiles = [unpacked(recv_buf[parity, 2 * p], recv_buf[parity, 2 * p + 1]) for p in pair]
            r0 = jnp.concatenate([t[0] for t in tiles], axis=1)
            r1 = jnp.concatenate([t[1] for t in tiles], axis=1)
            part = placed(r0, r1, cols)
            total = part if total is None else total + part
        complete(total, done, last)

    def step(s, carry):
        finish(s)
        advance(s + 1)
        return carry

    advance(1)
    lax.fori_loop(1, SUBSTEPS - 1, step, 0)
    finish(SUBSTEPS - 1, last=True)
    for q in range(QUANT):
        out[q] = u_s[q, 0:BASIS]


def body(
    initial_dofs, cluster, neighbours, orientation, send_slots, recv_slots, inv_jacobian, normals,
    face_area, bulk_modulus, inv_density, deriv_mats, face_proj,
):
    n_dev = lax.axis_size("dom")
    hbm = pl.BlockSpec(memory_space=pltpu.HBM)

    def call(*operands):
        return pl.pallas_call(
            lambda *refs: kernel(n_dev, *refs),
            out_shape=pltpu.VMEM((QUANT, BASIS, ELEMS), F32),
            in_specs=[hbm] * len(operands),
            out_specs=pl.BlockSpec(memory_space=pltpu.VMEM),
            scratch_shapes=[
                pltpu.VMEM((QUANT, BASIS, ELEMS), F32),
                pltpu.VMEM((1, ELEMS), jnp.int32),
                pltpu.VMEM((4, ELEMS), jnp.int32),
                pltpu.VMEM((4, ELEMS), jnp.int32),
                pltpu.VMEM((OFFSETS, CAP), jnp.int32),
                pltpu.VMEM((OFFSETS, CAP), jnp.int32),
                pltpu.VMEM((3, 3, ELEMS), F32),
                pltpu.VMEM((3, 4, ELEMS), F32),
                pltpu.VMEM((4, ELEMS), F32),
                pltpu.VMEM((1, ELEMS), F32),
                pltpu.VMEM((1, ELEMS), F32),
                pltpu.VMEM((3, BASIS, BASIS), F32),
                pltpu.VMEM((4, NODES, BASIS), F32),
                pltpu.VMEM((NROWS, 128), jnp.int32),
                pltpu.VMEM((QUANT, ROWS, ELEMS), F32),
                pltpu.VMEM((4 * NROWS, ELEMS), F32),
                pltpu.VMEM((QUANT, ROWS, ELEMS), F32),
                pltpu.VMEM((4 * NROWS, ELEMS), F32),
                pltpu.VMEM((3, 128, 128), F32),
                pltpu.VMEM((4, NROWS, 128), F32),
                pltpu.VMEM((3 * ROWS, 128), BF16),
                pltpu.VMEM((3 * ROWS, 128), BF16),
                pltpu.VMEM((ROWS, 384), BF16),
                pltpu.VMEM((ROWS, 384), BF16),
                pltpu.VMEM((6 * ROWS, 128), BF16),
                pltpu.VMEM((4 * NROWS, 128), BF16),
                pltpu.VMEM((ROWS, 256), BF16),
                pltpu.VMEM((ROWS, 768), BF16),
                pltpu.VMEM((6 * ROWS, 256), BF16),
                pltpu.VMEM((2, ROWS, ELEMS), F32),
                pltpu.VMEM((2, ROWS, ELEMS), F32),
                pltpu.VMEM((4 * NROWS, 512), BF16),
                pltpu.VMEM((16, SLOTS), F32),
                pltpu.VMEM((8, SLOTS), F32),
                pltpu.VMEM((2 * ELEMS, SLOTS), BF16),
                pltpu.VMEM((2 * ELEMS, FACES), BF16),
                pltpu.VMEM((SLOTS, ELEMS), BF16),
                pltpu.VMEM((16, 128), jnp.int32),
                pltpu.VMEM((4, 8, ELEMS), F32),
                pltpu.VMEM((8, FACES), F32),
                pltpu.VMEM((8, SLOTS), F32),
                pltpu.VMEM((8, SLOTS), jnp.int32),
                pltpu.VMEM((8, FACES), jnp.int32),
                pltpu.VMEM((8, SLOTS), jnp.int32),
                pltpu.VMEM((NROWS, SLOTS), jnp.int32),
                pltpu.VMEM((NROWS, FACES), jnp.int32),
                pltpu.VMEM((NROWS, SLOTS), jnp.int32),
                pltpu.VMEM((56, ELEMS), F32),
                pltpu.VMEM((8, SLOTS), F32),
                pltpu.VMEM((OFFSETS, 32, 128), F32),
                pltpu.VMEM((OFFSETS, 32, 128), F32),
                pltpu.VMEM((OFFSETS, 8, 128), F32),
                pltpu.VMEM((2, OFFSETS, 8, 128), F32),
                pltpu.SemaphoreType.DMA((20,)),
                pltpu.SemaphoreType.DMA((OFFSETS,)),
                pltpu.SemaphoreType.DMA((2, OFFSETS)),
            ],
            compiler_params=pltpu.CompilerParams(
                collective_id=0, has_side_effects=True, vmem_limit_bytes=VMEM_BYTES
            ),
        )(*operands)

    result = call(
        jnp.transpose(initial_dofs, (1, 0, 2)),
        cluster.reshape(1, ELEMS),
        neighbours,
        orientation,
        send_slots,
        recv_slots,
        inv_jacobian,
        jnp.transpose(normals, (1, 0, 2)),
        face_area,
        bulk_modulus.reshape(1, ELEMS),
        inv_density.reshape(1, ELEMS),
        deriv_mats,
        jnp.transpose(face_proj, (1, 0, 2)),
        jnp.asarray(turn_table()),
    )
    return result


def solution(mesh):
    return jax.shard_map(
        body,
        mesh=mesh,
        in_specs=(
            P(None, None, "dom"),
            P("dom"),
            P(None, "dom"),
            P(None, "dom"),
            P(None, "dom"),
            P(None, "dom"),
            P(None, None, "dom"),
            P(None, None, "dom"),
            P(None, "dom"),
            P("dom"),
            P("dom"),
            P(),
            P(),
        ),
        out_specs=P(None, None, "dom"),
        check_vma=False,
    )
```
